32 devices in a mesh: dp: 16 (over z, y, x), mp: 2 (over core).
Axes of the slice: x: 2, y: 2, z: 4, core: 2. Of those that a mesh axis runs over, the one named last changes fastest.
Arguments:
- tokens: bfloat16 [16384, 768], P(('dp', 'mp')), may hold values from -6 to 6
- memory: bfloat16 [16384, 768], P('dp'), may hold values from -6 to 6
- out_grad: bfloat16 [16384, 768], P(('dp', 'mp')), may hold values from -6 to 6
- tgt_lens: int32 [32], P('dp'), may hold values from 32 to 512, as said below
- mem_lens: int32 [32], P('dp'), may hold values from 32 to 512, as said below
- norm_gains: float32 [3, 768], replicated, may hold values from 0.5 to 1.5
- rel_table: float32 [32, 12], P(None, 'mp'), may hold values from -4 to 4
- self_qkv: bfloat16 [3, 768, 768], P(None, None, 'mp'), may hold values from -0.109375 to 0.109375
- self_out: bfloat16 [768, 768], P('mp'), may hold values from -0.875 to 0.875
- cross_q: bfloat16 [768, 768], P(None, 'mp'), may hold values from -0.109375 to 0.109375
- cross_kv: bfloat16 [2, 768, 768], P(None, None, 'mp'), may hold values from -0.109375 to 0.109375
- cross_out: bfloat16 [768, 768], P('mp'), may hold values from -0.875 to 0.875
- ffn_in: bfloat16 [2, 768, 2048], P(None, None, 'mp'), may hold values from -0.21875 to 0.21875
- ffn_out: bfloat16 [2048, 768], P('mp'), may hold values from -0.125 to 0.125
Outputs:
- result: bfloat16 [16384, 768], P(('dp', 'mp'))
- input_grad: bfloat16 [16384, 768], P(('dp', 'mp'))
- memory_grad: bfloat16 [16384, 768], P(('dp', 'mp'))
- gain_grads: float32 [3, 768], replicated
- table_grad: float32 [32, 12], P(None, 'mp')
- new_self_qkv: float32 [3, 768, 768], P(None, 'dp', 'mp')
- row_self_qkv: float32 [3, 768], P(None, 'dp')
- col_self_qkv: float32 [3, 768], P(None, 'mp')
- new_self_out: float32 [768, 768], P('mp', 'dp')
- row_self_out: float32 [768], P('mp')
- col_self_out: float32 [768], P('dp')
- new_cross_q: float32 [768, 768], P('dp', 'mp')
- row_cross_q: float32 [768], P('dp')
- col_cross_q: float32 [768], P('mp')
- new_cross_kv: float32 [2, 768, 768], P(None, 'dp', 'mp')
- row_cross_kv: float32 [2, 768], P(None, 'dp')
- col_cross_kv: float32 [2, 768], P(None, 'mp')
- new_cross_out: float32 [768, 768], P('mp', 'dp')
- row_cross_out: float32 [768], P('mp')
- col_cross_out: float32 [768], P('dp')
- new_ffn_in: float32 [2, 768, 2048], P(None, 'dp', 'mp')
- row_ffn_in: float32 [2, 768], P(None, 'dp')
- col_ffn_in: float32 [2, 2048], P(None, 'mp')
- new_ffn_out: float32 [2048, 768], P('mp', 'dp')
- row_ffn_out: float32 [2048], P('mp')
- col_ffn_out: float32 [768], P('dp')
- grad_norm: float32 [], replicated
The draws below stay inside these ranges and needn't reach their ends.
Inputs may be any that keep to these rules, and one draw needn't show every extreme that they name: Slots of sequence s at and past tgt_lens[s] are padding; in every draw some sequence fills all 512 slots. Encoder outputs of sequence s at and past mem_lens[s] are padding; in every draw some sequence uses all 512.
All inputs are finite; a program needn't handle non-finite values.
Results may differ from the reference program's by a relative error of at most 0.028.
The reference program's roundings to bfloat16 on the way count: a program that leaves them out, or rounds other values in their place, can miss the bound.
Values may be sent and summed in bfloat16 or wider, within the bound.
No kernel may reach another device: no remote copies, remote signals or barrier semaphores. Data moves between devices by JAX's collectives and lax.ppermute only.
A program may use at most 256 MiB of HBM per device.

```python
import jax
import jax.numpy as jnp
import numpy as np
from jax import lax

D = 768
HEADS = 12
HEAD_DIM = 64
FF = 2048
BUCKETS = 32
MAX_DIST = 128
SEQ_LEN = 512
MEM_LEN = 512
MIN_LEN = 32
SEQS = 32
TOKENS = 16384
MEM_TOKENS = 16384


def draw_lengths(key, seq_count, longest_len):
    first_draw = jax.random.randint(jax.random.fold_in(key, 1), (seq_count,), MIN_LEN, longest_len + 1)
    second_draw = jax.random.randint(jax.random.fold_in(key, 2), (seq_count,), MIN_LEN, longest_len + 1)
    full_slot = jax.random.randint(jax.random.fold_in(key, 3), (), 0, seq_count)
    picked = jnp.maximum(first_draw, second_draw)
    return jnp.where(jnp.arange(seq_count) == full_slot, longest_len, picked).astype(jnp.int32)


def draw_tgt_lens(key, part):
    return draw_lengths(jax.random.fold_in(key, 101), SEQS, SEQ_LEN)


def draw_mem_lens(key, part):
    return draw_lengths(jax.random.fold_in(key, 202), SEQS, MEM_LEN)


def raised(array, key, source, target, parts, factor):
    owner, partner = [(jnp.arange(array.shape[position]) // (array.shape[position] // parts)).reshape([-1 if axis == position else 1 for axis in range(array.ndim)]) for position in (source, target)]
    chosen = jax.random.permutation(key, parts)[partner]
    strong = (owner == chosen) | (owner == (partner + parts // 2) % parts)
    return jnp.where(strong, factor * array, array)


def levels(rng, shape, shards, low, largest):
    def one(position, blocks):
        steps = jax.random.uniform(jax.random.fold_in(jax.random.fold_in(rng, 6), position), (blocks,), jnp.float32, low / len(shards), largest / len(shards))
        return jnp.repeat(jnp.exp(steps), shape[position] // blocks).reshape((-1,) + (1,) * (len(shape) - position - 1))

    loudness = one(*shards[0])
    for cut in shards[1:]:
        loudness = loudness * one(*cut)
    return loudness


def bell_draw(key, shape, deviation, reach, shards=(), held_as=jnp.bfloat16):
    result = deviation * jax.random.normal(key, shape, jnp.float32)
    if shards:
        result = result * levels(key, shape, shards, -0.22, 0.18)
    return jnp.clip(result, -reach, reach).astype(held_as)


def gaussian_with(key, shape, deviation, reach, pieces, heavy, dtype=jnp.bfloat16):
    array = deviation * jax.random.normal(key, shape, jnp.float32)
    if pieces:
        array = array * levels(key, shape, pieces, -0.22, 0.18)
    return jnp.clip(raised(array, jax.random.fold_in(key, 3), *heavy), -reach, reach).astype(dtype)


def setup_inputs(seed: int = 0) -> dict:
    keys = jax.random.split(jax.random.key(seed), 15)
    tokens = bell_draw(keys[0], (TOKENS, D), 1.0, 6.0, ((0, 32),))
    memory = bell_draw(keys[1], (MEM_TOKENS, D), 1.0, 6.0, ((0, 16),))
    out_grad = gaussian_with(keys[2], (TOKENS, D), 1.0, 6.0, ((0, 32),), (0, 1, 32, 2.75))
    tgt_lens = draw_tgt_lens(jax.random.fold_in(keys[14], 71), 0)
    mem_lens = draw_mem_lens(jax.random.fold_in(keys[14], 71), 0)
    norm_gains = jnp.clip(1.0 + 0.1 * jax.random.normal(keys[5], (3, D), jnp.float32), 0.5, 1.5)
    rel_table = bell_draw(keys[6], (BUCKETS, HEADS), 1.0, 4.0, ((1, 2),), jnp.float32)
    self_qkv = bell_draw(keys[7], (3, D, HEADS * HEAD_DIM), (4 * D) ** -0.5, 0.109375, ((2, 2),))
    self_out = bell_draw(keys[8], (HEADS * HEAD_DIM, D), (HEADS * HEAD_DIM // 16) ** -0.5, 0.875, ((0, 2),))
    cross_q = bell_draw(keys[9], (D, HEADS * HEAD_DIM), (4 * D) ** -0.5, 0.109375, ((1, 2),))
    cross_kv = bell_draw(keys[10], (2, D, HEADS * HEAD_DIM), (4 * D) ** -0.5, 0.109375, ((2, 2),))
    cross_out = bell_draw(keys[11], (HEADS * HEAD_DIM, D), (HEADS * HEAD_DIM // 16) ** -0.5, 0.875, ((0, 2),))
    ffn_in = bell_draw(keys[12], (2, D, FF), D ** -0.5, 0.21875, ((2, 2),))
    ffn_out = bell_draw(keys[13], (FF, D), FF ** -0.5, 0.125, ((0, 2),))
    return dict(tokens=tokens, memory=memory, out_grad=out_grad, tgt_lens=tgt_lens, mem_lens=mem_lens, norm_gains=norm_gains, rel_table=rel_table, self_qkv=self_qkv, self_out=self_out, cross_q=cross_q, cross_kv=cross_kv, cross_out=cross_out, ffn_in=ffn_in, ffn_out=ffn_out)


norm_eps = 1e-06
stat_eps = 1e-30
masked_value = -1e+30
learn_rate = 0.04
highest = lax.Precision.HIGHEST

@jax.custom_vjp
def low(v):
    return lax.optimization_barrier(v.astype(jnp.bfloat16)).astype(jnp.float32)

@jax.custom_vjp
def low_back(v):
    return v

def low_keep(v):
    return (low(v), None)

def low_pass(kept, grad):
    return (grad,)

def back_keep(v):
    return (v, None)

def back_low(kept, grad):
    return (low(grad),)
low.defvjp(low_keep, low_pass)
low_back.defvjp(back_keep, back_low)

def bucket_matrix(length):
    offsets = np.arange(length)
    rel_dist = np.maximum(offsets[:, None] - offsets[None, :], 0)
    exact_span = BUCKETS // 2
    log_ratio = np.log(np.maximum(rel_dist, 1) / exact_span) / np.log(MAX_DIST / exact_span)
    far_bucket = np.minimum(exact_span + np.floor(log_ratio * (BUCKETS - exact_span)).astype(np.int64), BUCKETS - 1)
    return np.where(rel_dist < exact_span, rel_dist, far_bucket).astype(np.int32)

def rms_apply(hidden, gain_vec):
    inv_rms = lax.rsqrt(lax.optimization_barrier(jnp.mean(hidden * hidden, axis=-1, keepdims=True)) + norm_eps)
    return hidden * inv_rms * gain_vec

def gated_gelu(gate_pre, up_pre):
    return jax.nn.gelu(gate_pre, approximate=True) * up_pre

def matmul(left_rows, weight):
    return jnp.dot(left_rows, weight, precision=highest)

def split_heads(flat_rows, seq_count, head_count):
    return flat_rows.reshape(seq_count, -1, head_count, flat_rows.shape[-1] // head_count)

def merge_heads(shaped):
    return shaped.reshape(-1, shaped.shape[-2] * shaped.shape[-1])

def self_mask(lengths, seq_len):
    row_ids = lax.broadcasted_iota(jnp.int32, (seq_len, seq_len), 0)
    col_ids = lax.broadcasted_iota(jnp.int32, (seq_len, seq_len), 1)
    return (col_ids <= row_ids)[None, None] & (col_ids[None, None] < lengths[:, None, None, None])

def memory_mask(lengths, mem_len):
    col_ids = lax.broadcasted_iota(jnp.int32, (1, 1, 1, mem_len), 3)
    return col_ids < lengths[:, None, None, None]

def attend(queries, keys_in, values, pos_bias, key_mask):
    scores = jnp.einsum('sqhe,skhe->shqk', queries, keys_in, precision=highest) + pos_bias
    scores = jnp.where(key_mask, low_back(scores), masked_value)
    attn_probs = low(jax.nn.softmax(scores, axis=-1))
    return jnp.einsum('shqk,skhe->sqhe', attn_probs, values, precision=highest)

def decoder_layer(param_list, tok_rows, mem_rows, tgt_group, mem_group, bucket_ids):
    norm_gains, rel_table, self_qkv, self_out, cross_q, cross_kv, cross_out, ffn_in, ffn_out = param_list
    seq_count = tgt_group.shape[0]
    normed_a = low(rms_apply(tok_rows, norm_gains[0]))
    q_self = low(low_back(matmul(normed_a, self_qkv[0])))
    k_self = low(low_back(matmul(normed_a, self_qkv[1])))
    v_self = low(low_back(matmul(normed_a, self_qkv[2])))
    pos_bias = jnp.transpose(rel_table[bucket_ids], (2, 0, 1))[None]
    att_self = attend(split_heads(q_self, seq_count, HEADS), split_heads(k_self, seq_count, HEADS), split_heads(v_self, seq_count, HEADS), pos_bias, self_mask(tgt_group, SEQ_LEN))
    o_self = low(low_back(merge_heads(att_self)))
    h_one = tok_rows + low_back(matmul(o_self, self_out))
    normed_b = low(rms_apply(h_one, norm_gains[1]))
    q_cross = low(low_back(matmul(normed_b, cross_q)))
    k_cross = low(low_back(matmul(mem_rows, cross_kv[0])))
    v_cross = low(low_back(matmul(mem_rows, cross_kv[1])))
    att_cross = attend(split_heads(q_cross, seq_count, HEADS), split_heads(k_cross, seq_count, HEADS), split_heads(v_cross, seq_count, HEADS), 0.0, memory_mask(mem_group, MEM_LEN))
    o_cross = low(low_back(merge_heads(att_cross)))
    h_two = h_one + low_back(matmul(o_cross, cross_out))
    normed_c = low(rms_apply(h_two, norm_gains[2]))
    gate_pre = low_back(matmul(normed_c, ffn_in[0]))
    up_pre = low_back(matmul(normed_c, ffn_in[1]))
    hidden = low(gated_gelu(gate_pre, up_pre))
    return h_two + low_back(matmul(hidden, ffn_out))

def adafactor(weight, grad_sum):
    squares = grad_sum * grad_sum
    row_stat = lax.optimization_barrier(jnp.mean(squares, axis=-1)) + stat_eps
    col_stat = lax.optimization_barrier(jnp.mean(squares, axis=-2)) + stat_eps
    v_hat = row_stat[..., :, None] * col_stat[..., None, :] / lax.optimization_barrier(jnp.mean(row_stat, axis=-1))[..., None, None]
    return (weight - learn_rate * grad_sum * lax.rsqrt(v_hat), row_stat, col_stat)

def reference(tokens, memory, out_grad, tgt_lens, mem_lens, norm_gains, rel_table, self_qkv, self_out, cross_q, cross_kv, cross_out, ffn_in, ffn_out):
    param_list = tuple((array_in.astype(jnp.float32) for array_in in (norm_gains, rel_table, self_qkv, self_out, cross_q, cross_kv, cross_out, ffn_in, ffn_out)))
    group_size = 8
    group_count = SEQS // group_size
    tok_groups = tokens.astype(jnp.float32).reshape(group_count, group_size * SEQ_LEN, D)
    mem_groups = memory.astype(jnp.float32).reshape(group_count, group_size * MEM_LEN, D)
    cot_groups = out_grad.astype(jnp.float32).reshape(group_count, group_size * SEQ_LEN, D)
    tgt_groups = tgt_lens.reshape(group_count, group_size)
    memlen_groups = mem_lens.reshape(group_count, group_size)
    bucket_ids = jnp.asarray(bucket_matrix(SEQ_LEN))

    def one_group(grad_acc, group_in):
        tok_rows, mem_rows, cot_rows, tgt_group, mem_group = group_in

        def forward(param_in, tok_in, mem_in):
            return decoder_layer(param_in, tok_in, mem_in, tgt_group, mem_group, bucket_ids)
        outcome, pullback = jax.vjp(forward, param_list, tok_rows, mem_rows)
        grad_params, grad_tok, grad_mem = pullback(cot_rows)
        grad_acc = jax.tree.map(jnp.add, grad_acc, grad_params)
        return (grad_acc, (outcome.astype(jnp.bfloat16), grad_tok.astype(jnp.bfloat16), grad_mem.astype(jnp.bfloat16)))
    zero_grads = jax.tree.map(jnp.zeros_like, param_list)
    grad_sums, (outcomes, tok_grads, mem_grads) = lax.scan(one_group, zero_grads, (tok_groups, mem_groups, cot_groups, tgt_groups, memlen_groups))
    new_self_qkv, row_self_qkv, col_self_qkv = adafactor(param_list[2], grad_sums[2])
    new_self_out, row_self_out, col_self_out = adafactor(param_list[3], grad_sums[3])
    new_cross_q, row_cross_q, col_cross_q = adafactor(param_list[4], grad_sums[4])
    new_cross_kv, row_cross_kv, col_cross_kv = adafactor(param_list[5], grad_sums[5])
    new_cross_out, row_cross_out, col_cross_out = adafactor(param_list[6], grad_sums[6])
    new_ffn_in, row_ffn_in, col_ffn_in = adafactor(param_list[7], grad_sums[7])
    new_ffn_out, row_ffn_out, col_ffn_out = adafactor(param_list[8], grad_sums[8])
    grad_norm = jnp.sqrt(jnp.sum(jnp.stack([jnp.sum(grad_part * grad_part) for grad_part in grad_sums])))
    return (outcomes.reshape(TOKENS, D), tok_grads.reshape(TOKENS, D), mem_grads.reshape(MEM_TOKENS, D), grad_sums[0], grad_sums[1], new_self_qkv, row_self_qkv, col_self_qkv, new_self_out, row_self_out, col_self_out, new_cross_q, row_cross_q, col_cross_q, new_cross_kv, row_cross_kv, col_cross_kv, new_cross_out, row_cross_out, col_cross_out, new_ffn_in, row_ffn_in, col_ffn_in, new_ffn_out, row_ffn_out, col_ffn_out, grad_norm)
```

```python
import functools

import jax
import jax.numpy as jnp
import numpy as np
from jax import lax
from jax.experimental import pallas as pl
from jax.experimental.pallas import tpu as pltpu
from jax.sharding import PartitionSpec as P

BUCKETS = 32
MAX_DIST = 128
HD = 64
LANE = 128
QB = 256
norm_eps = 1e-06
stat_eps = 1e-30
masked_value = -1e30
learn_rate = 0.04
highest = lax.Precision.HIGHEST
F32 = jnp.float32
BF16 = jnp.bfloat16
VMEM = pl.BlockSpec(memory_space=pltpu.VMEM)
SMEM = pl.BlockSpec(memory_space=pltpu.SMEM)


def bucket_of(dist):
    exact_span = BUCKETS // 2
    dist = np.maximum(dist, 0)
    log_ratio = np.log(np.maximum(dist, 1) / exact_span) / np.log(MAX_DIST / exact_span)
    far = np.minimum(
        exact_span + np.floor(log_ratio * (BUCKETS - exact_span)).astype(np.int64), BUCKETS - 1
    )
    return np.where(dist < exact_span, dist, far).astype(np.int32)


def nn(a, b):
    return lax.dot_general(a, b, (((1,), (0,)), ((), ())), preferred_element_type=F32)


def nt(a, b):
    return lax.dot_general(a, b, (((1,), (1,)), ((), ())), preferred_element_type=F32)


def tn(a, b):
    return lax.dot_general(a, b, (((0,), (0,)), ((), ())), preferred_element_type=F32)


def call(kernel, out_shape, args, n_smem, scratch=(), flops=0, trans=0):
    in_specs = [SMEM] * n_smem + [VMEM] * (len(args) - n_smem)
    outs = jax.tree.leaves(out_shape)
    moved = sum(a.size * a.dtype.itemsize for a in list(args) + outs)
    return pl.pallas_call(
        kernel,
        out_shape=out_shape,
        in_specs=in_specs,
        out_specs=jax.tree.map(lambda _: VMEM, out_shape),
        scratch_shapes=list(scratch),
        compiler_params=pltpu.CompilerParams(vmem_limit_bytes=56 * 1024 * 1024),
        cost_estimate=pl.CostEstimate(flops=flops, bytes_accessed=moved, transcendentals=trans),
    )(*args)


def sds(shape, dtype):
    return jax.ShapeDtypeStruct(shape, dtype)


def head_masks(dtype):
    lane = lax.broadcasted_iota(jnp.int32, (1, LANE), 1)
    return [(lane < HD).astype(dtype), (lane >= HD).astype(dtype)]


def bias_chunks(bias_ref, head, block, count):
    near = bias_ref[head, 0:LANE, :]
    diag = bias_ref[head, LANE : 2 * LANE, :]
    const = jnp.broadcast_to(bias_ref[head, 0:1, :], (LANE, LANE))
    none = jnp.full((LANE, LANE), masked_value, F32)
    pieces = {-1: (none, diag), 0: (diag, near), 1: (near, const)}
    return [
        jnp.concatenate(pieces.get(2 * block - j, (const, const)), axis=1) for j in range(count)
    ]


def score_chunks(keys_masked, queries, bias_ref, head, block, count, length):
    scores = nt(keys_masked[: count * LANE], queries)
    row = lax.broadcasted_iota(jnp.int32, (LANE, QB), 0)
    chunks = []
    bias = bias_chunks(bias_ref, head, block, count) if bias_ref is not None else None
    for j in range(count):
        part = scores[j * LANE : (j + 1) * LANE]
        if bias is not None:
            part = part + bias[j]
        chunks.append(jnp.where(row < length - j * LANE, part, masked_value))
    return chunks


def attend_pairs(q_ref, k_ref, v_ref, o_ref, lse_ref, bias_ref, length, lse_base=0):
    rows, width = q_ref.shape
    keys = k_ref.shape[0]
    masks = head_masks(BF16)

    def pair(p, carry):
        lanes = pl.ds(pl.multiple_of(p * LANE, LANE), LANE)
        k_pair = k_ref[:, lanes]
        v_t = jnp.transpose(v_ref[:, lanes].astype(F32)).astype(BF16)
        halves = []
        for t in range(2):
            k_m = k_pair * masks[t]
            outs = []
            for block in range(rows // QB):
                count = 2 * block + 2 if bias_ref is not None else keys // LANE
                q_blk = q_ref[pl.ds(block * QB, QB), lanes]
                chunks = score_chunks(k_m, q_blk, bias_ref, 2 * p + t, block, count, length)
                top = functools.reduce(
                    jnp.maximum, [jnp.max(c, axis=0, keepdims=True) for c in chunks]
                )
                exps = [jnp.exp(c - top) for c in chunks]
                total = functools.reduce(
                    jnp.add, [jnp.sum(c, axis=0, keepdims=True) for c in exps]
                )
                scale = 1.0 / total
                probs = jnp.concatenate([(c * scale).astype(BF16) for c in exps], axis=0)
                outs.append(nn(v_t[t * HD : (t + 1) * HD, : count * LANE], probs))
                lse_ref[lse_base + 2 * p + t, :, block * QB : (block + 1) * QB] = top + jnp.log(
                    total
                )
            halves.append(jnp.concatenate(outs, axis=1))
        o_t = jnp.concatenate(halves, axis=0)
        o_ref[:, lanes] = jnp.transpose(o_t).astype(BF16)
        return carry

    lax.fori_loop(0, width // LANE, pair, 0)


def attend_back_pairs(
    q_ref, k_ref, v_ref, do_ref, dqkv_ref, lse_ref, bias_ref, length, lse_base=0, diag_ref=None
):
    rows, width = q_ref.shape
    keys = k_ref.shape[0]
    masks = head_masks(BF16)
    lane_id = lax.broadcasted_iota(jnp.int32, (1, QB), 1)

    def pair(p, carry):
        lanes = pl.ds(pl.multiple_of(p * LANE, LANE), LANE)
        k_pair = k_ref[:, lanes]
        v_pair = v_ref[:, lanes]
        k_t = jnp.transpose(k_pair.astype(F32)).astype(BF16)
        dv = [jnp.zeros((LANE, LANE), F32) for _ in range(keys // LANE)]
        dk = [jnp.zeros((LANE, LANE), F32) for _ in range(keys // LANE)]
        halves = []
        for t in range(2):
            k_m = k_pair * masks[t]
            v_m = v_pair * masks[t]
            outs = []
            near_sum = jnp.zeros((LANE, LANE), F32)
            diag_sum = jnp.zeros((LANE, LANE), F32)
            far_sum = jnp.zeros((1, LANE), F32)
            for block in range(rows // QB):
                count = 2 * block + 2 if bias_ref is not None else keys // LANE
                q_blk = q_ref[pl.ds(block * QB, QB), lanes]
                do_blk = do_ref[pl.ds(block * QB, QB), lanes]
                chunks = score_chunks(k_m, q_blk, bias_ref, 2 * p + t, block, count, length)
                lse = lse_ref[lse_base + 2 * p + t, :, block * QB : (block + 1) * QB]
                probs = [jnp.exp(c - lse) for c in chunks]
                d_probs = nt(v_m[: count * LANE], do_blk)
                d_probs = [d_probs[j * LANE : (j + 1) * LANE] for j in range(count)]
                dot = functools.reduce(
                    jnp.add,
                    [jnp.sum(a * b, axis=0, keepdims=True) for a, b in zip(probs, d_probs)],
                )
                d_scores = [
                    (a * (b - dot)).astype(BF16) for a, b in zip(probs, d_probs)
                ]
                if diag_ref is not None:
                    for j in range(count):
                        wide = d_scores[j].astype(F32)
                        left, right = wide[:, :LANE], wide[:, LANE:]
                        offset = 2 * block - j
                        if offset == -1:
                            diag_sum = diag_sum + right
                        elif offset == 0:
                            diag_sum = diag_sum + left
                            near_sum = near_sum + right
                        elif offset == 1:
                            near_sum = near_sum + left
                            far_sum = far_sum + jnp.sum(right, axis=0, keepdims=True)
                        else:
                            far_sum = far_sum + jnp.sum(left + right, axis=0, keepdims=True)
                d_all = jnp.concatenate(d_scores, axis=0)
                p_all = jnp.concatenate([a.astype(BF16) for a in probs], axis=0)
                dv_new = nn(p_all, do_blk * masks[t])
                dk_new = nn(d_all, q_blk * masks[t])
                for j in range(count):
                    dv[j] = dv[j] + dv_new[j * LANE : (j + 1) * LANE]
                    dk[j] = dk[j] + dk_new[j * LANE : (j + 1) * LANE]
                outs.append(nn(k_t[t * HD : (t + 1) * HD, : count * LANE], d_all))
            halves.append(jnp.concatenate(outs, axis=1))
            if diag_ref is not None:
                both = jnp.concatenate([near_sum, diag_sum], axis=0)
                both = jnp.concatenate([both, jnp.zeros_like(both)], axis=1)
                acc = jnp.zeros((8, QB), F32)
                for g in range(QB // 8):
                    piece = both[8 * g : 8 * g + 8]
                    turn = (LANE - 8 * g) % QB
                    acc = acc + (pltpu.roll(piece, turn, 1) if turn else piece)
                line = acc[0:1]
                for g in range(1, 8):
                    line = line + pltpu.roll(acc, QB - g, 1)[g : g + 1]
                far_total = jnp.sum(far_sum, axis=1, keepdims=True)
                diag_ref[2 * p + t] = line + jnp.where(lane_id == QB - 1, far_total, 0.0)
        dq_t = jnp.concatenate(halves, axis=0)
        dqkv_ref[:, lanes] = jnp.transpose(dq_t).astype(BF16)
        lanes_k = pl.ds(pl.multiple_of(width + p * LANE, LANE), LANE)
        lanes_v = pl.ds(pl.multiple_of(2 * width + p * LANE, LANE), LANE)
        dqkv_ref[:, lanes_k] = jnp.concatenate(dk, axis=0).astype(BF16)
        dqkv_ref[:, lanes_v] = jnp.concatenate(dv, axis=0).astype(BF16)
        return carry

    lax.fori_loop(0, width // LANE, pair, 0)


def row_blocks(rows, step, fn):
    def one(i, carry):
        fn(pl.ds(pl.multiple_of(i * step, step), step))
        return carry

    lax.fori_loop(0, rows // step, one, 0)


def rms_rows(h, gain):
    return h * lax.rsqrt(jnp.mean(h * h, axis=-1, keepdims=True) + norm_eps) * gain


def rms_back(h, gain, dn):
    inv = lax.rsqrt(jnp.mean(h * h, axis=-1, keepdims=True) + norm_eps)
    gd = gain * dn
    dh = gd * inv - h * (jnp.mean(gd * h, axis=-1, keepdims=True) * (inv * inv * inv))
    return dh, jnp.sum(dn * h * inv, axis=0, keepdims=True)


ROWS = 128


def self_forward(first, sc, *refs):
    if first:
        x_ref, gain_ref, w_ref, line_ref, a_ref, q_ref, k_ref, v_ref, o_ref, lse_ref, bias_ref = refs

        def norm(rows):
            a_ref[rows, :] = rms_rows(x_ref[rows, :].astype(F32), gain_ref[0:1, :]).astype(BF16)

        row_blocks(x_ref.shape[0], ROWS, norm)
    else:
        a_ref, w_ref, line_ref, q_ref, k_ref, v_ref, o_ref, lse_ref, bias_ref = refs
    for h in range(bias_ref.shape[0]):
        line = jnp.broadcast_to(line_ref[h : h + 1, :], (QB, QB))
        tile = pltpu.roll(line, 0, 1, stride=1, stride_axis=0)[:, :LANE]
        row = lax.broadcasted_iota(jnp.int32, (QB, LANE), 0)
        col = lax.broadcasted_iota(jnp.int32, (QB, LANE), 1)
        bias_ref[h] = jnp.where(col - row + LANE < 0, masked_value, tile)

    def project(rows):
        for i, ref in enumerate((q_ref, k_ref, v_ref)):
            ref[rows, :] = nn(a_ref[rows, :], w_ref[i]).astype(BF16)

    row_blocks(a_ref.shape[0], QB, project)
    attend_pairs(q_ref, k_ref, v_ref, o_ref, lse_ref, bias_ref, sc[0])


def cross_forward(
    sc, x_ref, gain_ref, m_ref, oo, on, woo, won, wqo, wqn, wkvo, wkvn, wco, wcn,
    h1_ref, b_ref, qo, qn, ko, kn, vo, vn, oco, ocn, lse_ref, h2_ref, c_ref,
):
    def first(rows):
        h1 = x_ref[rows, :].astype(F32) + nn(oo[rows, :], woo[...]) + nn(on[rows, :], won[...])
        h1_ref[rows, :] = h1
        b_ref[rows, :] = rms_rows(h1, gain_ref[1:2, :]).astype(BF16)
        for q, k, v, wq, wkv in ((qo, ko, vo, wqo, wkvo), (qn, kn, vn, wqn, wkvn)):
            q[rows, :] = nn(b_ref[rows, :], wq[...]).astype(BF16)
            k[rows, :] = nn(m_ref[rows, :], wkv[0]).astype(BF16)
            v[rows, :] = nn(m_ref[rows, :], wkv[1]).astype(BF16)

    row_blocks(x_ref.shape[0], ROWS, first)
    heads = qo.shape[1] // HD
    attend_pairs(qo, ko, vo, oco, lse_ref, None, sc[1])
    attend_pairs(qn, kn, vn, ocn, lse_ref, None, sc[1], heads)

    def last(rows):
        h2 = h1_ref[rows, :] + nn(oco[rows, :], wco[...]) + nn(ocn[rows, :], wcn[...])
        h2_ref[rows, :] = h2
        c_ref[rows, :] = rms_rows(h2, gain_ref[2:3, :]).astype(BF16)

    row_blocks(x_ref.shape[0], ROWS, last)


HB = 256


def ffn(c_ref, h2_ref, og_ref, gain_ref, wio, win, wdo, wdn, res_ref, own, nbr, g1_ref, w1_ref, dgain, acc, dacc):
    root = np.float32(np.sqrt(2.0 / np.pi))
    width = wdo.shape[0]
    acc[...] = jnp.zeros_like(acc)
    dacc[...] = jnp.zeros_like(dacc)
    rows_all = c_ref.shape[0]
    for wi, wd, out in ((wio, wdo, own), (win, wdn, nbr)):

        def block(j, carry, wi=wi, wd=wd, out=out):
            cols = pl.ds(pl.multiple_of(j * HB, HB), HB)
            up_cols = pl.ds(pl.multiple_of(width + j * HB, HB), HB)
            hid_cols = pl.ds(pl.multiple_of(2 * width + j * HB, HB), HB)
            wg = wi[0, :, cols]
            wu = wi[1, :, cols]
            wo = wd[cols, :]

            def some(rows):
                c = c_ref[rows, :]
                gate = nn(c, wg)
                up = nn(c, wu)
                d_hid = nt(og_ref[rows, :], wo)
                sq = gate * gate
                th = jnp.tanh(root * gate * (1.0 + 0.044715 * sq))
                half = 0.5 + 0.5 * th
                gelu = gate * half
                slope = half + 0.5 * gate * (1.0 - th * th) * (
                    root * (1.0 + np.float32(3 * 0.044715) * sq)
                )
                hid = (gelu * up).astype(BF16)
                d_gate = (d_hid * up * slope).astype(BF16)
                d_up = (d_hid * gelu).astype(BF16)
                out[rows, cols] = d_gate
                out[rows, up_cols] = d_up
                out[rows, hid_cols] = hid
                acc[rows, :] += nn(hid, wo)
                dacc[rows, :] += nt(d_gate, wg) + nt(d_up, wu)

            row_blocks(rows_all, QB, some)
            return carry

        lax.fori_loop(0, width // HB, block, 0)
    dgain[...] = jnp.zeros_like(dgain)

    def last(rows):
        h2 = h2_ref[rows, :]
        res_ref[rows, :] = (h2 + acc[rows, :]).astype(BF16)
        dh, dg = rms_back(h2, gain_ref[2:3, :], dacc[rows, :])
        g1 = og_ref[rows, :].astype(F32) + dh
        g1_ref[rows, :] = g1
        w1_ref[rows, :] = g1.astype(BF16)
        dgain[...] += dg

    row_blocks(rows_all, ROWS, last)


def cross_backward(
    sc, w1_ref, g1_ref, h1_ref, gain_ref, qo, qn, ko, kn, vo, vn, lse_ref, wco, wcn, wqo, wqn, wkvo, wkvn,
    do_own, do_nbr, g0_ref, w0_ref, dm_ref, dgain, doo, don,
):
    rows_all, half = qo.shape
    heads = half // HD

    def first(rows):
        doo[rows, :] = nt(w1_ref[rows, :], wco[...]).astype(BF16)
        don[rows, :] = nt(w1_ref[rows, :], wcn[...]).astype(BF16)

    row_blocks(rows_all, ROWS, first)
    attend_back_pairs(qo, ko, vo, doo, do_own, lse_ref, None, sc[1])
    attend_back_pairs(qn, kn, vn, don, do_nbr, lse_ref, None, sc[1], heads)
    dgain[...] = jnp.zeros_like(dgain)

    def last(rows):
        d_b = nt(do_own[rows, 0:half], wqo[...]) + nt(do_nbr[rows, 0:half], wqn[...])
        dm = nt(do_own[rows, half : 2 * half], wkvo[0]) + nt(do_nbr[rows, half : 2 * half], wkvn[0])
        dm = dm + nt(do_own[rows, 2 * half :], wkvo[1]) + nt(do_nbr[rows, 2 * half :], wkvn[1])
        dm_ref[rows, :] = dm.astype(BF16)
        dh, dg = rms_back(h1_ref[rows, :], gain_ref[1:2, :], d_b)
        g0 = g1_ref[rows, :] + dh
        g0_ref[rows, :] = g0
        w0_ref[rows, :] = g0.astype(BF16)
        dgain[...] += dg

    row_blocks(rows_all, ROWS, last)


def self_backward(sc, w0_ref, wo, q_ref, k_ref, v_ref, lse_ref, bias_ref, out_ref, diag_ref, do_ref):
    def first(rows):
        do_ref[rows, :] = nt(w0_ref[rows, :], wo[...]).astype(BF16)

    row_blocks(w0_ref.shape[0], ROWS, first)
    attend_back_pairs(
        q_ref, k_ref, v_ref, do_ref, out_ref, lse_ref, bias_ref, sc[0], 0, diag_ref
    )


def input_backward(own, nbr, wo, wn, x_ref, gain_ref, g0_ref, out_ref, dgain):
    half = own.shape[1] // 3
    dgain[...] = jnp.zeros_like(dgain)

    def some(rows):
        d_a = nt(own[rows, 0:half], wo[0]) + nt(nbr[rows, 0:half], wn[0])
        for i in (1, 2):
            cols = slice(i * half, (i + 1) * half)
            d_a = d_a + nt(own[rows, cols], wo[i]) + nt(nbr[rows, cols], wn[i])
        dh, dg = rms_back(x_ref[rows, :].astype(F32), gain_ref[0:1, :], d_a)
        out_ref[rows, :] = (g0_ref[rows, :] + dh).astype(BF16)
        dgain[...] += dg

    row_blocks(own.shape[0], ROWS, some)


WB = 384


def weight_grads(jobs, masks, sc, *refs):
    keep_ref, send_ref, total = refs[-3:]
    at = 0
    depth = total.shape[0]
    for lo, ln, ro, rn, column, width in jobs:
        step = WB if width % WB == 0 else 256
        for d in range(depth // WB):
            left = slice(d * WB, (d + 1) * WB)

            def block(j, carry, lo=lo, ln=ln, ro=ro, rn=rn, left=left, column=column, at=at, step=step):
                src = pl.ds(pl.multiple_of(column + j * step, LANE), step)
                dst = pl.ds(pl.multiple_of(at + j * step, LANE), step)
                total[left, dst] = tn(refs[lo][:, left], refs[ro][:, src]) + tn(
                    refs[ln][:, left], refs[rn][:, src]
                )
                return carry

            lax.fori_loop(0, width // step, block, 0)
        at += width
    rows = keep_ref.shape[1]
    half = len(masks) // 2
    for pos, mask in enumerate(masks):
        chunk = lax.bitwise_xor(sc[3], jnp.int32(mask))
        part = total[pl.ds(pl.multiple_of(chunk * rows, 16), rows), :]
        if pos < half:
            keep_ref[pos] = part
        else:
            send_ref[pos - half] = part.astype(BF16)


def reduce_stage(count, *refs):
    for i in range(count):
        keep, got, new_keep, new_send = refs[i], refs[count + i], refs[2 * count + i], refs[3 * count + i]
        half = keep.shape[0] // 2
        for j in range(half):
            new_keep[j] = keep[j] + got[j].astype(F32)
            new_send[j] = (keep[half + j] + got[half + j].astype(F32)).astype(BF16)


def order_masks(order):
    out = []
    for pos in range(16):
        mask = 0
        for bit in range(4):
            if pos >> (3 - bit) & 1:
                mask ^= order[bit]
        out.append(mask)
    return out


def swap_dp(v, mask):
    return lax.ppermute(v, "dp", [(i, i ^ mask) for i in range(16)])


def swap_mp(v):
    return lax.ppermute(v, "mp", [(0, 1), (1, 0)])


def make_grads(jobs, arrays, order, sc, n_data):
    width = sum(job[5] for job in jobs)
    depth = arrays[jobs[0][0]].shape[1]
    if n_data != 16:
        cols = []
        for lo, ln, ro, rn, column, w in jobs:
            cols.append(
                tn(arrays[lo], arrays[ro][:, column : column + w])
                + tn(arrays[ln], arrays[rn][:, column : column + w])
            )
        return lax.psum_scatter(
            jnp.concatenate(cols, axis=1), "dp", scatter_dimension=0, tiled=True
        )
    rows = depth // 16
    flops = 4 * arrays[jobs[0][0]].shape[0] * depth * width
    return call(
        functools.partial(weight_grads, jobs, order_masks(order)),
        [sds((8, rows, width), F32), sds((8, rows, width), BF16)],
        [sc] + list(arrays),
        1,
        [pltpu.VMEM((depth, width), F32)],
        flops=flops,
    )


def reduce_group(parts, orders, n_data):
    if n_data != 16:
        return parts
    keeps = [p[0] for p in parts]
    sends = [p[1] for p in parts]
    for stage in range(4):
        gots = [swap_dp(s, o[stage]) for s, o in zip(sends, orders)]
        if stage == 3:
            return [k[0] + g[0].astype(F32) for k, g in zip(keeps, gots)]
        half = keeps[0].shape[0] // 2
        shapes = [sds((half,) + k.shape[1:], F32) for k in keeps]
        shapes += [sds((half,) + k.shape[1:], BF16) for k in keeps]
        outs = call(
            functools.partial(reduce_stage, len(keeps)), shapes, list(keeps) + list(gots), 0
        )
        keeps, sends = outs[: len(keeps)], outs[len(keeps) :]


def sum_dp(v, n_data):
    if n_data != 16:
        return lax.psum(v, "dp")
    for mask in (1, 2, 4, 12):
        v = v + swap_dp(v, mask)
    return v


def body(
    tokens,
    memory,
    out_grad,
    tgt_lens,
    mem_lens,
    norm_gains,
    rel_table,
    self_qkv,
    self_out,
    cross_q,
    cross_kv,
    cross_out,
    ffn_in,
    ffn_out,
):
    n_data = lax.axis_size("dp")
    mp = lax.axis_index("mp")
    dp = lax.axis_index("dp")
    rows = tokens.shape[0]
    depth = tokens.shape[1]
    heads = rel_table.shape[1]
    half = heads * HD
    width = ffn_out.shape[0]
    sc = jnp.stack(
        [
            lax.dynamic_index_in_dim(tgt_lens, mp, 0, False),
            lax.dynamic_index_in_dim(mem_lens, mp, 0, False),
            mp.astype(jnp.int32),
            dp.astype(jnp.int32),
        ]
    )
    qkv_n = swap_mp(self_qkv)
    table_n = swap_mp(rel_table)
    so_n = swap_mp(self_out)
    cq_n = swap_mp(cross_q)
    ckv_n = swap_mp(cross_kv)
    co_n = swap_mp(cross_out)
    fi_n = swap_mp(ffn_in)
    fo_n = swap_mp(ffn_out)
    og_n = swap_mp(out_grad)

    dist = np.arange(QB)
    dist = np.where(dist < LANE, dist + LANE, dist - LANE)
    spread = jnp.asarray((bucket_of(dist)[:, None] == np.arange(BUCKETS)).astype(np.float32))

    def line_of(table):
        return lax.dot_general(
            table, spread, (((0,), (1,)), ((), ())), precision=highest, preferred_element_type=F32
        )

    attn_flops = 4 * rows * rows * HD * heads
    bias_shape = sds((heads, QB, LANE), F32)
    act = sds((rows, half), BF16)
    wide = sds((rows, depth), BF16)
    full = sds((rows, depth), F32)
    gain_row = sds((1, depth), F32)
    lse = sds((heads, 1, rows), F32)
    lse2 = sds((2 * heads, 1, rows), F32)
    a, qs_o, ks_o, vs_o, os_o, lses_o, bias_o = call(
        functools.partial(self_forward, True),
        [wide, act, act, act, act, lse, bias_shape],
        [sc, tokens, norm_gains, self_qkv, line_of(rel_table)],
        1,
        flops=6 * rows * depth * half + attn_flops,
    )
    a_n = swap_mp(a)
    qs_n, ks_n, vs_n, os_n, lses_n, bias_n = call(
        functools.partial(self_forward, False),
        [act, act, act, act, lse, bias_shape],
        [sc, a, qkv_n, line_of(table_n)],
        1,
        flops=6 * rows * depth * half + attn_flops,
    )
    os_x = swap_mp(os_n)
    mem_own = lax.dynamic_slice_in_dim(memory, mp * rows, rows, 0)
    mem_nbr = lax.dynamic_slice_in_dim(memory, (1 - mp) * rows, rows, 0)
    h1, b, qc_o, qc_n, kc_o, kc_n, vc_o, vc_n, oc_o, oc_n, lsec, h2, c = call(
        cross_forward,
        [full, wide, act, act, act, act, act, act, act, act, lse2, full, wide],
        [sc, tokens, norm_gains, mem_own, os_o, os_n, self_out, so_n, cross_q, cq_n, cross_kv, ckv_n, cross_out, co_n],
        1,
        flops=20 * rows * depth * half + 2 * attn_flops,
    )
    b_n = swap_mp(b)
    oc_x = swap_mp(oc_n)
    c_n = swap_mp(c)
    hid = sds((rows, 3 * width), BF16)
    result, f_own, f_nbr, g1, w1, gain_c = call(
        ffn,
        [wide, hid, hid, full, wide, gain_row],
        [c, h2, out_grad, norm_gains, ffn_in, fi_n, ffn_out, fo_n],
        0,
        [pltpu.VMEM((rows, depth), F32), pltpu.VMEM((rows, depth), F32)],
        flops=24 * rows * depth * width,
    )
    f_x = swap_mp(f_nbr)
    w1_n = swap_mp(w1)
    order_a = ((1, 2, 4, 12), (4, 12, 1, 2))
    order_b = ((2, 1, 12, 4), (12, 4, 2, 1))
    ffn_parts = [
        make_grads(((0, 1, 2, 3, 0, 3 * width // 2),), [c, c_n, f_own, f_x], order_a[0], sc, n_data),
        make_grads(
            ((0, 1, 4, 5, 3 * width // 2, width // 2), (2, 3, 4, 5, 2 * width, width)),
            [c, c_n, out_grad, og_n, f_own, f_x],
            order_a[1],
            sc,
            n_data,
        ),
    ]
    c_own, c_nbr, g0, w0, d_mem, gain_b = call(
        cross_backward,
        [sds((rows, 3 * half), BF16), sds((rows, 3 * half), BF16), full, wide, wide, gain_row],
        [sc, w1, g1, h1, norm_gains, qc_o, qc_n, kc_o, kc_n, vc_o, vc_n, lsec, cross_out, co_n, cross_q, cq_n, cross_kv, ckv_n],
        1,
        [pltpu.VMEM((rows, half), BF16), pltpu.VMEM((rows, half), BF16)],
        flops=16 * rows * depth * half + 5 * attn_flops,
    )
    c_x = swap_mp(c_nbr)
    w0_n = swap_mp(w0)
    ffn_sums = reduce_group(ffn_parts, order_a, n_data)
    diag = sds((heads, 1, QB), F32)

    def self_back(out_w, q, k, v, row_lse, bias):
        return call(
            self_backward,
            [sds((rows, 3 * half), BF16), diag],
            [sc, w0, out_w, q, k, v, row_lse, bias],
            1,
            [pltpu.VMEM((rows, half), BF16)],
            flops=2 * rows * depth * half + 3 * attn_flops,
        )

    s_nbr, diag_n = self_back(so_n, qs_n, ks_n, vs_n, lses_n, bias_n)
    s_x = swap_mp(s_nbr)
    cross_parts = [
        make_grads(
            ((0, 1, 4, 5, 0, half), (2, 3, 4, 5, half, half)),
            [b, b_n, mem_own, mem_nbr, c_own, c_x],
            order_b[0],
            sc,
            n_data,
        ),
        make_grads(
            ((2, 3, 4, 5, 2 * half, half), (0, 1, 6, 7, 0, half)),
            [w1, w1_n, mem_own, mem_nbr, c_own, c_x, oc_o, oc_x],
            order_b[1],
            sc,
            n_data,
        ),
    ]
    cross_sums = reduce_group(cross_parts, order_b, n_data)
    s_own, diag_o = self_back(self_out, qs_o, ks_o, vs_o, lses_o, bias_o)
    self_parts = [
        make_grads(((0, 1, 2, 3, 0, 2 * half),), [a, a_n, s_own, s_x], order_a[0], sc, n_data),
        make_grads(
            ((0, 1, 4, 5, 2 * half, half), (2, 3, 6, 7, 0, half)),
            [a, a_n, w0, w0_n, s_own, s_x, os_o, os_x],
            order_a[1],
            sc,
            n_data,
        ),
    ]
    self_sums = reduce_group(self_parts, order_a, n_data)
    grad_in, gain_a = call(
        input_backward,
        [wide, gain_row],
        [s_own, s_nbr, self_qkv, qkv_n, tokens, norm_gains, g0],
        0,
        flops=12 * rows * depth * half,
    )

    bucket_sum = jnp.asarray((bucket_of(np.arange(QB))[:, None] == np.arange(BUCKETS)).astype(np.float32))

    def table_of(d):
        return lax.dot_general(
            bucket_sum, d[:, 0, :], (((0,), (1,)), ((), ())), precision=highest,
            preferred_element_type=F32,
        )

    table_o = table_of(diag_o)
    table_x = table_of(diag_n)
    g_gate_up = jnp.concatenate([ffn_sums[0], ffn_sums[1][:, : width // 2]], axis=1)
    mats = {
        "gate": g_gate_up[:, :width],
        "up": g_gate_up[:, width:],
        "down": ffn_sums[1][:, width // 2 :],
        "cq": cross_sums[0][:, :half],
        "ck": cross_sums[0][:, half:],
        "cv": cross_sums[1][:, :half],
        "co": cross_sums[1][:, half:],
        "q": self_sums[0][:, :half],
        "k": self_sums[0][:, half:],
        "v": self_sums[1][:, :half],
        "so": self_sums[1][:, half:],
    }
    names = list(mats)
    squares = {n: g * g for n, g in mats.items()}
    col_parts = jnp.concatenate([jnp.sum(squares[n], axis=0) for n in names])
    row_parts = jnp.stack([jnp.sum(squares[n], axis=1) for n in names])
    gains = jnp.concatenate([gain_a, gain_b, gain_c], axis=0)
    chunk = row_parts.shape[1]
    sent = jnp.concatenate(
        [row_parts.reshape(-1), gains.reshape(-1), table_x.reshape(-1), table_o.reshape(-1)]
    )
    got = swap_mp(sent)
    n_rows = row_parts.size
    row_full = row_parts + got[:n_rows].reshape(row_parts.shape)
    gains = gains + got[n_rows : n_rows + gains.size].reshape(gains.shape)
    t0 = n_rows + gains.size
    table_o = table_o + got[t0 : t0 + table_o.size].reshape(table_o.shape)
    table_x = table_x + got[t0 + table_o.size :].reshape(table_x.shape)
    total_parts = jnp.sum(row_full, axis=1)
    summed = sum_dp(
        jnp.concatenate(
            [col_parts, total_parts, gains.reshape(-1), table_o.reshape(-1), table_x.reshape(-1)]
        ),
        n_data,
    )
    n_cols = col_parts.size
    n_mats = len(names)
    col_all = summed[:n_cols]
    totals = summed[n_cols : n_cols + n_mats]
    g0_at = n_cols + n_mats
    gain_grads = summed[g0_at : g0_at + gains.size].reshape(gains.shape)
    tables = summed[g0_at + gains.size :]
    table_grad = tables[: table_o.size].reshape(table_o.shape)
    grad_norm = jnp.sqrt(
        jnp.sum(totals) + jnp.sum(gain_grads * gain_grads) + jnp.sum(tables * tables)
    )
    cols = {}
    start = 0
    for n in names:
        size = mats[n].shape[1]
        cols[n] = col_all[start : start + size]
        start += size

    def update(name, weight_part):
        i = names.index(name)
        size = mats[name].shape[1] * 2
        row = row_full[i] / size + stat_eps
        col = cols[name] / depth + stat_eps
        mean = totals[i] / (size * depth) + stat_eps
        v_hat = row[:, None] * col[None, :] / mean
        return weight_part.astype(F32) - learn_rate * mats[name] * lax.rsqrt(v_hat), row, col

    def natural(members, weight):
        part = lax.dynamic_slice_in_dim(weight, dp * chunk, chunk, weight.ndim - 2)
        if weight.ndim == 2:
            return list(update(members[0], part))
        done = [update(n, part[i]) for i, n in enumerate(members)]
        return [jnp.stack(v) for v in zip(*done)]

    def turned(name, weight):
        part = lax.dynamic_slice_in_dim(weight, dp * chunk, chunk, 1).T
        new, row, col = update(name, part)
        return [new.T, col, row]

    outs = [result, grad_in, d_mem, gain_grads, table_grad]
    outs += natural(("q", "k", "v"), self_qkv)
    outs += turned("so", self_out)
    outs += natural(("cq",), cross_q)
    outs += natural(("ck", "cv"), cross_kv)
    outs += turned("co", cross_out)
    outs += natural(("gate", "up"), ffn_in)
    outs += turned("down", ffn_out)
    return tuple(outs + [grad_norm])


def solution(mesh):
    placed = (
        P(("dp", "mp"), None),
        P("dp", None),
        P(("dp", "mp"), None),
        P("dp"),
        P("dp"),
        P(),
        P(None, "mp"),
        P(None, None, "mp"),
        P("mp", None),
        P(None, "mp"),
        P(None, None, "mp"),
        P("mp", None),
        P(None, None, "mp"),
        P("mp", None),
    )
    return jax.shard_map(
        body,
        mesh=mesh,
        in_specs=placed,
        out_specs=(
            P(("dp", "mp"), None),
            P(("dp", "mp"), None),
            P(("dp", "mp"), None),
            P(),
            P(None, "mp"),
            P(None, "dp", "mp"),
            P(None, "dp"),
            P(None, "mp"),
            P("mp", "dp"),
            P("mp"),
            P("dp"),
            P("dp", "mp"),
            P("dp"),
            P("mp"),
            P(None, "dp", "mp"),
            P(None, "dp"),
            P(None, "mp"),
            P("mp", "dp"),
            P("mp"),
            P("dp"),
            P(None, "dp", "mp"),
            P(None, "dp"),
            P(None, "mp"),
            P("mp", "dp"),
            P("mp"),
            P("dp"),
            P(),
        ),
        check_vma=False,
    )
```

```python
import functools

import jax
import jax.numpy as jnp
import numpy as np
from jax import lax
from jax.experimental import pallas as pl
from jax.experimental.pallas import tpu as pltpu
from jax.sharding import PartitionSpec as P

BUCKETS = 32
MAX_DIST = 128
HD = 64
LANE = 128
VMEM_BYTES = 64 * 1024 * 1024 - 512 * 1024
QB = 256
norm_eps = 1e-06
stat_eps = 1e-30
masked_value = -1e30
learn_rate = 0.04
highest = lax.Precision.HIGHEST
F32 = jnp.float32
BF16 = jnp.bfloat16
VMEM = pl.BlockSpec(memory_space=pltpu.VMEM)
SMEM = pl.BlockSpec(memory_space=pltpu.SMEM)


def bucket_of(dist):
    exact_span = BUCKETS // 2
    dist = np.maximum(dist, 0)
    log_ratio = np.log(np.maximum(dist, 1) / exact_span) / np.log(MAX_DIST / exact_span)
    far = np.minimum(
        exact_span + np.floor(log_ratio * (BUCKETS - exact_span)).astype(np.int64), BUCKETS - 1
    )
    return np.where(dist < exact_span, dist, far).astype(np.int32)


def nn(a, b):
    return lax.dot_general(a, b, (((1,), (0,)), ((), ())), preferred_element_type=F32)


def nt(a, b):
    return lax.dot_general(a, b, (((1,), (1,)), ((), ())), preferred_element_type=F32)


def tn(a, b):
    return lax.dot_general(a, b, (((0,), (0,)), ((), ())), preferred_element_type=F32)


class Copies:
    def __init__(self, pairs_in, pairs_out, sem_in, sem_out):
        self.reads = [
            (dst, pltpu.make_async_copy(src, dst, sem_in.at[i]))
            for i, (src, dst) in enumerate(pairs_in)
        ]
        self.writes = [
            (src, pltpu.make_async_copy(src, dst, sem_out.at[i]))
            for i, (src, dst) in enumerate(pairs_out)
        ]
        self.pairs_out, self.sem_out = pairs_out, sem_out
        self.pending, self.begun = list(self.reads), []
        for _, copy in self.reads:
            copy.start()

    def wait(self, *refs):
        for ref in refs:
            for entry in self.pending:
                if entry[0] is ref:
                    entry[1].wait()
                    self.pending = [e for e in self.pending if e is not entry]
                    break

    def flush(self, *refs):
        for ref in refs:
            for src, copy in self.writes:
                if src is ref:
                    copy.start()
                    self.begun.append(copy)

    def flush_columns(self, start, size, *refs):
        cols = pl.ds(start, size)
        for src, dst in self.pairs_out:
            if not any(src is r for r in refs):
                continue
            copy = pltpu.make_async_copy(
                src.at[..., cols], dst.at[..., cols], self.sem_out.at[len(self.begun)]
            )
            copy.start()
            self.begun.append(copy)

    def close(self):
        assert not self.pending and len(self.begun) >= len(self.writes)
        for copy in self.begun:
            copy.wait()


def columns(array, start, size):
    return cut(array, -1, start, size)


def leading(array, start, size):
    return cut(array, 0, start, size)


def cut(array, axis, start, size):
    array, cuts = array if isinstance(array, tuple) else (array, ())
    return (array, cuts + ((axis % array.ndim, start, size),))


def dma_call(kernel, outs, args, n_smem=0, scratch=(), flops=0, n_writes=0):
    args = [a if isinstance(a, tuple) else (a, ()) for a in args]
    arrays = [a[0] for a in args]
    n_in, n_out = len(arrays), len(outs)
    held = []
    for i, (a, cuts) in enumerate(args):
        shape = list(a.shape)
        for axis, _, size in cuts:
            shape[axis] = size
        shape = tuple(shape)
        held.append((pltpu.SMEM if i < n_smem else pltpu.VMEM)(shape, a.dtype))
    held += [pltpu.VMEM(o.shape, o.dtype) for o in outs]

    def part(ref, arg):
        index = [slice(None)] * arg[0].ndim
        for axis, start, size in arg[1]:
            index[axis] = pl.ds(start() if callable(start) else start, size)
        return ref.at[tuple(index)] if arg[1] else ref

    def run(*refs):
        given, made = refs[:n_in], refs[n_in : n_in + n_out]
        local = refs[n_in + n_out : 2 * (n_in + n_out)]
        rest, (sem_in, sem_out) = refs[2 * (n_in + n_out) : -2], refs[-2:]
        sources = [part(r, a) for r, a in zip(given, args)]
        io = Copies(
            list(zip(sources, local[:n_in])), list(zip(local[n_in:], made)), sem_in, sem_out
        )
        kernel(io, *local, *rest)
        io.close()

    moved = sum(h.shape[0] * int(np.prod(h.shape[1:])) * np.dtype(h.dtype).itemsize for h in held)
    return pl.pallas_call(
        run,
        out_shape=list(outs),
        in_specs=[pl.BlockSpec(memory_space=pltpu.HBM)] * n_in,
        out_specs=[pl.BlockSpec(memory_space=pltpu.HBM)] * n_out,
        scratch_shapes=held
        + list(scratch)
        + [pltpu.SemaphoreType.DMA((n_in,)), pltpu.SemaphoreType.DMA((max(n_out, n_writes),))],
        compiler_params=pltpu.CompilerParams(vmem_limit_bytes=VMEM_BYTES),
        cost_estimate=pl.CostEstimate(flops=flops, bytes_accessed=moved, transcendentals=0),
    )(*arrays)


def sds(shape, dtype):
    return jax.ShapeDtypeStruct(shape, dtype)


def head_masks(dtype):
    lane = lax.broadcasted_iota(jnp.int32, (1, LANE), 1)
    return [(lane < HD).astype(dtype), (lane >= HD).astype(dtype)]


def bias_chunks(bias_ref, head, first, count, blocks):
    near = bias_ref[head, 0:LANE, :]
    diag = bias_ref[head, LANE : 2 * LANE, :]
    const = jnp.broadcast_to(bias_ref[head, 0:1, :], (LANE, LANE))
    none = jnp.full((LANE, LANE), masked_value, F32)

    def tile(offset):
        return none if offset < 0 else diag if offset == 0 else near if offset == 1 else const

    return [
        jnp.concatenate([tile(first + i - j) for i in range(blocks)], axis=1)
        for j in range(count)
    ]


def score_chunks(keys_masked, queries, bias_ref, head, first, count, length):
    width = queries.shape[0]
    scores = nt(keys_masked[: count * LANE], queries)
    row = lax.broadcasted_iota(jnp.int32, (LANE, width), 0)
    chunks = []
    if bias_ref is not None:
        bias = bias_chunks(bias_ref, head, first, count, width // LANE)
    for j in range(count):
        part = scores[j * LANE : (j + 1) * LANE]
        if bias_ref is not None:
            part = part + bias[j]
        chunks.append(jnp.where(row < length - j * LANE, part, masked_value))
    return chunks


def attend_pairs(q_ref, k_ref, v_ref, o_ref, lse_ref, bias_ref, length, lse_base=0):
    width = q_ref.shape[1]
    keys = k_ref.shape[0]
    masks = head_masks(BF16)

    def pair(p, carry):
        lanes = pl.ds(pl.multiple_of(p * LANE, LANE), LANE)
        k_pair = k_ref[:, lanes]
        v_t = jnp.transpose(v_ref[:, lanes].astype(F32)).astype(BF16)
        halves = []
        for t in range(2):
            chunks = score_chunks(
                k_pair * masks[t], q_ref[:, lanes], bias_ref, 2 * p + t, 0, keys // LANE, length
            )
            top = functools.reduce(
                jnp.maximum, [jnp.max(c, axis=0, keepdims=True) for c in chunks]
            )
            exps = [jnp.exp(c - top) for c in chunks]
            total = functools.reduce(jnp.add, [jnp.sum(c, axis=0, keepdims=True) for c in exps])
            scale = 1.0 / total
            probs = jnp.concatenate([(c * scale).astype(BF16) for c in exps], axis=0)
            halves.append(nn(v_t[t * HD : (t + 1) * HD], probs))
            lse_ref[lse_base + 2 * p + t] = top + jnp.log(total)
        o_ref[:, lanes] = jnp.transpose(jnp.concatenate(halves, axis=0)).astype(BF16)
        return carry

    lax.fori_loop(0, width // LANE, pair, 0)


def attend_back_pairs(
    q_ref, k_ref, v_ref, do_ref, dqkv_ref, lse_ref, bias_ref, length, lse_base=0, diag_ref=None
):
    rows, width = q_ref.shape
    keys = k_ref.shape[0]
    masks = head_masks(BF16)
    lane_id = lax.broadcasted_iota(jnp.int32, (1, QB), 1)

    def pair(p, carry):
        lanes = pl.ds(pl.multiple_of(p * LANE, LANE), LANE)
        k_pair = k_ref[:, lanes]
        v_pair = v_ref[:, lanes]
        k_t = jnp.transpose(k_pair.astype(F32)).astype(BF16)
        dv = [jnp.zeros((LANE, LANE), F32) for _ in range(keys // LANE)]
        dk = [jnp.zeros((LANE, LANE), F32) for _ in range(keys // LANE)]
        halves = []
        for t in range(2):
            k_m = k_pair * masks[t]
            v_m = v_pair * masks[t]
            outs = []
            near_sum = jnp.zeros((LANE, LANE), F32)
            diag_sum = jnp.zeros((LANE, LANE), F32)
            far_sum = jnp.zeros((1, LANE), F32)
            for block in range(rows // QB):
                count = 2 * block + 2 if bias_ref is not None else keys // LANE
                q_blk = q_ref[pl.ds(block * QB, QB), lanes]
                do_blk = do_ref[pl.ds(block * QB, QB), lanes]
                chunks = score_chunks(k_m, q_blk, bias_ref, 2 * p + t, 2 * block, count, length)
                lse = lse_ref[lse_base + 2 * p + t, :, block * QB : (block + 1) * QB]
                probs = [jnp.exp(c - lse) for c in chunks]
                d_probs = nt(v_m[: count * LANE], do_blk)
                d_probs = [d_probs[j * LANE : (j + 1) * LANE] for j in range(count)]
                dot = functools.reduce(
                    jnp.add,
                    [jnp.sum(a * b, axis=0, keepdims=True) for a, b in zip(probs, d_probs)],
                )
                d_scores = [
                    (a * (b - dot)).astype(BF16) for a, b in zip(probs, d_probs)
                ]
                if diag_ref is not None:
                    for j in range(count):
                        wide = d_scores[j].astype(F32)
                        left, right = wide[:, :LANE], wide[:, LANE:]
                        offset = 2 * block - j
                        if offset == -1:
                            diag_sum = diag_sum + right
                        elif offset == 0:
                            diag_sum = diag_sum + left
                            near_sum = near_sum + right
                        elif offset == 1:
                            near_sum = near_sum + left
                            far_sum = far_sum + jnp.sum(right, axis=0, keepdims=True)
                        else:
                            far_sum = far_sum + jnp.sum(left + right, axis=0, keepdims=True)
                d_all = jnp.concatenate(d_scores, axis=0)
                p_all = jnp.concatenate([a.astype(BF16) for a in probs], axis=0)
                dv_new = nn(p_all, do_blk * masks[t])
                dk_new = nn(d_all, q_blk * masks[t])
                for j in range(count):
                    dv[j] = dv[j] + dv_new[j * LANE : (j + 1) * LANE]
                    dk[j] = dk[j] + dk_new[j * LANE : (j + 1) * LANE]
                outs.append(nn(k_t[t * HD : (t + 1) * HD, : count * LANE], d_all))
            halves.append(jnp.concatenate(outs, axis=1))
            if diag_ref is not None:
                both = jnp.concatenate([near_sum, diag_sum], axis=0)
                both = jnp.concatenate([both, jnp.zeros_like(both)], axis=1)
                acc = jnp.zeros((8, QB), F32)
                for g in range(QB // 8):
                    piece = both[8 * g : 8 * g + 8]
                    turn = (LANE - 8 * g) % QB
                    acc = acc + (pltpu.roll(piece, turn, 1) if turn else piece)
                line = acc[0:1]
                for g in range(1, 8):
                    line = line + pltpu.roll(acc, QB - g, 1)[g : g + 1]
                far_total = jnp.sum(far_sum, axis=1, keepdims=True)
                diag_ref[2 * p + t] = line + jnp.where(lane_id == QB - 1, far_total, 0.0)
        dq_t = jnp.concatenate(halves, axis=0)
        dqkv_ref[:, lanes] = jnp.transpose(dq_t).astype(BF16)
        lanes_k = pl.ds(pl.multiple_of(width + p * LANE, LANE), LANE)
        lanes_v = pl.ds(pl.multiple_of(2 * width + p * LANE, LANE), LANE)
        dqkv_ref[:, lanes_k] = jnp.concatenate(dk, axis=0).astype(BF16)
        dqkv_ref[:, lanes_v] = jnp.concatenate(dv, axis=0).astype(BF16)
        return carry

    lax.fori_loop(0, width // LANE, pair, 0)


def row_blocks(rows, step, fn):
    def one(i, carry):
        fn(pl.ds(pl.multiple_of(i * step, step), step))
        return carry

    lax.fori_loop(0, rows // step, one, 0)


def rms_rows(h, gain):
    return h * lax.rsqrt(jnp.mean(h * h, axis=-1, keepdims=True) + norm_eps) * gain


def rms_back(h, gain, dn):
    inv = lax.rsqrt(jnp.mean(h * h, axis=-1, keepdims=True) + norm_eps)
    gd = gain * dn
    dh = gd * inv - h * (jnp.mean(gd * h, axis=-1, keepdims=True) * (inv * inv * inv))
    return dh, jnp.sum(dn * h * inv, axis=0, keepdims=True)


ROWS = 128
NB = 768


def col_blocks(width):
    return [slice(i, min(i + NB, width)) for i in range(0, width, NB)]


def self_forward(first, io, *refs):
    if first:
        lens, x_ref, gain_ref, w_ref, table_ref, spread_ref, a_ref, q_ref, k_ref, v_ref, o_ref, lse_ref, bias_ref = refs

        io.wait(x_ref, gain_ref)

        def norm(rows):
            a_ref[rows, :] = rms_rows(x_ref[rows, :].astype(F32), gain_ref[0:1, :]).astype(BF16)

        row_blocks(x_ref.shape[0], ROWS, norm)
        io.flush(a_ref)
    else:
        lens, a_ref, w_ref, table_ref, spread_ref, q_ref, k_ref, v_ref, o_ref, lse_ref, bias_ref = refs
    io.wait(table_ref, spread_ref)
    lines = lax.dot_general(
        table_ref[...], spread_ref[...], (((1,), (1,)), ((), ())), precision=highest,
        preferred_element_type=F32,
    )
    row = lax.broadcasted_iota(jnp.int32, (QB, LANE), 0)
    col = lax.broadcasted_iota(jnp.int32, (QB, LANE), 1)
    for h in range(bias_ref.shape[0]):
        line = jnp.broadcast_to(lines[h : h + 1, :], (QB, QB))
        tile = pltpu.roll(line, 0, 1, stride=1, stride_axis=0)[:, :LANE]
        bias_ref[h] = jnp.where(col - row + LANE < 0, masked_value, tile)
    io.flush(bias_ref)
    io.wait(lens, a_ref, w_ref)
    for i, ref in enumerate((q_ref, k_ref, v_ref)):
        ref[...] = nn(a_ref[...], w_ref[i]).astype(BF16)
        io.flush(ref)
    attend_pairs(q_ref, k_ref, v_ref, o_ref, lse_ref, bias_ref, lens[lax.axis_index("mp")])
    io.flush(o_ref, lse_ref)


def cross_forward(
    io, lens, x_ref, gain_ref, m_ref, oo, on, woo, won, wqo, wqn, wkvo, wkvn, wco, wcn,
    h1_ref, b_ref, qo, qn, ko, kn, vo, vn, oco, ocn, lse_ref, h2_ref, c_ref,
):
    io.wait(lens, m_ref)
    for k, v, w in ((ko, vo, wkvo), (kn, vn, wkvn)):
        io.wait(w)
        k[...] = nn(m_ref[...], w[0]).astype(BF16)
        v[...] = nn(m_ref[...], w[1]).astype(BF16)
        io.flush(k, v)
    io.wait(x_ref, gain_ref, oo, on, woo, won)
    for c in col_blocks(x_ref.shape[1]):
        h1_ref[:, c] = x_ref[:, c].astype(F32) + nn(oo[...], woo[:, c]) + nn(on[...], won[:, c])

    def first(rows):
        b_ref[rows, :] = rms_rows(h1_ref[rows, :], gain_ref[1:2, :]).astype(BF16)

    row_blocks(x_ref.shape[0], ROWS, first)
    io.flush(h1_ref, b_ref)
    io.wait(wqo, wqn)
    qo[...] = nn(b_ref[...], wqo[...]).astype(BF16)
    qn[...] = nn(b_ref[...], wqn[...]).astype(BF16)
    io.flush(qo, qn)
    heads = qo.shape[1] // HD
    length = lens[lax.axis_index("mp")]
    attend_pairs(qo, ko, vo, oco, lse_ref, None, length)
    attend_pairs(qn, kn, vn, ocn, lse_ref, None, length, heads)
    io.flush(oco, ocn, lse_ref)
    io.wait(wco, wcn)
    for c in col_blocks(x_ref.shape[1]):
        h2_ref[:, c] = h1_ref[:, c] + nn(oco[...], wco[:, c]) + nn(ocn[...], wcn[:, c])

    def last(rows):
        c_ref[rows, :] = rms_rows(h2_ref[rows, :], gain_ref[2:3, :]).astype(BF16)

    row_blocks(x_ref.shape[0], ROWS, last)
    io.flush(h2_ref, c_ref)


HB = 512


def ffn_hidden(count, io, c_ref, og_ref, *refs):
    root = np.float32(np.sqrt(2.0 / np.pi))
    weights, (nbr, own) = refs[: 2 * count], refs[2 * count :]
    width = own.shape[1] // 3
    io.wait(c_ref, og_ref)
    for i in range(count):
        out = nbr if i < count // 2 else own
        wi, wd = weights[2 * i : 2 * i + 2]
        io.wait(wi, wd)
        at = i % (count // 2) * HB
        gate = nn(c_ref[...], wi[0])
        up = nn(c_ref[...], wi[1])
        d_hid = nt(og_ref[...], wd[...])
        sq = gate * gate
        th = jnp.tanh(root * gate * (1.0 + 0.044715 * sq))
        half = 0.5 + 0.5 * th
        gelu = gate * half
        slope = half + 0.5 * gate * (1.0 - th * th) * (
            root * (1.0 + np.float32(3 * 0.044715) * sq)
        )
        out[:, at : at + HB] = (d_hid * up * slope).astype(BF16)
        out[:, width + at : width + at + HB] = (d_hid * gelu).astype(BF16)
        out[:, 2 * width + at : 2 * width + at + HB] = (gelu * up).astype(BF16)
        if i == count // 2 - 1:
            io.flush(nbr)
    io.flush(own)


def ffn_output(io, h2_ref, og_ref, gain_ref, *refs):
    parts, (res_ref, g1_ref, w1_ref, dgain, acc) = refs[:12], refs[12:]
    for i in (0, 6):
        for k in (0, 2):
            d_ref, w_ref = parts[i + k : i + k + 2]
            io.wait(d_ref, w_ref)
            term = nt(d_ref[...], w_ref[0])
            g1_ref[...] = term if i + k == 0 else g1_ref[...] + term
        h_ref, w_ref = parts[i + 4 : i + 6]
        io.wait(h_ref, w_ref)
        term = nn(h_ref[...], w_ref[...])
        acc[...] = term if i == 0 else acc[...] + term
    io.wait(h2_ref, og_ref, gain_ref)
    dgain[...] = jnp.zeros_like(dgain)

    def last(rows):
        h2 = h2_ref[rows, :]
        res_ref[rows, :] = (h2 + acc[rows, :]).astype(BF16)
        dh, dg = rms_back(h2, gain_ref[2:3, :], g1_ref[rows, :])
        g1 = og_ref[rows, :].astype(F32) + dh
        g1_ref[rows, :] = g1
        w1_ref[rows, :] = g1.astype(BF16)
        dgain[...] += dg

    row_blocks(h2_ref.shape[0], ROWS, last)
    io.flush(res_ref, g1_ref, w1_ref, dgain)


def cross_backward(
    io, lens, w1_ref, g1_ref, h1_ref, gain_ref, qo, qn, ko, kn, vo, vn, lse_ref, wco, wcn, wqo, wqn, wkvo, wkvn,
    do_own, do_nbr, g0_ref, w0_ref, dm_ref, dgain, doo, don,
):
    half = qo.shape[1]
    heads = half // HD
    io.wait(lens, w1_ref, wco, wcn)
    doo[...] = nt(w1_ref[...], wco[...]).astype(BF16)
    don[...] = nt(w1_ref[...], wcn[...]).astype(BF16)
    length = lens[lax.axis_index("mp")]
    io.wait(qn, kn, vn, lse_ref)
    attend_back_pairs(qn, kn, vn, don, do_nbr, lse_ref, None, length, heads)
    io.flush(do_nbr)
    io.wait(qo, ko, vo)
    attend_back_pairs(qo, ko, vo, doo, do_own, lse_ref, None, length)
    io.flush(do_own)
    io.wait(wqo, wqn, wkvo, wkvn)
    for c in col_blocks(w1_ref.shape[1]):
        g0_ref[:, c] = nt(do_own[:, 0:half], wqo[c, :]) + nt(do_nbr[:, 0:half], wqn[c, :])
        dm_ref[:, c] = (
            nt(do_own[:, half : 2 * half], wkvo[0, c, :])
            + nt(do_own[:, 2 * half :], wkvo[1, c, :])
            + nt(do_nbr[:, half : 2 * half], wkvn[0, c, :])
            + nt(do_nbr[:, 2 * half :], wkvn[1, c, :])
        ).astype(BF16)
    io.flush(dm_ref)
    io.wait(g1_ref, h1_ref, gain_ref)
    dgain[...] = jnp.zeros_like(dgain)

    def last(rows):
        dh, dg = rms_back(h1_ref[rows, :], gain_ref[1:2, :], g0_ref[rows, :])
        g0 = g1_ref[rows, :] + dh
        g0_ref[rows, :] = g0
        w0_ref[rows, :] = g0.astype(BF16)
        dgain[...] += dg

    row_blocks(w1_ref.shape[0], ROWS, last)
    io.flush(g0_ref, w0_ref, dgain)


def self_backward(io, lens, w0_ref, wo, q_ref, k_ref, v_ref, lse_ref, bias_ref, out_ref, diag_ref, do_ref):
    io.wait(w0_ref, wo)
    do_ref[...] = nt(w0_ref[...], wo[...]).astype(BF16)
    io.wait(lens, q_ref, k_ref, v_ref, lse_ref, bias_ref)
    attend_back_pairs(
        q_ref, k_ref, v_ref, do_ref, out_ref, lse_ref, bias_ref, lens[lax.axis_index("mp")], 0, diag_ref
    )
    io.flush(out_ref, diag_ref)


def input_backward(io, own, nbr, wo, wn, x_ref, gain_ref, g0_ref, out_ref, dgain, acc):
    half = own.shape[1] // 3
    io.wait(own, nbr, wo, wn)
    for c in col_blocks(x_ref.shape[1]):
        d_a = nt(own[:, 0:half], wo[0, c, :]) + nt(nbr[:, 0:half], wn[0, c, :])
        for i in (1, 2):
            part = slice(i * half, (i + 1) * half)
            d_a = d_a + nt(own[:, part], wo[i, c, :]) + nt(nbr[:, part], wn[i, c, :])
        acc[:, c] = d_a
    io.wait(x_ref, gain_ref, g0_ref)
    dgain[...] = jnp.zeros_like(dgain)

    def some(rows):
        dh, dg = rms_back(x_ref[rows, :].astype(F32), gain_ref[0:1, :], acc[rows, :])
        out_ref[rows, :] = (g0_ref[rows, :] + dh).astype(BF16)
        dgain[...] += dg

    row_blocks(own.shape[0], ROWS, some)
    io.flush(out_ref, dgain)


LINE = (0, 8, 4, 12)
ORDERS = ((1, 2), (2, 1))


def weight_grads(parts, io, *refs):
    outs, total = refs[-1 - 2 * len(parts) : -1], refs[-1]
    rows = outs[0].shape[1]
    device = lax.axis_index("dp")
    for i, jobs in enumerate(parts):
        keep_ref, send_ref = outs[2 * i : 2 * i + 2]
        one, two = ORDERS[i]
        at = 0
        for lo, ln, ro, rn, width in jobs:
            done = 0
            while done < width:
                step = width if width <= 640 else min(512, width - done)
                src = slice(done, done + step)
                io.wait(refs[lo], refs[ro])
                total[:, 0:step] = tn(refs[lo][...], refs[ro][:, src])
                io.wait(refs[ln], refs[rn])
                total[:, 0:step] += tn(refs[ln][...], refs[rn][:, src])
                dst = slice(at + done, at + done + step)
                for out, nears in ((keep_ref, (0, two)), (send_ref, (one, one ^ two))):
                    for j, mask in enumerate([near ^ far for near in nears for far in LINE]):
                        chunk = lax.bitwise_xor(device, jnp.int32(mask))
                        part = total[pl.ds(pl.multiple_of(chunk * rows, 16), rows), 0:step]
                        out[j, :, dst] = part.astype(out.dtype)
                io.flush_columns(at + done, step, keep_ref, send_ref)
                done += step
            at += width


def add_terms(plan, io, *refs):
    at = 0
    outs = refs[-len(plan) :]
    for counts, out in zip(plan, outs):
        start = 0
        for count in counts:
            terms = refs[at : at + count]
            at += count
            io.wait(*terms)
            cols = slice(start, start + terms[0].shape[-1])
            start = cols.stop
            for j in range(out.shape[0]):
                total = terms[0][j]
                for t in terms[1:]:
                    total = total + t[j].astype(F32)
                out[j, :, cols] = total.astype(out.dtype)
        io.flush(out)


def swap_dp(v, mask):
    return lax.ppermute(v, "dp", [(i, i ^ mask) for i in range(16)])


def swap_mp(v):
    return lax.ppermute(v, "mp", [(0, 1), (1, 0)])


def make_grads(parts, depth, n_data):
    if n_data != 16:

        def piece(a):
            if not isinstance(a, tuple):
                return a
            value = a[0]
            for axis, start, size in a[1]:
                start = start() if callable(start) else start
                value = lax.dynamic_slice_in_dim(value, start, size, axis)
            return value

        cols = []
        for job in [job for jobs in parts for job in jobs]:
            lo, ln, ro, rn = [piece(a) for a in job]
            cols.append(tn(lo, ro) + tn(ln, rn))
        return lax.psum_scatter(
            jnp.concatenate(cols, axis=1), "dp", scatter_dimension=0, tiled=True
        )
    arrays, keys, plan, shapes = [], [], [], []
    rows = depth // 16
    for jobs in parts:
        spots = []
        for job in jobs:
            place = []
            for a in job:
                key = (id(a[0]),) + a[1:] if isinstance(a, tuple) else id(a)
                if key not in keys:
                    arrays.append(a)
                    keys.append(key)
                place.append(keys.index(key))
            spots.append(tuple(place) + (job[2][1][-1][2],))
        plan.append(tuple(spots))
        width = sum(job[2][1][-1][2] for job in jobs)
        shapes += [sds((8, rows, width), F32), sds((8, rows, width), BF16)]
    widest = max(job[4] if job[4] <= 640 else 512 for jobs in plan for job in jobs)
    return dma_call(
        functools.partial(weight_grads, tuple(plan)),
        shapes,
        arrays,
        0,
        [pltpu.VMEM((depth, widest), F32)],
        flops=4 * 512 * depth * sum(s.shape[-1] for s in shapes[::2]),
        n_writes=64,
    )


class Reduction:
    def __init__(self, made, n_data, direct=False):
        self.plain = n_data != 16
        self.made, self.direct = made, direct
        self.done = 1
        self.far = []
        if not self.plain:
            self.keeps = list(made[::2])
            self.got = [[swap_dp(v, o[0])] for v, o in zip(made[1::2], ORDERS)]

    def near(self, start, size):
        return [[leading(t, start, size) for t in [k] + g] for k, g in zip(self.keeps, self.got)]

    def sends(self):
        rows, widths = self.keeps[0].shape[1], [k.shape[2] for k in self.keeps]
        if self.done == 1:
            parts = self.near(4, 4)
            shapes = [sds((4, rows, w), BF16) for w in widths]
            return [(len(p),) for p in parts], shapes, [t for p in parts for t in p]
        if self.direct:
            spots = ((1, 1), (2, 1), (3, 1))
        else:
            spots = ((2, 2),) if self.done == 2 else ((1, 1),)
        plan, shapes, terms = [], [], []
        for start, size in spots:
            parts, at = self.near(start, size), 0
            for part, w in zip(parts, widths):
                part += [leading(columns(t, at, w), start, size) for t in self.far]
                at += w
            plan.append(tuple(len(p) for p in parts))
            shapes.append(sds((size, rows, sum(widths)), BF16))
            terms += [t for part in parts for t in part]
        return plan, shapes, terms

    def sent(self, sends):
        if self.done == 1:
            for got, send, order in zip(self.got, sends, ORDERS):
                got.append(swap_dp(send, order[1]))
        elif self.direct:
            self.far = [swap_dp(v, m) for v, m in zip(sends, LINE[1:])]
        else:
            self.far.append(swap_dp(sends[0], 4 if self.done == 2 else 8))
        self.done += 1

    def terms(self):
        if self.plain:
            return [[self.made[None]]]
        parts, at = self.near(0, 1), 0
        for part, k in zip(parts, self.keeps):
            part += [leading(columns(t, at, k.shape[2]), 0, 1) for t in self.far]
            at += k.shape[2]
        return parts


def exchange(*steps, others=()):
    steps = [r for r in steps if not r.plain]
    if not steps:
        return []
    made = [r.sends() for r in steps]
    plan = [p for m in made for p in m[0]]
    shapes = [p for m in made for p in m[1]]
    terms = [p for m in made for p in m[2]]
    if others:
        terms[0] = (after(terms[0][0], *others), terms[0][1])
    sends = dma_call(functools.partial(add_terms, tuple(plan)), shapes, terms)
    at = 0
    for r, m in zip(steps, made):
        r.sent(sends[at : at + len(m[0])])
        at += len(m[0])
    return list(sends)


def squares_of(mats, first, all_ref, cols_ref, row_sums):
    rows = all_ref.shape[0]
    lane = lax.broadcasted_iota(jnp.int32, (rows, LANE), 1)
    for i, (start, width) in enumerate(mats):
        part = all_ref[:, start : start + width]
        sq = part * part
        cols_ref[:, start : start + width] = jnp.sum(sq, axis=0, keepdims=True)
        row_sums = row_sums + jnp.where(lane == first + i, jnp.sum(sq, axis=1, keepdims=True), 0.0)
    return row_sums


def end_sums(counts, io, refs, all_ref):
    start = at = 0
    for count in counts:
        terms = refs[at : at + count]
        io.wait(*terms)
        total = terms[0][0]
        for t in terms[1:]:
            total = total + t[0].astype(F32)
        all_ref[:, start : start + total.shape[1]] = total
        at += count
        start += total.shape[1]


def early_statistics(counts, mats, io, *refs):
    all_ref, cols_ref, rows_ref = refs[-3:]
    end_sums(counts, io, refs, all_ref)
    rows_ref[...] = squares_of(mats, 0, all_ref, cols_ref, jnp.zeros_like(rows_ref))
    io.flush(all_ref, cols_ref, rows_ref)


def statistics(counts, mats, first, io, *refs):
    all_ref, pack_ref, cols_ref = refs[-3:]
    rows_ref, spread = refs[-10], refs[-4]
    gains, diags = refs[-9:-6], refs[-6:-4]
    io.wait(rows_ref, *gains, *diags, spread)
    pack_ref[...] = jnp.zeros_like(pack_ref)
    for i, gain in enumerate(gains):
        pack_ref[i : i + 1, :] = gain[...]
    for i, diag in enumerate(diags):
        heads = diag.shape[0]
        lines = jnp.concatenate([diag[h] for h in range(heads)], axis=0)
        pack_ref[8 : 8 + heads, i * LANE : i * LANE + BUCKETS] = lax.dot_general(
            lines, spread[...], (((1,), (0,)), ((), ())), precision=highest,
            preferred_element_type=F32,
        )
    end_sums(counts, io, refs, all_ref)
    rows = all_ref.shape[0]
    pack_ref[16 : 16 + rows, 0:LANE] = squares_of(mats, first, all_ref, cols_ref, rows_ref[...])
    io.flush(all_ref, pack_ref, cols_ref)


def merge_kernel(io, own_ref, got_ref, early_ref, late_ref, out_ref, rows_ref):
    io.wait(own_ref, got_ref, early_ref, late_ref)
    rows = rows_ref.shape[0]
    n_early, depth = early_ref.shape[1], own_ref.shape[1]
    n_all = n_early + late_ref.shape[1]
    full = own_ref[16 : 16 + rows, 0:LANE] + got_ref[16 : 16 + rows, 0:LANE]
    rows_ref[...] = full
    out_ref[:, 0:n_early] = early_ref[...]
    out_ref[:, n_early:n_all] = late_ref[...]
    at = n_all
    for i in range(3):
        out_ref[:, at : at + depth] = own_ref[i : i + 1, :] + got_ref[i : i + 1, :]
        at += depth
    out_ref[:, at : at + LANE] = jnp.sum(full, axis=0, keepdims=True)
    for side in range(2):
        mine = own_ref[8:16, side * LANE : (side + 1) * LANE]
        theirs = got_ref[8:16, (1 - side) * LANE : (2 - side) * LANE]
        both = mine + theirs
        for h in range(8):
            at += LANE
            out_ref[:, at : at + LANE] = both[h : h + 1]
    io.flush(out_ref, rows_ref)


def turn(v):
    rows = v.shape[0]
    if rows < LANE:
        v = jnp.concatenate([v, jnp.zeros((LANE - rows, v.shape[1]), v.dtype)], axis=0)
    return jnp.transpose(v)[:, :rows]


def update_kernel(plan, n_terms, io, *refs):
    terms = refs[:n_terms]
    rows_ref, early_ref, late_ref = refs[n_terms : n_terms + 3]
    weights = refs[n_terms + 3 : n_terms + 3 + len(plan)]
    outs = refs[n_terms + 3 + len(plan) :]
    io.wait(*terms)
    line = functools.reduce(jnp.add, [p[...] for p in terms])
    n_early = early_ref.shape[1]
    n_all = n_early + late_ref.shape[1]
    gain_ref, table_ref, norm_ref = outs[0], outs[1], outs[-1]
    depth = gain_ref.shape[1]
    gains_at, totals_at = n_all, n_all + 3 * depth
    tables_at = totals_at + LANE
    for i in range(3):
        gain_ref[i : i + 1, :] = line[:, gains_at + i * depth : gains_at + (i + 1) * depth]
    for h in range(table_ref.shape[0]):
        at = tables_at + h * LANE
        table_ref[h : h + 1, :] = line[:, at : at + BUCKETS]
    totals = line[:, totals_at:tables_at]
    gains, tables = line[:, gains_at:totals_at], line[:, tables_at:]
    squares = (
        jnp.sum(gains * gains, axis=1, keepdims=True)
        + jnp.sum(tables * tables, axis=1, keepdims=True)
        + jnp.sum(totals, axis=1, keepdims=True)
    )
    norm_ref[...] = jnp.sqrt(squares)
    io.flush(gain_ref, table_ref, norm_ref)
    io.wait(rows_ref, early_ref, late_ref)
    row_sums = rows_ref[...]
    row_lines = turn(row_sums)
    at = 2
    for (natural, members), weight in zip(plan, weights):
        new_ref, row_out, col_out = outs[at : at + 3]
        at += 3
        io.wait(weight)
        for k, (i, start, width) in enumerate(members):
            size = 2 * width
            by_row = row_sums[:, i : i + 1] / size + stat_eps
            by_col = line[:, start : start + width] / depth + stat_eps
            mean = totals[:, i : i + 1] / (size * depth) + stat_eps
            if start < n_early:
                grad = early_ref[:, start : start + width]
            else:
                grad = late_ref[:, start - n_early : start - n_early + width]
            change = (
                learn_rate
                * grad
                * lax.rsqrt(by_row * by_col / mean)
            )
            row_line = row_lines[i : i + 1, :] / size + stat_eps
            new_ref[k] = weight[k].astype(F32) - change
            row_out[k : k + 1, :] = row_line if natural else by_col
            col_out[k : k + 1, :] = by_col if natural else row_line
        io.flush(new_ref, row_out, col_out)


def after(value, *others):
    return lax.optimization_barrier((value,) + others)[0]


def body(
    tokens,
    memory,
    out_grad,
    tgt_lens,
    mem_lens,
    norm_gains,
    rel_table,
    self_qkv,
    self_out,
    cross_q,
    cross_kv,
    cross_out,
    ffn_in,
    ffn_out,
):
    n_data = lax.axis_size("dp")
    mp = lax.axis_index("mp")
    dp = lax.axis_index("dp")
    rows = tokens.shape[0]
    depth = tokens.shape[1]
    heads = rel_table.shape[1]
    half = heads * HD
    width = ffn_out.shape[0]
    chunk = depth // n_data
    qkv_n = swap_mp(self_qkv)
    table = rel_table.T
    table_n = swap_mp(table)
    so_n = swap_mp(self_out)
    ckv_n = swap_mp(cross_kv)
    cq_n = swap_mp(cross_q)
    co_n = swap_mp(cross_out)

    dist = np.arange(QB)
    line_dist = np.where(dist < LANE, dist + LANE, dist - LANE)
    spread = jnp.asarray((bucket_of(line_dist)[:, None] == np.arange(BUCKETS)).astype(np.float32))
    gather = jnp.asarray((bucket_of(dist)[:, None] == np.arange(BUCKETS)).astype(np.float32))

    attn_flops = 4 * rows * rows * HD * heads
    bias_shape = sds((heads, QB, LANE), F32)
    act = sds((rows, half), BF16)
    wide = sds((rows, depth), BF16)
    full = sds((rows, depth), F32)
    gain_row = sds((1, depth), F32)
    lse = sds((heads, 1, rows), F32)
    lse2 = sds((2 * heads, 1, rows), F32)
    a, qs_o, ks_o, vs_o, os_o, lses_o, bias_o = dma_call(
        functools.partial(self_forward, True),
        [wide, act, act, act, act, lse, bias_shape],
        [tgt_lens, tokens, norm_gains, self_qkv, table, spread],
        1,
        flops=6 * rows * depth * half + attn_flops,
    )
    a, qkv_n, table_n, so_n, cq_n, ckv_n, co_n, ffn_in_b, ffn_out_b, out_grad_b = lax.optimization_barrier(
        (a, qkv_n, table_n, so_n, cq_n, ckv_n, co_n, ffn_in, ffn_out, out_grad)
    )
    fi_n = swap_mp(ffn_in_b)
    fo_n = swap_mp(ffn_out_b)
    og_n = swap_mp(out_grad_b)
    a_n = swap_mp(a)
    qs_n, ks_n, vs_n, os_n, lses_n, bias_n = dma_call(
        functools.partial(self_forward, False),
        [act, act, act, act, lse, bias_shape],
        [tgt_lens, a, qkv_n, table_n, spread],
        1,
        flops=6 * rows * depth * half + attn_flops,
    )
    mem_own = leading(memory, lambda: pl.multiple_of(lax.axis_index("mp") * rows, rows), rows)
    mem_nbr = leading(memory, lambda: pl.multiple_of((1 - lax.axis_index("mp")) * rows, rows), rows)
    os_n, fi_n, fo_n, og_n, a_n = lax.optimization_barrier((os_n, fi_n, fo_n, og_n, a_n))
    os_x = swap_mp(os_n)
    h1, b, qc_o, qc_n, kc_o, kc_n, vc_o, vc_n, oc_o, oc_n, lsec, h2, c = dma_call(
        cross_forward,
        [full, wide, act, act, act, act, act, act, act, act, lse2, full, wide],
        [mem_lens, tokens, norm_gains, mem_own, os_o, os_n, self_out, so_n, cross_q, cq_n, cross_kv, ckv_n, cross_out, co_n],
        1,
        flops=20 * rows * depth * half + 2 * attn_flops,
    )
    c, os_x = lax.optimization_barrier((c, os_x))
    b_n = swap_mp(b)
    oc_x = swap_mp(oc_n)
    c_n = swap_mp(c)
    hid = sds((rows, 3 * width), BF16)
    count = width // HB
    hidden_weights = []
    for wi, wd in ((fi_n, fo_n), (ffn_in, ffn_out)):
        for i in range(count):
            hidden_weights += [columns(wi, i * HB, HB), leading(wd, i * HB, HB)]
    f_nbr, f_own = dma_call(
        functools.partial(ffn_hidden, 2 * count),
        [hid, hid],
        [c, out_grad] + hidden_weights,
        flops=12 * rows * depth * width,
    )
    f_x = swap_mp(f_nbr)
    output_parts = []
    for f, wi, wd in ((f_nbr, fi_n, fo_n), (f_own, ffn_in, ffn_out)):
        for i in range(2):
            output_parts += [columns(f, i * width, width), leading(wi, i, 1)]
        output_parts += [columns(f, 2 * width, width), wd]
    result, g1, w1, gain_c = dma_call(
        ffn_output,
        [wide, full, wide, gain_row],
        [h2, out_grad, norm_gains] + output_parts,
        0,
        [pltpu.VMEM((rows, depth), F32)],
        flops=12 * rows * depth * width,
    )
    w1_n = swap_mp(w1)
    def pair(own, nbr, start, size):
        return columns(own, start, size), columns(nbr, start, size)

    middle = 3 * width // 2
    w1, f_own = lax.optimization_barrier((w1, f_own))
    ffn_made = make_grads(
        (
            ((c, c_n) + pair(f_own, f_x, 0, middle),),
            (
                (c, c_n) + pair(f_own, f_x, middle, width // 2),
                (out_grad, og_n) + pair(f_own, f_x, 2 * width, width),
            ),
        ),
        depth,
        n_data,
    )
    w1_b = after(w1, b_n, oc_x, *jax.tree.leaves(ffn_made))
    ffn_sum = Reduction(ffn_made, n_data)
    c_own, c_nbr, g0, w0, d_mem, gain_b = dma_call(
        cross_backward,
        [sds((rows, 3 * half), BF16), sds((rows, 3 * half), BF16), full, wide, wide, gain_row],
        [mem_lens, w1_b, g1, h1, norm_gains, qc_o, qc_n, kc_o, kc_n, vc_o, vc_n, lsec, cross_out, co_n, cross_q, cq_n, cross_kv, ckv_n],
        1,
        [pltpu.VMEM((rows, half), BF16), pltpu.VMEM((rows, half), BF16)],
        flops=16 * rows * depth * half + 5 * attn_flops,
    )
    c_x = swap_mp(c_nbr)
    w0_n = swap_mp(w0)
    diag = sds((heads, 1, QB), F32)

    def self_back(d_out, out_w, q, k, v, row_lse, bias):
        return dma_call(
            self_backward,
            [sds((rows, 3 * half), BF16), diag],
            [tgt_lens, d_out, out_w, q, k, v, row_lse, bias],
            1,
            [pltpu.VMEM((rows, half), BF16)],
            flops=2 * rows * depth * half + 3 * attn_flops,
        )

    w0_b = after(w0, w1_n, *exchange(ffn_sum, others=(c_own,)))
    s_nbr, diag_n = self_back(w0_b, so_n, qs_n, ks_n, vs_n, lses_n, bias_n)
    sent = exchange(ffn_sum, others=(s_nbr,))
    if sent:
        w0, w0_n, c_x = lax.optimization_barrier((w0, w0_n, c_x, *sent))[:3]
    cross_made = make_grads(
        (
            (
                (w1, w1_n) + pair(oc_o, oc_x, 0, half),
                (w0, w0_n) + pair(os_o, os_x, 0, half),
                (b, b_n) + pair(c_own, c_x, 0, LANE),
            ),
            (
                (b, b_n) + pair(c_own, c_x, LANE, half - LANE),
                (mem_own, mem_nbr) + pair(c_own, c_x, half, 2 * half),
            ),
        ),
        depth,
        n_data,
    )
    cross_sum = Reduction(cross_made, n_data)
    w0_b, s_nbr = lax.optimization_barrier((w0, s_nbr, *jax.tree.leaves(cross_made)))[:2]
    s_x = swap_mp(s_nbr)
    s_own, diag_o = self_back(w0_b, self_out, qs_o, ks_o, vs_o, lses_o, bias_o)
    s_own, s_x = lax.optimization_barrier((s_own, s_x))
    self_made = make_grads(
        (
            ((a, a_n) + pair(s_own, s_x, 0, 512),),
            ((a, a_n) + pair(s_own, s_x, 512, 3 * half - 512),),
        ),
        depth,
        n_data,
    )
    self_sum = Reduction(self_made, n_data, direct=True)
    sent = exchange(ffn_sum, cross_sum, others=jax.tree.leaves(self_made))
    grad_in, gain_a = dma_call(
        input_backward,
        [wide, gain_row],
        [after(s_own, *sent, *jax.tree.leaves(self_made)), s_nbr, self_qkv, qkv_n, tokens, norm_gains, g0],
        0,
        [pltpu.VMEM((rows, depth), F32)],
        flops=12 * rows * depth * half,
    )
    exchange(self_sum, cross_sum, others=(grad_in,))

    sizes = [width, width, width] + [half] * 8
    starts = [int(v) for v in np.cumsum([0] + sizes[:-1])]
    mats = tuple(zip(starts, sizes))
    n_all = sum(sizes)
    plan = (
        (True, (8, 9, 10)),
        (False, (4,)),
        (True, (5,)),
        (True, (6, 7)),
        (False, (3,)),
        (True, (0, 1)),
        (False, (2,)),
    )
    plan = tuple((n, tuple((i, starts[i], sizes[i]) for i in m)) for n, m in plan)
    weights = (self_qkv, self_out, cross_q, cross_kv, cross_out, ffn_in, ffn_out)
    slices, shapes = [], [sds((3, depth), F32), sds((heads, BUCKETS), F32)]
    for (natural, members), weight in zip(plan, weights):
        count, size = len(members), members[0][2]
        if natural:
            weight = weight.reshape((count,) + weight.shape[-2:])
            part = cut(weight, 1, lambda: pl.multiple_of(lax.axis_index("dp") * chunk, chunk), chunk)
            if n_data != 16:
                part = lax.dynamic_slice_in_dim(weight, dp * chunk, chunk, 1)
        else:
            part = lax.dynamic_slice_in_dim(weight, dp * chunk, chunk, 1).T[None]
        slices.append(part)
        line_sizes = (chunk, size) if natural else (size, chunk)
        shapes += [sds((count, chunk, size), F32)] + [sds((count, n), F32) for n in line_sizes]
    shapes.append(sds((1, 1), F32))
    exchange(cross_sum, others=[grad_in])
    sent = exchange(self_sum, others=[v for v in slices if not isinstance(v, tuple)])
    n_early = starts[8]
    early = ffn_sum.terms() + cross_sum.terms()
    if sent:
        early[0][0] = (after(early[0][0][0], *sent), early[0][0][1])
    grads, cols, row_parts = dma_call(
        functools.partial(early_statistics, tuple(len(t) for t in early), mats[:8]),
        [sds((chunk, n_early), F32), sds((1, n_early), F32), sds((chunk, LANE), F32)],
        [t for part in early for t in part],
    )
    late = self_sum.terms()
    pack_rows = -(-(16 + chunk) // 8) * 8
    late_grads, pack, late_cols = dma_call(
        functools.partial(statistics, tuple(len(t) for t in late), tuple((a - n_early, b) for a, b in mats[8:]), 8),
        [sds((chunk, n_all - n_early), F32), sds((pack_rows, depth), F32), sds((1, n_all - n_early), F32)],
        [t for part in late for t in part] + [row_parts, gain_a, gain_b, gain_c, diag_o, diag_n, gather],
    )
    line, row_sums = dma_call(
        merge_kernel,
        [sds((1, n_all + 3 * depth + 17 * LANE), F32), sds((chunk, LANE), F32)],
        [pack, swap_mp(pack), cols, late_cols],
    )
    if n_data == 16:
        terms = [line]
        for group in ((1, 2, 3), (4, 8, 12)):
            if len(terms) > 1:
                terms = [functools.reduce(jnp.add, terms)]
            terms = terms + [swap_dp(terms[0], m) for m in group]
    else:
        terms = [lax.psum(line, "dp")]

    done = dma_call(
        functools.partial(update_kernel, plan, len(terms)),
        shapes,
        terms + [row_sums, grads, late_grads] + slices,
    )
    finals = [result, grad_in, d_mem, done[0], done[1].T]
    for i, ((natural, _), weight) in enumerate(zip(plan, weights)):
        new, row, col = done[2 + 3 * i : 5 + 3 * i]
        if weight.ndim == 2:
            new, row, col = new[0] if natural else new[0].T, row[0], col[0]
        finals += [new, row, col]
    return tuple(finals + [done[-1][0, 0]])


def solution(mesh):
    placed = (
        P(("dp", "mp"), None),
        P("dp", None),
        P(("dp", "mp"), None),
        P("dp"),
        P("dp"),
        P(),
        P(None, "mp"),
        P(None, None, "mp"),
        P("mp", None),
        P(None, "mp"),
        P(None, None, "mp"),
        P("mp", None),
        P(None, None, "mp"),
        P("mp", None),
    )
    return jax.shard_map(
        body,
        mesh=mesh,
        in_specs=placed,
        out_specs=(
            P(("dp", "mp"), None),
            P(("dp", "mp"), None),
            P(("dp", "mp"), None),
            P(),
            P(None, "mp"),
            P(None, "dp", "mp"),
            P(None, "dp"),
            P(None, "mp"),
            P("mp", "dp"),
            P("mp"),
            P("dp"),
            P("dp", "mp"),
            P("dp"),
            P("mp"),
            P(None, "dp", "mp"),
            P(None, "dp"),
            P(None, "mp"),
            P("mp", "dp"),
            P("mp"),
            P("dp"),
            P(None, "dp", "mp"),
            P(None, "dp"),
            P(None, "mp"),
            P("mp", "dp"),
            P("mp"),
            P("dp"),
            P(),
        ),
        check_vma=False,
    )
```

```python
import functools

import jax
import jax.numpy as jnp
import numpy as np
from jax import lax
from jax.experimental import pallas as pl
from jax.experimental.pallas import tpu as pltpu
from jax.sharding import PartitionSpec as P

BUCKETS = 32
MAX_DIST = 128
HD = 64
LANE = 128
VMEM_BYTES = 64 * 1024 * 1024 - 512 * 1024
QB = 256
AHEAD = 3
norm_eps = 1e-06
stat_eps = 1e-30
masked_value = -1e30
learn_rate = 0.04
highest = lax.Precision.HIGHEST
F32 = jnp.float32
BF16 = jnp.bfloat16
VMEM = pl.BlockSpec(memory_space=pltpu.VMEM)
SMEM = pl.BlockSpec(memory_space=pltpu.SMEM)


def bucket_of(dist):
    exact_span = BUCKETS // 2
    dist = np.maximum(dist, 0)
    log_ratio = np.log(np.maximum(dist, 1) / exact_span) / np.log(MAX_DIST / exact_span)
    far = np.minimum(
        exact_span + np.floor(log_ratio * (BUCKETS - exact_span)).astype(np.int64), BUCKETS - 1
    )
    return np.where(dist < exact_span, dist, far).astype(np.int32)


def nn(a, b):
    return lax.dot_general(a, b, (((1,), (0,)), ((), ())), preferred_element_type=F32)


def nt(a, b):
    return lax.dot_general(a, b, (((1,), (1,)), ((), ())), preferred_element_type=F32)


def tn(a, b):
    return lax.dot_general(a, b, (((0,), (0,)), ((), ())), preferred_element_type=F32)


class Copies:
    def __init__(self, pairs_in, pairs_out, sem_in, sem_out):
        self.reads = [
            (dst, pltpu.make_async_copy(src, dst, sem_in.at[i]))
            for i, (src, dst) in enumerate(pairs_in)
        ]
        self.writes = [
            (src, pltpu.make_async_copy(src, dst, sem_out.at[i]))
            for i, (src, dst) in enumerate(pairs_out)
        ]
        self.pairs_out, self.sem_out = pairs_out, sem_out
        self.pending, self.begun = list(self.reads), []
        for _, copy in self.reads:
            copy.start()

    def wait(self, *refs):
        for ref in refs:
            for entry in self.pending:
                if entry[0] is ref:
                    entry[1].wait()
                    self.pending = [e for e in self.pending if e is not entry]
                    break

    def flush(self, *refs):
        for ref in refs:
            for src, copy in self.writes:
                if src is ref:
                    copy.start()
                    self.begun.append(copy)

    def flush_columns(self, start, size, *refs):
        cols = pl.ds(start, size)
        for src, dst in self.pairs_out:
            if not any(src is r for r in refs):
                continue
            copy = pltpu.make_async_copy(
                src.at[..., cols], dst.at[..., cols], self.sem_out.at[len(self.begun)]
            )
            copy.start()
            self.begun.append(copy)

    def close(self):
        assert not self.pending and len(self.begun) >= len(self.writes)
        for copy in self.begun:
            copy.wait()


def columns(array, start, size):
    return cut(array, -1, start, size)


def leading(array, start, size):
    return cut(array, 0, start, size)


def cut(array, axis, start, size):
    array, cuts = array if isinstance(array, tuple) else (array, ())
    return (array, cuts + ((axis % array.ndim, start, size),))


def dma_call(kernel, outs, args, n_smem=0, scratch=(), flops=0, n_writes=0):
    args = [a if isinstance(a, tuple) else (a, ()) for a in args]
    arrays = [a[0] for a in args]
    n_in, n_out = len(arrays), len(outs)
    held = []
    for i, (a, cuts) in enumerate(args):
        shape = list(a.shape)
        for axis, _, size in cuts:
            shape[axis] = size
        shape = tuple(shape)
        held.append((pltpu.SMEM if i < n_smem else pltpu.VMEM)(shape, a.dtype))
    held += [pltpu.VMEM(o.shape, o.dtype) for o in outs]

    def part(ref, arg):
        index = [slice(None)] * arg[0].ndim
        for axis, start, size in arg[1]:
            index[axis] = pl.ds(start() if callable(start) else start, size)
        return ref.at[tuple(index)] if arg[1] else ref

    def run(*refs):
        given, made = refs[:n_in], refs[n_in : n_in + n_out]
        local = refs[n_in + n_out : 2 * (n_in + n_out)]
        rest, (sem_in, sem_out) = refs[2 * (n_in + n_out) : -2], refs[-2:]
        sources = [part(r, a) for r, a in zip(given, args)]
        io = Copies(
            list(zip(sources, local[:n_in])), list(zip(local[n_in:], made)), sem_in, sem_out
        )
        kernel(io, *local, *rest)
        io.close()

    moved = sum(h.shape[0] * int(np.prod(h.shape[1:])) * np.dtype(h.dtype).itemsize for h in held)
    return pl.pallas_call(
        run,
        out_shape=list(outs),
        in_specs=[pl.BlockSpec(memory_space=pltpu.HBM)] * n_in,
        out_specs=[pl.BlockSpec(memory_space=pltpu.HBM)] * n_out,
        scratch_shapes=held
        + list(scratch)
        + [pltpu.SemaphoreType.DMA((n_in,)), pltpu.SemaphoreType.DMA((max(n_out, n_writes),))],
        compiler_params=pltpu.CompilerParams(vmem_limit_bytes=VMEM_BYTES),
        cost_estimate=pl.CostEstimate(flops=flops, bytes_accessed=moved, transcendentals=0),
    )(*arrays)


def sds(shape, dtype):
    return jax.ShapeDtypeStruct(shape, dtype)


def head_masks(dtype):
    lane = lax.broadcasted_iota(jnp.int32, (1, LANE), 1)
    return [(lane < HD).astype(dtype), (lane >= HD).astype(dtype)]


def bias_chunks(bias_ref, head, first, count, blocks):
    near = bias_ref[head, 0:LANE, :]
    diag = bias_ref[head, LANE : 2 * LANE, :]
    const = jnp.broadcast_to(bias_ref[head, 0:1, :], (LANE, LANE))
    none = jnp.full((LANE, LANE), masked_value, F32)

    def tile(offset):
        return none if offset < 0 else diag if offset == 0 else near if offset == 1 else const

    return [
        jnp.concatenate([tile(first + i - j) for i in range(blocks)], axis=1)
        for j in range(count)
    ]


def score_chunks(keys_masked, queries, bias_ref, head, first, count, length):
    width = queries.shape[0]
    scores = nt(keys_masked[: count * LANE], queries)
    row = lax.broadcasted_iota(jnp.int32, (LANE, width), 0)
    chunks = []
    if bias_ref is not None:
        bias = bias_chunks(bias_ref, head, first, count, width // LANE)
    for j in range(count):
        part = scores[j * LANE : (j + 1) * LANE]
        if bias_ref is not None:
            part = part + bias[j]
        chunks.append(jnp.where(row < length - j * LANE, part, masked_value))
    return chunks


def attend_back_pairs(
    q_ref, k_ref, v_ref, do_ref, grads, lse_ref, bias_ref, length, lse_base=0, diag_ref=None
):
    rows, width = q_ref.shape
    keys = k_ref.shape[0]
    masks = head_masks(BF16)
    lane_id = lax.broadcasted_iota(jnp.int32, (1, QB), 1)
    step = QB
    n_blocks = rows // step
    units = [(h, b) for h in range(width // HD) for b in range(n_blocks)]
    kept = {}

    def pair_values(p):
        if p not in kept:
            lanes = slice(p * LANE, (p + 1) * LANE)
            k_pair, v_pair = k_ref[:, lanes], v_ref[:, lanes]
            kept[p] = (
                [k_pair * m for m in masks],
                [v_pair * m for m in masks],
                jnp.transpose(k_pair.astype(F32)).astype(BF16),
            )
        return kept[p]

    def start(h, block):
        p, t = divmod(h, 2)
        lanes = slice(p * LANE, (p + 1) * LANE)
        count = (block + 1) * step // LANE if bias_ref is not None else keys // LANE
        k_m, v_m, _ = pair_values(p)
        at = slice(block * step, (block + 1) * step)
        q_blk, do_blk = q_ref[at, lanes], do_ref[at, lanes]
        chunks = score_chunks(k_m[t], q_blk, bias_ref, h, block * step // LANE, count, length)
        d_probs = nt(v_m[t][: count * LANE], do_blk)
        return chunks, [d_probs[j * LANE : (j + 1) * LANE] for j in range(count)]

    ahead = start(*units[0])
    sums = {}
    for i, (h, block) in enumerate(units):
        p, t = divmod(h, 2)
        lanes = slice(p * LANE, (p + 1) * LANE)
        at = slice(block * step, (block + 1) * step)
        chunks, d_probs = ahead
        if i + 1 < len(units):
            ahead = start(*units[i + 1])
        count = len(chunks)
        lse = lse_ref[lse_base + h, :, at]
        probs = [jnp.exp(c - lse) for c in chunks]
        dot = functools.reduce(
            jnp.add, [jnp.sum(a * b, axis=0, keepdims=True) for a, b in zip(probs, d_probs)]
        )
        d_scores = [(a * (b - dot)).astype(BF16) for a, b in zip(probs, d_probs)]
        if t == 0 and block == 0:
            sums = dict(
                dv=[None] * (keys // LANE), dk=[None] * (keys // LANE), dq=[[], []]
            )
        if block == 0:
            near_sum = jnp.zeros((LANE, LANE), F32)
            diag_sum = jnp.zeros((LANE, LANE), F32)
            far_sum = jnp.zeros((1, LANE), F32)
        if diag_ref is not None:
            for j in range(count):
                wide = d_scores[j].astype(F32)
                for c in range(step // LANE):
                    tile = wide[:, c * LANE : (c + 1) * LANE]
                    offset = block * step // LANE + c - j
                    if offset == 0:
                        diag_sum = diag_sum + tile
                    elif offset == 1:
                        near_sum = near_sum + tile
                    elif offset > 1:
                        far_sum = far_sum + jnp.sum(tile, axis=0, keepdims=True)
        d_all = jnp.concatenate(d_scores, axis=0)
        p_all = jnp.concatenate([a.astype(BF16) for a in probs], axis=0)
        dv_new = nn(p_all, do_ref[at, lanes] * masks[t])
        dk_new = nn(d_all, q_ref[at, lanes] * masks[t])
        for name, new in (("dv", dv_new), ("dk", dk_new)):
            for j in range(count):
                part = new[j * LANE : (j + 1) * LANE]
                old = sums[name][j]
                sums[name][j] = part if old is None else old + part
        k_t = pair_values(p)[2]
        sums["dq"][t].append(nn(k_t[t * HD : (t + 1) * HD, : count * LANE], d_all))
        if diag_ref is not None and block == n_blocks - 1:
            both = jnp.concatenate([near_sum, diag_sum], axis=0)
            both = jnp.concatenate([both, jnp.zeros_like(both)], axis=1)
            acc = jnp.zeros((8, QB), F32)
            for g in range(QB // 8):
                piece = both[8 * g : 8 * g + 8]
                turned = (LANE - 8 * g) % QB
                acc = acc + (pltpu.roll(piece, turned, 1) if turned else piece)
            line = acc[0:1]
            for g in range(1, 8):
                line = line + pltpu.roll(acc, QB - g, 1)[g : g + 1]
            far_total = jnp.sum(far_sum, axis=1, keepdims=True)
            diag_ref[h] = line + jnp.where(lane_id == QB - 1, far_total, 0.0)
        if t == 1 and block == n_blocks - 1:
            dq_t = jnp.concatenate([jnp.concatenate(v, axis=1) for v in sums["dq"]], axis=0)
            done = (
                jnp.transpose(dq_t),
                jnp.concatenate(sums["dk"], axis=0),
                jnp.concatenate(sums["dv"], axis=0),
            )
            for (ref, first), value in zip(grads, done):
                ref[:, first + p * LANE : first + (p + 1) * LANE] = value.astype(BF16)


def attend_pairs(q_ref, k_ref, v_ref, o_ref, lse_ref, bias_ref, length, lse_base=0):
    rows, width = q_ref.shape
    keys = k_ref.shape[0]
    masks = head_masks(BF16)
    step = QB
    n_blocks = rows // step
    units = [(h, b) for h in range(width // HD) for b in range(n_blocks)]

    def start(h, block):
        p, t = divmod(h, 2)
        lanes = slice(p * LANE, (p + 1) * LANE)
        k_m = k_ref[:, lanes] * masks[t]
        count = (block + 1) * step // LANE if bias_ref is not None else keys // LANE
        q_blk = q_ref[block * step : (block + 1) * step, lanes]
        return score_chunks(k_m, q_blk, bias_ref, h, block * step // LANE, count, length)

    queue = [start(*u) for u in units[:AHEAD]]
    for i, (h, block) in enumerate(units):
        p, t = divmod(h, 2)
        lanes = slice(p * LANE, (p + 1) * LANE)
        chunks = queue.pop(0)
        if i + AHEAD < len(units):
            queue.append(start(*units[i + AHEAD]))
        if t == 0 and block == 0:
            v_t = jnp.transpose(v_ref[:, lanes].astype(F32)).astype(BF16)
            halves = []
        if block == 0:
            outs = []
        top = functools.reduce(jnp.maximum, [jnp.max(c, axis=0, keepdims=True) for c in chunks])
        exps = [jnp.exp(c - top) for c in chunks]
        total = functools.reduce(jnp.add, [jnp.sum(c, axis=0, keepdims=True) for c in exps])
        scale = 1.0 / total
        probs = jnp.concatenate([(c * scale).astype(BF16) for c in exps], axis=0)
        outs.append(nn(v_t[t * HD : (t + 1) * HD, : probs.shape[0]], probs))
        lse_ref[lse_base + h, :, block * step : (block + 1) * step] = top + jnp.log(total)
        if block == n_blocks - 1:
            halves.append(jnp.concatenate(outs, axis=1))
            if t == 1:
                o_ref[:, lanes] = jnp.transpose(jnp.concatenate(halves, axis=0)).astype(BF16)


def row_blocks(rows, step, fn):
    def one(i, carry):
        fn(pl.ds(pl.multiple_of(i * step, step), step))
        return carry

    lax.fori_loop(0, rows // step, one, 0)


def rms_rows(h, gain):
    return h * lax.rsqrt(jnp.mean(h * h, axis=-1, keepdims=True) + norm_eps) * gain


def rms_back(h, gain, dn):
    inv = lax.rsqrt(jnp.mean(h * h, axis=-1, keepdims=True) + norm_eps)
    gd = gain * dn
    dh = gd * inv - h * (jnp.mean(gd * h, axis=-1, keepdims=True) * (inv * inv * inv))
    return dh, jnp.sum(dn * h * inv, axis=0, keepdims=True)


ROWS = 128
NB = 768


def col_blocks(width):
    return [slice(i, min(i + NB, width)) for i in range(0, width, NB)]


def self_forward(first, io, *refs):
    if first:
        lens, x_ref, gain_ref, w_ref, table_ref, spread_ref, a_ref, q_ref, k_ref, v_ref, o_ref, lse_ref, bias_ref = refs

        io.wait(x_ref, gain_ref)

        def norm(rows):
            a_ref[rows, :] = rms_rows(x_ref[rows, :].astype(F32), gain_ref[0:1, :]).astype(BF16)

        row_blocks(x_ref.shape[0], ROWS, norm)
        io.flush(a_ref)
    else:
        lens, a_ref, w_ref, table_ref, spread_ref, q_ref, k_ref, v_ref, o_ref, lse_ref, bias_ref = refs
    io.wait(table_ref, spread_ref)
    lines = lax.dot_general(
        table_ref[...], spread_ref[...], (((1,), (1,)), ((), ())), precision=highest,
        preferred_element_type=F32,
    )
    row = lax.broadcasted_iota(jnp.int32, (QB, LANE), 0)
    col = lax.broadcasted_iota(jnp.int32, (QB, LANE), 1)
    for h in range(bias_ref.shape[0]):
        line = jnp.broadcast_to(lines[h : h + 1, :], (QB, QB))
        tile = pltpu.roll(line, 0, 1, stride=1, stride_axis=0)[:, :LANE]
        bias_ref[h] = jnp.where(col - row + LANE < 0, masked_value, tile)
    io.flush(bias_ref)
    io.wait(lens, a_ref, w_ref)
    for i, ref in enumerate((q_ref, k_ref, v_ref)):
        ref[...] = nn(a_ref[...], w_ref[i]).astype(BF16)
        io.flush(ref)
    attend_pairs(q_ref, k_ref, v_ref, o_ref, lse_ref, bias_ref, lens[lax.axis_index("mp")])
    io.flush(o_ref, lse_ref)


def cross_forward(
    io, lens, x_ref, gain_ref, m_ref, oo, on, woo, won, wqo, wqn, wkvo, wkvn, wco, wcn,
    h1_ref, b_ref, qo, qn, ko, kn, vo, vn, oco, ocn, lse_ref, h2_ref, c_ref,
):
    io.wait(lens, m_ref)
    for k, v, w in ((ko, vo, wkvo), (kn, vn, wkvn)):
        io.wait(w)
        k[...] = nn(m_ref[...], w[0]).astype(BF16)
        v[...] = nn(m_ref[...], w[1]).astype(BF16)
        io.flush(k, v)
    io.wait(x_ref, gain_ref, oo, on, woo, won)
    for c in col_blocks(x_ref.shape[1]):
        h1_ref[:, c] = x_ref[:, c].astype(F32) + nn(oo[...], woo[:, c]) + nn(on[...], won[:, c])

    def first(rows):
        b_ref[rows, :] = rms_rows(h1_ref[rows, :], gain_ref[1:2, :]).astype(BF16)

    row_blocks(x_ref.shape[0], ROWS, first)
    io.flush(h1_ref, b_ref)
    io.wait(wqo, wqn)
    qo[...] = nn(b_ref[...], wqo[...]).astype(BF16)
    qn[...] = nn(b_ref[...], wqn[...]).astype(BF16)
    io.flush(qo, qn)
    heads = qo.shape[1] // HD
    length = lens[lax.axis_index("mp")]
    attend_pairs(qo, ko, vo, oco, lse_ref, None, length)
    attend_pairs(qn, kn, vn, ocn, lse_ref, None, length, heads)
    io.flush(oco, ocn, lse_ref)
    io.wait(wco, wcn)
    for c in col_blocks(x_ref.shape[1]):
        h2_ref[:, c] = h1_ref[:, c] + nn(oco[...], wco[:, c]) + nn(ocn[...], wcn[:, c])

    def last(rows):
        c_ref[rows, :] = rms_rows(h2_ref[rows, :], gain_ref[2:3, :]).astype(BF16)

    row_blocks(x_ref.shape[0], ROWS, last)
    io.flush(h2_ref, c_ref)


HB = 512


def hidden_block(c_ref, og_ref, wi, wd, out, at):
    root = np.float32(np.sqrt(2.0 / np.pi))
    width = out.shape[1] // 3
    gate = nn(c_ref[...], wi[0])
    up = nn(c_ref[...], wi[1])
    d_hid = nt(og_ref[...], wd[...])
    sq = gate * gate
    th = jnp.tanh(root * gate * (1.0 + 0.044715 * sq))
    half = 0.5 + 0.5 * th
    gelu = gate * half
    slope = half + 0.5 * gate * (1.0 - th * th) * (root * (1.0 + np.float32(3 * 0.044715) * sq))
    out[:, at : at + HB] = (d_hid * up * slope).astype(BF16)
    out[:, width + at : width + at + HB] = (d_hid * gelu).astype(BF16)
    out[:, 2 * width + at : 2 * width + at + HB] = (gelu * up).astype(BF16)


def ffn_other(io, c_ref, og_ref, *refs):
    weights, out = refs[:-1], refs[-1]
    io.wait(c_ref, og_ref)
    for i in range(0, len(weights), 2):
        io.wait(*weights[i : i + 2])
        hidden_block(c_ref, og_ref, weights[i], weights[i + 1], out, i // 2 * HB)
        for k in range(3):
            io.flush_columns(k * out.shape[1] // 3 + i // 2 * HB, HB, out)


def ffn_own(io, c_ref, og_ref, h2_ref, gain_ref, *refs):
    own, res_ref, g1_ref, w1_ref, dgain, acc = refs[-6:]
    weights, (nbr, win, wdn) = refs[:-9], refs[-9:-6]
    width = own.shape[1] // 3
    io.wait(c_ref, og_ref)
    for i in range(0, len(weights), 2):
        io.wait(*weights[i : i + 2])
        hidden_block(c_ref, og_ref, weights[i], weights[i + 1], own, i // 2 * HB)
    io.flush(own)
    first = True
    for i in range(0, len(weights), 2):
        wi, wd = weights[i], weights[i + 1]
        at = i // 2 * HB
        gate, up, hid = [own[:, k * width + at : k * width + at + HB] for k in range(3)]
        down, out = nt(gate, wi[0]) + nt(up, wi[1]), nn(hid, wd[...])
        g1_ref[...] = down if first else g1_ref[...] + down
        acc[...] = out if first else acc[...] + out
        first = False
    io.wait(nbr, win, wdn)
    g1_ref[...] += nt(nbr[:, 0:width], win[0]) + nt(nbr[:, width : 2 * width], win[1])
    acc[...] += nn(nbr[:, 2 * width :], wdn[...])
    io.wait(h2_ref, gain_ref)
    dgain[...] = jnp.zeros_like(dgain)

    def last(rows):
        h2 = h2_ref[rows, :]
        res_ref[rows, :] = (h2 + acc[rows, :]).astype(BF16)
        dh, dg = rms_back(h2, gain_ref[2:3, :], g1_ref[rows, :])
        g1 = og_ref[rows, :].astype(F32) + dh
        g1_ref[rows, :] = g1
        w1_ref[rows, :] = g1.astype(BF16)
        dgain[...] += dg

    row_blocks(h2_ref.shape[0], ROWS, last)
    io.flush(res_ref, g1_ref, w1_ref, dgain)


def cross_backward(
    io, lens, w1_ref, g1_ref, h1_ref, gain_ref, qo, qn, ko, kn, vo, vn, lse_ref, wco, wcn, wqo, wqn, wkvo, wkvn,
    do_own, dq_nbr, dkv_nbr, g0_ref, w0_ref, dm_ref, dgain, doo, don,
):
    half = qo.shape[1]
    heads = half // HD
    io.wait(lens, w1_ref, wco, wcn)
    doo[...] = nt(w1_ref[...], wco[...]).astype(BF16)
    don[...] = nt(w1_ref[...], wcn[...]).astype(BF16)
    length = lens[lax.axis_index("mp")]
    io.wait(qn, kn, vn, lse_ref)
    grads = ((dq_nbr, 0), (dkv_nbr, 0), (dkv_nbr, half))
    attend_back_pairs(qn, kn, vn, don, grads, lse_ref, None, length, heads)
    io.flush(dq_nbr, dkv_nbr)
    io.wait(qo, ko, vo)
    grads = ((do_own, 0), (do_own, half), (do_own, 2 * half))
    attend_back_pairs(qo, ko, vo, doo, grads, lse_ref, None, length)
    io.flush(do_own)
    io.wait(wqo, wqn, wkvo, wkvn)
    for c in col_blocks(w1_ref.shape[1]):
        g0_ref[:, c] = nt(do_own[:, 0:half], wqo[c, :]) + nt(dq_nbr[...], wqn[c, :])
        dm_ref[:, c] = (
            nt(do_own[:, half : 2 * half], wkvo[0, c, :])
            + nt(do_own[:, 2 * half :], wkvo[1, c, :])
            + nt(dkv_nbr[:, 0:half], wkvn[0, c, :])
            + nt(dkv_nbr[:, half:], wkvn[1, c, :])
        ).astype(BF16)
    io.flush(dm_ref)
    io.wait(g1_ref, h1_ref, gain_ref)
    dgain[...] = jnp.zeros_like(dgain)

    def last(rows):
        dh, dg = rms_back(h1_ref[rows, :], gain_ref[1:2, :], g0_ref[rows, :])
        g0 = g1_ref[rows, :] + dh
        g0_ref[rows, :] = g0
        w0_ref[rows, :] = g0.astype(BF16)
        dgain[...] += dg

    row_blocks(w1_ref.shape[0], ROWS, last)
    io.flush(g0_ref, w0_ref, dgain)


def self_backward(io, lens, w0_ref, *refs):
    parts, outs, do_ref = (refs[:6], refs[6:12]), refs[12:16], refs[16]
    io.wait(lens, w0_ref)
    for i, (wo, q_ref, k_ref, v_ref, lse_ref, bias_ref) in enumerate(parts):
        out_ref, diag_ref = outs[2 * i : 2 * i + 2]
        io.wait(wo)
        do_ref[...] = nt(w0_ref[...], wo[...]).astype(BF16)
        io.wait(q_ref, k_ref, v_ref, lse_ref, bias_ref)
        attend_back_pairs(
            q_ref, k_ref, v_ref, do_ref, [(out_ref, k * q_ref.shape[1]) for k in range(3)],
            lse_ref, bias_ref, lens[lax.axis_index("mp")], 0, diag_ref,
        )
        io.flush(out_ref, diag_ref)


def input_backward(io, *refs):
    pairs, (x_ref, gain_ref, g0_ref, out_ref, dgain, acc) = refs[:-6], refs[-6:]
    for i in range(0, len(pairs), 4):
        io.wait(*pairs[i : i + 4])
        term = nt(pairs[i][...], pairs[i + 1][0]) + nt(pairs[i + 2][...], pairs[i + 3][0])
        acc[...] = acc[...] + term if i else term
    io.wait(x_ref, gain_ref, g0_ref)
    dgain[...] = jnp.zeros_like(dgain)

    def some(rows):
        dh, dg = rms_back(x_ref[rows, :].astype(F32), gain_ref[0:1, :], acc[rows, :])
        out_ref[rows, :] = (g0_ref[rows, :] + dh).astype(BF16)
        dgain[...] += dg

    row_blocks(x_ref.shape[0], ROWS, some)
    io.flush(out_ref, dgain)


LINE = (0, 8, 4, 12)
ORDERS = ((1, 2), (2, 1))


def weight_grads(parts, layouts, io, *refs):
    outs, total = refs[-1 - sum(len(v) for v in layouts) : -1], refs[-1]
    rows = outs[0].shape[1]
    device = lax.axis_index("dp")
    first = 0
    for jobs, layout in zip(parts, layouts):
        mine = outs[first : first + len(layout)]
        first += len(layout)
        at = 0
        for lo, ln, ro, rn, width in jobs:
            done = 0
            while done < width:
                step = width if width <= 640 else min(512, width - done)
                src = slice(done, done + step)
                io.wait(refs[lo], refs[ro])
                total[:, 0:step] = tn(refs[lo][...], refs[ro][:, src])
                io.wait(refs[ln], refs[rn])
                total[:, 0:step] += tn(refs[ln][...], refs[rn][:, src])
                dst = slice(at + done, at + done + step)
                for out, nears in zip(mine, layout):
                    for j, mask in enumerate([near ^ far for near in nears for far in LINE]):
                        chunk = lax.bitwise_xor(device, jnp.int32(mask))
                        part = total[pl.ds(pl.multiple_of(chunk * rows, 16), rows), 0:step]
                        out[j, :, dst] = part.astype(out.dtype)
                io.flush_columns(at + done, step, *mine)
                done += step
            at += width


def add_terms(plan, io, *refs):
    at = 0
    outs = refs[-len(plan) :]
    for counts, out in zip(plan, outs):
        start = 0
        for count in counts:
            terms = refs[at : at + count]
            at += count
            io.wait(*terms)
            cols = slice(start, start + terms[0].shape[-1])
            start = cols.stop
            for j in range(out.shape[0]):
                total = terms[0][j]
                for t in terms[1:]:
                    total = total + t[j].astype(F32)
                out[j, :, cols] = total.astype(out.dtype)
        io.flush(out)


def swap_dp(v, mask):
    return lax.ppermute(v, "dp", [(i, i ^ mask) for i in range(16)])


def swap_mp(v):
    return lax.ppermute(v, "mp", [(0, 1), (1, 0)])


def make_grads(parts, depth, n_data, direct=False):
    if n_data != 16:

        def piece(a):
            if not isinstance(a, tuple):
                return a
            value = a[0]
            for axis, start, size in a[1]:
                start = start() if callable(start) else start
                value = lax.dynamic_slice_in_dim(value, start, size, axis)
            return value

        cols = []
        for job in [job for jobs in parts for job in jobs]:
            lo, ln, ro, rn = [piece(a) for a in job]
            cols.append(tn(lo, ro) + tn(ln, rn))
        return lax.psum_scatter(
            jnp.concatenate(cols, axis=1), "dp", scatter_dimension=0, tiled=True
        )
    arrays, keys, plan, shapes, layouts = [], [], [], [], []
    rows = depth // 16
    for jobs in parts:
        spots = []
        for job in jobs:
            place = []
            for a in job:
                key = (id(a[0]),) + a[1:] if isinstance(a, tuple) else id(a)
                if key not in keys:
                    arrays.append(a)
                    keys.append(key)
                place.append(keys.index(key))
            spots.append(tuple(place) + (job[2][1][-1][2],))
        plan.append(tuple(spots))
        width = sum(job[2][1][-1][2] for job in jobs)
        if direct:
            layouts.append(((0,), (1,), (2,), (3,)))
        else:
            one, two = ORDERS[len(layouts)]
            layouts.append(((0, two), (one, one ^ two)))
        for nears in layouts[-1]:
            shapes.append(sds((4 * len(nears), rows, width), F32 if 0 in nears else BF16))
    widest = max(job[4] if job[4] <= 640 else 512 for jobs in plan for job in jobs)
    return dma_call(
        functools.partial(weight_grads, tuple(plan), tuple(layouts)),
        shapes,
        arrays,
        0,
        [pltpu.VMEM((depth, widest), F32)],
        flops=4 * 512 * depth * 1024,
        n_writes=64,
    )


class Reduction:
    def __init__(self, made, n_data, direct=False):
        self.plain = n_data != 16
        self.made, self.direct = made, direct
        self.far = []
        if not self.plain:
            if direct:
                self.keeps, self.done = [made[0]], 2
                self.got = [[swap_dp(v, m) for v, m in zip(made[1:], (1, 2, 3))]]
            else:
                self.keeps, self.done = list(made[::2]), 1
                self.got = [[swap_dp(v, o[0])] for v, o in zip(made[1::2], ORDERS)]

    def near(self, start, size):
        return [[leading(t, start, size) for t in [k] + g] for k, g in zip(self.keeps, self.got)]

    def sends(self):
        rows, widths = self.keeps[0].shape[1], [k.shape[2] for k in self.keeps]
        if self.done == 1:
            parts = self.near(4, 4)
            shapes = [sds((4, rows, w), BF16) for w in widths]
            return [(len(p),) for p in parts], shapes, [t for p in parts for t in p]
        if self.direct:
            spots = ((1, 1), (2, 1), (3, 1))
        else:
            spots = ((2, 2),) if self.done == 2 else ((1, 1),)
        plan, shapes, terms = [], [], []
        for start, size in spots:
            parts, at = self.near(start, size), 0
            for part, w in zip(parts, widths):
                part += [leading(columns(t, at, w), start, size) for t in self.far]
                at += w
            plan.append(tuple(len(p) for p in parts))
            shapes.append(sds((size, rows, sum(widths)), BF16))
            terms += [t for part in parts for t in part]
        return plan, shapes, terms

    def sent(self, sends):
        if self.done == 1:
            for got, send, order in zip(self.got, sends, ORDERS):
                got.append(swap_dp(send, order[1]))
        elif self.direct:
            self.far = [swap_dp(v, m) for v, m in zip(sends, LINE[1:])]
        else:
            self.far.append(swap_dp(sends[0], 4 if self.done == 2 else 8))
        self.done += 1

    def terms(self):
        if self.plain:
            return [[self.made[None]]]
        parts, at = self.near(0, 1), 0
        for part, k in zip(parts, self.keeps):
            part += [leading(columns(t, at, k.shape[2]), 0, 1) for t in self.far]
            at += k.shape[2]
        return parts


def exchange(*steps, others=()):
    steps = [r for r in steps if not r.plain]
    if not steps:
        return []
    made = [r.sends() for r in steps]
    plan = [p for m in made for p in m[0]]
    shapes = [p for m in made for p in m[1]]
    terms = [p for m in made for p in m[2]]
    if others:
        terms[0] = (after(terms[0][0], *others), terms[0][1])
    sends = dma_call(functools.partial(add_terms, tuple(plan)), shapes, terms)
    at = 0
    for r, m in zip(steps, made):
        r.sent(sends[at : at + len(m[0])])
        at += len(m[0])
    return list(sends)


def squares_of(mats, first, all_ref, cols_ref, row_sums):
    rows = all_ref.shape[0]
    lane = lax.broadcasted_iota(jnp.int32, (rows, LANE), 1)
    for i, (start, width) in enumerate(mats):
        part = all_ref[:, start : start + width]
        sq = part * part
        cols_ref[:, start : start + width] = jnp.sum(sq, axis=0, keepdims=True)
        row_sums = row_sums + jnp.where(lane == first + i, jnp.sum(sq, axis=1, keepdims=True), 0.0)
    return row_sums


def end_sums(counts, io, refs, all_ref):
    start = at = 0
    for count in counts:
        terms = refs[at : at + count]
        io.wait(*terms)
        total = terms[0][0]
        for t in terms[1:]:
            total = total + t[0].astype(F32)
        all_ref[:, start : start + total.shape[1]] = total
        at += count
        start += total.shape[1]


def early_statistics(counts, mats, io, *refs):
    all_ref, cols_ref, rows_ref = refs[-3:]
    end_sums(counts, io, refs, all_ref)
    rows_ref[...] = squares_of(mats, 0, all_ref, cols_ref, jnp.zeros_like(rows_ref))
    io.flush(all_ref, cols_ref, rows_ref)


def statistics(counts, mats, first, io, *refs):
    all_ref, pack_ref, cols_ref = refs[-3:]
    rows_ref, spread = refs[-10], refs[-4]
    gains, diags = refs[-9:-6], refs[-6:-4]
    io.wait(rows_ref, *gains, *diags, spread)
    pack_ref[...] = jnp.zeros_like(pack_ref)
    for i, gain in enumerate(gains):
        pack_ref[i : i + 1, :] = gain[...]
    for i, diag in enumerate(diags):
        heads = diag.shape[0]
        lines = jnp.concatenate([diag[h] for h in range(heads)], axis=0)
        pack_ref[8 : 8 + heads, i * LANE : i * LANE + BUCKETS] = lax.dot_general(
            lines, spread[...], (((1,), (0,)), ((), ())), precision=highest,
            preferred_element_type=F32,
        )
    end_sums(counts, io, refs, all_ref)
    rows = all_ref.shape[0]
    pack_ref[16 : 16 + rows, 0:LANE] = squares_of(mats, first, all_ref, cols_ref, rows_ref[...])
    io.flush(all_ref, pack_ref, cols_ref)


def merge_kernel(io, own_ref, got_ref, early_ref, late_ref, out_ref, rows_ref):
    io.wait(own_ref, got_ref, early_ref, late_ref)
    rows = rows_ref.shape[0]
    n_early, depth = early_ref.shape[1], own_ref.shape[1]
    n_all = n_early + late_ref.shape[1]
    full = own_ref[16 : 16 + rows, 0:LANE] + got_ref[16 : 16 + rows, 0:LANE]
    rows_ref[...] = full
    out_ref[:, 0:n_early] = early_ref[...]
    out_ref[:, n_early:n_all] = late_ref[...]
    at = n_all
    for i in range(3):
        out_ref[:, at : at + depth] = own_ref[i : i + 1, :] + got_ref[i : i + 1, :]
        at += depth
    out_ref[:, at : at + LANE] = jnp.sum(full, axis=0, keepdims=True)
    for side in range(2):
        mine = own_ref[8:16, side * LANE : (side + 1) * LANE]
        theirs = got_ref[8:16, (1 - side) * LANE : (2 - side) * LANE]
        both = mine + theirs
        for h in range(8):
            at += LANE
            out_ref[:, at : at + LANE] = both[h : h + 1]
    io.flush(out_ref, rows_ref)


def turn(v):
    rows = v.shape[0]
    if rows < LANE:
        v = jnp.concatenate([v, jnp.zeros((LANE - rows, v.shape[1]), v.dtype)], axis=0)
    return jnp.transpose(v)[:, :rows]


def update_kernel(plan, n_terms, io, *refs):
    terms = refs[:n_terms]
    rows_ref, early_ref, late_ref = refs[n_terms : n_terms + 3]
    weights = refs[n_terms + 3 : n_terms + 3 + len(plan)]
    outs = refs[n_terms + 3 + len(plan) :]
    io.wait(*terms)
    line = functools.reduce(jnp.add, [p[...] for p in terms])
    n_early = early_ref.shape[1]
    n_all = n_early + late_ref.shape[1]
    gain_ref, table_ref, norm_ref = outs[0], outs[1], outs[-1]
    depth = gain_ref.shape[1]
    gains_at, totals_at = n_all, n_all + 3 * depth
    tables_at = totals_at + LANE
    for i in range(3):
        gain_ref[i : i + 1, :] = line[:, gains_at + i * depth : gains_at + (i + 1) * depth]
    for h in range(table_ref.shape[0]):
        at = tables_at + h * LANE
        table_ref[h : h + 1, :] = line[:, at : at + BUCKETS]
    totals = line[:, totals_at:tables_at]
    gains, tables = line[:, gains_at:totals_at], line[:, tables_at:]
    squares = (
        jnp.sum(gains * gains, axis=1, keepdims=True)
        + jnp.sum(tables * tables, axis=1, keepdims=True)
        + jnp.sum(totals, axis=1, keepdims=True)
    )
    norm_ref[...] = jnp.sqrt(squares)
    io.flush(gain_ref, table_ref, norm_ref)
    io.wait(rows_ref, early_ref, late_ref)
    row_sums = rows_ref[...]
    row_lines = turn(row_sums)
    at = 2
    for (natural, members), weight in zip(plan, weights):
        new_ref, row_out, col_out = outs[at : at + 3]
        at += 3
        io.wait(weight)
        for k, (i, start, width) in enumerate(members):
            size = 2 * width
            by_row = row_sums[:, i : i + 1] / size + stat_eps
            by_col = line[:, start : start + width] / depth + stat_eps
            mean = totals[:, i : i + 1] / (size * depth) + stat_eps
            if start < n_early:
                grad = early_ref[:, start : start + width]
            else:
                grad = late_ref[:, start - n_early : start - n_early + width]
            change = (
                learn_rate
                * grad
                * lax.rsqrt(by_row * by_col / mean)
            )
            row_line = row_lines[i : i + 1, :] / size + stat_eps
            new_ref[k] = weight[k].astype(F32) - change
            lines = (row_line, by_col) if natural else (by_col, row_line)
            for out, value in zip((row_out, col_out), lines):
                if len(out.shape) == 1:
                    out[...] = value.reshape(out.shape)
                else:
                    out[k : k + 1, :] = value
        io.flush(new_ref, row_out, col_out)


def after(value, *others):
    return lax.optimization_barrier((value,) + others)[0]


def body(
    tokens,
    memory,
    out_grad,
    tgt_lens,
    mem_lens,
    norm_gains,
    rel_table,
    self_qkv,
    self_out,
    cross_q,
    cross_kv,
    cross_out,
    ffn_in,
    ffn_out,
):
    n_data = lax.axis_size("dp")
    mp = lax.axis_index("mp")
    dp = lax.axis_index("dp")
    rows = tokens.shape[0]
    depth = tokens.shape[1]
    heads = rel_table.shape[1]
    half = heads * HD
    width = ffn_out.shape[0]
    chunk = depth // n_data
    qkv_n = swap_mp(self_qkv)
    table = rel_table.T
    table_n = swap_mp(table)
    so_n = swap_mp(self_out)
    ckv_n = swap_mp(cross_kv)
    cq_n = swap_mp(cross_q)
    co_n = swap_mp(cross_out)

    dist = np.arange(QB)
    line_dist = np.where(dist < LANE, dist + LANE, dist - LANE)
    spread = jnp.asarray((bucket_of(line_dist)[:, None] == np.arange(BUCKETS)).astype(np.float32))
    gather = jnp.asarray((bucket_of(dist)[:, None] == np.arange(BUCKETS)).astype(np.float32))

    attn_flops = 4 * rows * rows * HD * heads
    bias_shape = sds((heads, QB, LANE), F32)
    act = sds((rows, half), BF16)
    wide = sds((rows, depth), BF16)
    full = sds((rows, depth), F32)
    gain_row = sds((1, depth), F32)
    lse = sds((heads, 1, rows), F32)
    lse2 = sds((2 * heads, 1, rows), F32)
    a, qs_o, ks_o, vs_o, os_o, lses_o, bias_o = dma_call(
        functools.partial(self_forward, True),
        [wide, act, act, act, act, lse, bias_shape],
        [tgt_lens, tokens, norm_gains, self_qkv, table, spread],
        1,
        flops=6 * rows * depth * half + attn_flops,
    )
    a, qkv_n, table_n, so_n, cq_n, ckv_n, co_n, ffn_in_b, ffn_out_b, out_grad_b = lax.optimization_barrier(
        (a, qkv_n, table_n, so_n, cq_n, ckv_n, co_n, ffn_in, ffn_out, out_grad)
    )
    fi_n = swap_mp(ffn_in_b)
    fo_n = swap_mp(ffn_out_b)
    og_n = swap_mp(out_grad_b)
    a_n = swap_mp(a)
    qs_n, ks_n, vs_n, os_n, lses_n, bias_n = dma_call(
        functools.partial(self_forward, False),
        [act, act, act, act, lse, bias_shape],
        [tgt_lens, a, qkv_n, table_n, spread],
        1,
        flops=6 * rows * depth * half + attn_flops,
    )
    mem_own = leading(memory, lambda: pl.multiple_of(lax.axis_index("mp") * rows, rows), rows)
    mem_nbr = leading(memory, lambda: pl.multiple_of((1 - lax.axis_index("mp")) * rows, rows), rows)
    os_n, a_n = lax.optimization_barrier((os_n, a_n))
    os_x = swap_mp(os_n)
    h1, b, qc_o, qc_n, kc_o, kc_n, vc_o, vc_n, oc_o, oc_n, lsec, h2, c = dma_call(
        cross_forward,
        [full, wide, act, act, act, act, act, act, act, act, lse2, full, wide],
        [mem_lens, tokens, norm_gains, mem_own, os_o, os_n, self_out, so_n, cross_q, cq_n, cross_kv, ckv_n, cross_out, co_n],
        1,
        flops=20 * rows * depth * half + 2 * attn_flops,
    )
    c, os_x = lax.optimization_barrier((c, os_x))
    b_n = swap_mp(b)
    oc_x = swap_mp(oc_n)
    c_n = swap_mp(c)
    hid = sds((rows, 3 * width), BF16)
    def hidden_weights(wi, wd):
        return [v for i in range(0, width, HB) for v in (columns(wi, i, HB), leading(wd, i, HB))]

    f_nbr = dma_call(
        ffn_other,
        [hid],
        [c, out_grad] + hidden_weights(fi_n, fo_n),
        flops=6 * rows * depth * width,
        n_writes=3 * width // HB,
    )[0]
    f_x = swap_mp(f_nbr)
    f_own, result, g1, w1, gain_c = dma_call(
        ffn_own,
        [hid, wide, full, wide, gain_row],
        [c, out_grad, h2, norm_gains] + hidden_weights(ffn_in, ffn_out) + [f_nbr, fi_n, fo_n],
        0,
        [pltpu.VMEM((rows, depth), F32)],
        flops=18 * rows * depth * width,
    )
    w1_n = swap_mp(w1)
    def pair(own, nbr, start, size):
        return columns(own, start, size), columns(nbr, start, size)

    w1, f_own = lax.optimization_barrier((w1, f_own))
    early_down = width // 2
    left = (2 * width + early_down) // 2
    ffn_made = make_grads(
        (
            ((c, c_n) + pair(f_own, f_x, 0, left),),
            (
                (c, c_n) + pair(f_own, f_x, left, 2 * width - left),
                (out_grad, og_n) + pair(f_own, f_x, 2 * width, early_down),
            ),
        ),
        depth,
        n_data,
    )
    w1_b = after(w1, w1_n, b_n, oc_x, *jax.tree.leaves(ffn_made))
    ffn_sum = Reduction(ffn_made, n_data)
    c_own, cq_nbr, ckv_nbr, g0, w0, d_mem, gain_b = dma_call(
        cross_backward,
        [sds((rows, 3 * half), BF16), act, sds((rows, 2 * half), BF16), full, wide, wide, gain_row],
        [mem_lens, w1_b, g1, h1, norm_gains, qc_o, qc_n, kc_o, kc_n, vc_o, vc_n, lsec, cross_out, co_n, cross_q, cq_n, cross_kv, ckv_n],
        1,
        [pltpu.VMEM((rows, half), BF16), pltpu.VMEM((rows, half), BF16)],
        flops=16 * rows * depth * half + 5 * attn_flops,
    )
    cq_x, ckv_x = swap_mp(cq_nbr), swap_mp(ckv_nbr)
    w0_n = swap_mp(w0)
    diag = sds((heads, 1, QB), F32)

    sent = exchange(ffn_sum, others=(c_own,))
    if sent:
        w0, w0_n, cq_x, ckv_x = lax.optimization_barrier((w0, w0_n, cq_x, ckv_x, *sent))[:4]
    split = 2 * LANE
    cross_made = make_grads(
        (
            (
                (out_grad, og_n) + pair(f_own, f_x, 2 * width + early_down, width - early_down),
                (w1, w1_n) + pair(oc_o, oc_x, 0, half),
                (w0, w0_n) + pair(os_o, os_x, 0, split),
            ),
            (
                (w0, w0_n) + pair(os_o, os_x, split, half - split),
                (b, b_n, columns(c_own, 0, half), columns(cq_x, 0, half)),
                (mem_own, mem_nbr, columns(c_own, half, 2 * half), columns(ckv_x, 0, 2 * half)),
            ),
        ),
        depth,
        n_data,
    )
    cross_sum = Reduction(cross_made, n_data)
    sent = exchange(ffn_sum, others=jax.tree.leaves(cross_made))
    w0_b = after(w0, *sent, *jax.tree.leaves(cross_made))
    s_nbr, diag_n, s_own, diag_o = dma_call(
        self_backward,
        [sds((rows, 3 * half), BF16), diag] * 2,
        [tgt_lens, w0_b, so_n, qs_n, ks_n, vs_n, lses_n, bias_n]
        + [self_out, qs_o, ks_o, vs_o, lses_o, bias_o],
        1,
        [pltpu.VMEM((rows, half), BF16)],
        flops=4 * rows * depth * half + 6 * attn_flops,
    )
    sent = exchange(ffn_sum, cross_sum, others=(s_own,))
    s_nbr, s_own = lax.optimization_barrier((s_nbr, s_own, *sent))[:2]
    s_x = swap_mp(s_nbr)
    self_made = make_grads(
        (((a, a_n) + pair(s_own, s_x, 0, 3 * half),),), depth, n_data, direct=True
    )
    self_sum = Reduction(self_made, n_data, direct=True)
    sent = exchange(cross_sum, others=jax.tree.leaves(self_made))
    s_own_b = after(s_own, *sent, *jax.tree.leaves(self_made))
    grad_in, gain_a = dma_call(
        input_backward,
        [wide, gain_row],
        [
            v
            for i in range(3)
            for d, w in ((s_own_b, self_qkv), (s_nbr, qkv_n))
            for v in (columns(d, i * half, half), leading(w, i, 1))
        ]
        + [tokens, norm_gains, g0],
        0,
        [pltpu.VMEM((rows, depth), F32)],
        flops=12 * rows * depth * half,
    )
    exchange(cross_sum, others=(grad_in,))

    sizes = [width, width, width] + [half] * 8
    starts = [int(v) for v in np.cumsum([0] + sizes[:-1])]
    mats = tuple(zip(starts, sizes))
    n_all = sum(sizes)
    plan = (
        (True, (8, 9, 10)),
        (False, (4,)),
        (True, (5,)),
        (True, (6, 7)),
        (False, (3,)),
        (True, (0, 1)),
        (False, (2,)),
    )
    plan = tuple((n, tuple((i, starts[i], sizes[i]) for i in m)) for n, m in plan)
    weights = (self_qkv, self_out, cross_q, cross_kv, cross_out, ffn_in, ffn_out)
    slices, shapes = [], [sds((3, depth), F32), sds((heads, BUCKETS), F32)]
    for (natural, members), weight in zip(plan, weights):
        count, size = len(members), members[0][2]
        if natural:
            stacked = weight.reshape((count,) + weight.shape[-2:])
            part = cut(stacked, 1, lambda: pl.multiple_of(lax.axis_index("dp") * chunk, chunk), chunk)
            if n_data != 16:
                part = lax.dynamic_slice_in_dim(stacked, dp * chunk, chunk, 1)
        else:
            part = lax.dynamic_slice_in_dim(weight, dp * chunk, chunk, 1).T[None]
        slices.append(part)
        line_sizes = (chunk, size) if natural else (size, chunk)
        shapes += [sds((count, chunk, size), F32)]
        shapes += [sds((n,) if weight.ndim == 2 else (count, n), F32) for n in line_sizes]
    shapes.append(sds((1, 1), F32))
    n_early = starts[8]
    early = ffn_sum.terms() + cross_sum.terms()
    grads, cols, row_parts = dma_call(
        functools.partial(early_statistics, tuple(len(t) for t in early), mats[:8]),
        [sds((chunk, n_early), F32), sds((1, n_early), F32), sds((chunk, LANE), F32)],
        [t for part in early for t in part],
    )
    exchange(self_sum, others=[row_parts] + [v for v in slices if not isinstance(v, tuple)])
    late = self_sum.terms()
    pack_rows = -(-(16 + chunk) // 8) * 8
    late_grads, pack, late_cols = dma_call(
        functools.partial(statistics, tuple(len(t) for t in late), tuple((a - n_early, b) for a, b in mats[8:]), 8),
        [sds((chunk, n_all - n_early), F32), sds((pack_rows, depth), F32), sds((1, n_all - n_early), F32)],
        [t for part in late for t in part] + [row_parts, gain_a, gain_b, gain_c, diag_o, diag_n, gather],
    )
    line, row_sums = dma_call(
        merge_kernel,
        [sds((1, n_all + 3 * depth + 17 * LANE), F32), sds((chunk, LANE), F32)],
        [pack, swap_mp(pack), cols, late_cols],
    )
    if n_data == 16:
        terms = [line]
        for group in ((1, 2, 3), (4, 8, 12)):
            if len(terms) > 1:
                terms = [functools.reduce(jnp.add, terms)]
            terms = terms + [swap_dp(terms[0], m) for m in group]
    else:
        terms = [lax.psum(line, "dp")]

    done = dma_call(
        functools.partial(update_kernel, plan, len(terms)),
        shapes,
        terms + [row_sums, grads, late_grads] + slices,
    )
    finals = [result, grad_in, d_mem, done[0], done[1].T]
    for i, ((natural, _), weight) in enumerate(zip(plan, weights)):
        new, row, col = done[2 + 3 * i : 5 + 3 * i]
        if weight.ndim == 2:
            new = new[0] if natural else new[0].T
        finals += [new, row, col]
    return tuple(finals + [done[-1][0, 0]])


def solution(mesh):
    placed = (
        P(("dp", "mp"), None),
        P("dp", None),
        P(("dp", "mp"), None),
        P("dp"),
        P("dp"),
        P(),
        P(None, "mp"),
        P(None, None, "mp"),
        P("mp", None),
        P(None, "mp"),
        P(None, None, "mp"),
        P("mp", None),
        P(None, None, "mp"),
        P("mp", None),
    )
    return jax.shard_map(
        body,
        mesh=mesh,
        in_specs=placed,
        out_specs=(
            P(("dp", "mp"), None),
            P(("dp", "mp"), None),
            P(("dp", "mp"), None),
            P(),
            P(None, "mp"),
            P(None, "dp", "mp"),
            P(None, "dp"),
            P(None, "mp"),
            P("mp", "dp"),
            P("mp"),
            P("dp"),
            P("dp", "mp"),
            P("dp"),
            P("mp"),
            P(None, "dp", "mp"),
            P(None, "dp"),
            P(None, "mp"),
            P("mp", "dp"),
            P("mp"),
            P("dp"),
            P(None, "dp", "mp"),
            P(None, "dp"),
            P(None, "mp"),
            P("mp", "dp"),
            P("mp"),
            P("dp"),
            P(),
        ),
        check_vma=False,
    )
```

```python
import functools

import jax
import jax.numpy as jnp
import numpy as np
from jax import lax
from jax.experimental import pallas as pl
from jax.experimental.pallas import tpu as pltpu
from jax.sharding import PartitionSpec as P

BUCKETS = 32
MAX_DIST = 128
HD = 64
LANE = 128
VMEM_BYTES = 64 * 1024 * 1024 - 512 * 1024
QB = 256
AHEAD = 3
norm_eps = 1e-06
stat_eps = 1e-30
masked_value = -1e30
learn_rate = 0.04
highest = lax.Precision.HIGHEST
F32 = jnp.float32
BF16 = jnp.bfloat16
VMEM = pl.BlockSpec(memory_space=pltpu.VMEM)
SMEM = pl.BlockSpec(memory_space=pltpu.SMEM)


def bucket_of(dist):
    exact_span = BUCKETS // 2
    dist = np.maximum(dist, 0)
    log_ratio = np.log(np.maximum(dist, 1) / exact_span) / np.log(MAX_DIST / exact_span)
    far = np.minimum(
        exact_span + np.floor(log_ratio * (BUCKETS - exact_span)).astype(np.int64), BUCKETS - 1
    )
    return np.where(dist < exact_span, dist, far).astype(np.int32)


def nn(a, b):
    return lax.dot_general(a, b, (((1,), (0,)), ((), ())), preferred_element_type=F32)


def nt(a, b):
    return lax.dot_general(a, b, (((1,), (1,)), ((), ())), preferred_element_type=F32)


def tn(a, b):
    return lax.dot_general(a, b, (((0,), (0,)), ((), ())), preferred_element_type=F32)


class Copies:
    def __init__(self, pairs_in, pairs_out, sem_in, sem_out):
        self.reads = [
            (dst, pltpu.make_async_copy(src, dst, sem_in.at[i]))
            for i, (src, dst) in enumerate(pairs_in)
        ]
        self.writes = [
            (src, pltpu.make_async_copy(src, dst, sem_out.at[i]))
            for i, (src, dst) in enumerate(pairs_out)
        ]
        self.pairs_out, self.sem_out = pairs_out, sem_out
        self.pending, self.begun = list(self.reads), []
        for _, copy in self.reads:
            copy.start()

    def wait(self, *refs):
        for ref in refs:
            for entry in self.pending:
                if entry[0] is ref:
                    entry[1].wait()
                    self.pending = [e for e in self.pending if e is not entry]
                    break

    def flush(self, *refs):
        for ref in refs:
            for src, copy in self.writes:
                if src is ref:
                    copy.start()
                    self.begun.append(copy)

    def flush_columns(self, start, size, *refs):
        cols = pl.ds(start, size)
        for src, dst in self.pairs_out:
            if not any(src is r for r in refs):
                continue
            copy = pltpu.make_async_copy(
                src.at[..., cols], dst.at[..., cols], self.sem_out.at[len(self.begun)]
            )
            copy.start()
            self.begun.append(copy)

    def close(self):
        assert not self.pending and len(self.begun) >= len(self.writes)
        for copy in self.begun:
            copy.wait()


def columns(array, start, size):
    return cut(array, -1, start, size)


def leading(array, start, size):
    return cut(array, 0, start, size)


def cut(array, axis, start, size):
    array, cuts = array if isinstance(array, tuple) else (array, ())
    return (array, cuts + ((axis % array.ndim, start, size),))


def dma_call(kernel, outs, args, n_smem=0, scratch=(), flops=0, n_writes=0):
    args = [a if isinstance(a, tuple) else (a, ()) for a in args]
    arrays = [a[0] for a in args]
    n_in, n_out = len(arrays), len(outs)
    held = []
    for i, (a, cuts) in enumerate(args):
        shape = list(a.shape)
        for axis, _, size in cuts:
            shape[axis] = size
        shape = tuple(shape)
        held.append((pltpu.SMEM if i < n_smem else pltpu.VMEM)(shape, a.dtype))
    held += [pltpu.VMEM(o.shape, o.dtype) for o in outs]

    def part(ref, arg):
        index = [slice(None)] * arg[0].ndim
        for axis, start, size in arg[1]:
            index[axis] = pl.ds(start() if callable(start) else start, size)
        return ref.at[tuple(index)] if arg[1] else ref

    def run(*refs):
        given, made = refs[:n_in], refs[n_in : n_in + n_out]
        local = refs[n_in + n_out : 2 * (n_in + n_out)]
        rest, (sem_in, sem_out) = refs[2 * (n_in + n_out) : -2], refs[-2:]
        sources = [part(r, a) for r, a in zip(given, args)]
        io = Copies(
            list(zip(sources, local[:n_in])), list(zip(local[n_in:], made)), sem_in, sem_out
        )
        kernel(io, *local, *rest)
        io.close()

    moved = sum(h.shape[0] * int(np.prod(h.shape[1:])) * np.dtype(h.dtype).itemsize for h in held)
    return pl.pallas_call(
        run,
        out_shape=list(outs),
        in_specs=[pl.BlockSpec(memory_space=pltpu.HBM)] * n_in,
        out_specs=[pl.BlockSpec(memory_space=pltpu.HBM)] * n_out,
        scratch_shapes=held
        + list(scratch)
        + [pltpu.SemaphoreType.DMA((n_in,)), pltpu.SemaphoreType.DMA((max(n_out, n_writes),))],
        compiler_params=pltpu.CompilerParams(vmem_limit_bytes=VMEM_BYTES),
        cost_estimate=pl.CostEstimate(flops=flops, bytes_accessed=moved, transcendentals=0),
    )(*arrays)


def sds(shape, dtype):
    return jax.ShapeDtypeStruct(shape, dtype)


def head_masks(dtype):
    lane = lax.broadcasted_iota(jnp.int32, (1, LANE), 1)
    return [(lane < HD).astype(dtype), (lane >= HD).astype(dtype)]


def bias_chunks(bias_ref, head, first, count, blocks):
    near = bias_ref[head, 0:LANE, :]
    diag = bias_ref[head, LANE : 2 * LANE, :]
    const = jnp.broadcast_to(bias_ref[head, 0:1, :], (LANE, LANE))
    none = jnp.full((LANE, LANE), masked_value, F32)

    def tile(offset):
        return none if offset < 0 else diag if offset == 0 else near if offset == 1 else const

    return [
        jnp.concatenate([tile(first + i - j) for i in range(blocks)], axis=1)
        for j in range(count)
    ]


def score_chunks(keys_masked, queries, bias_ref, head, first, count, length):
    width = queries.shape[0]
    scores = nt(keys_masked[: count * LANE], queries)
    row = lax.broadcasted_iota(jnp.int32, (LANE, width), 0)
    chunks = []
    if bias_ref is not None:
        bias = bias_chunks(bias_ref, head, first, count, width // LANE)
    for j in range(count):
        part = scores[j * LANE : (j + 1) * LANE]
        if bias_ref is not None:
            part = part + bias[j]
        chunks.append(jnp.where(row < length - j * LANE, part, masked_value))
    return chunks


def attend_back_pairs(
    q_ref, k_ref, v_ref, do_ref, grads, lse_ref, bias_ref, length, lse_base=0, diag_ref=None
):
    rows, width = q_ref.shape
    keys = k_ref.shape[0]
    masks = head_masks(BF16)
    lane_id = lax.broadcasted_iota(jnp.int32, (1, QB), 1)
    step = QB
    n_blocks = rows // step
    units = [(h, b) for h in range(width // HD) for b in range(n_blocks)]
    kept = {}

    def pair_values(p):
        if p not in kept:
            lanes = slice(p * LANE, (p + 1) * LANE)
            k_pair, v_pair = k_ref[:, lanes], v_ref[:, lanes]
            kept[p] = (
                [k_pair * m for m in masks],
                [v_pair * m for m in masks],
                jnp.transpose(k_pair.astype(F32)).astype(BF16),
            )
        return kept[p]

    def start(h, block):
        p, t = divmod(h, 2)
        lanes = slice(p * LANE, (p + 1) * LANE)
        count = (block + 1) * step // LANE if bias_ref is not None else keys // LANE
        k_m, v_m, _ = pair_values(p)
        at = slice(block * step, (block + 1) * step)
        q_blk, do_blk = q_ref[at, lanes], do_ref[at, lanes]
        chunks = score_chunks(k_m[t], q_blk, bias_ref, h, block * step // LANE, count, length)
        d_probs = nt(v_m[t][: count * LANE], do_blk)
        return chunks, [d_probs[j * LANE : (j + 1) * LANE] for j in range(count)]

    ahead = start(*units[0])
    sums = {}
    for i, (h, block) in enumerate(units):
        p, t = divmod(h, 2)
        lanes = slice(p * LANE, (p + 1) * LANE)
        at = slice(block * step, (block + 1) * step)
        chunks, d_probs = ahead
        if i + 1 < len(units):
            ahead = start(*units[i + 1])
        count = len(chunks)
        lse = lse_ref[lse_base + h, :, at]
        probs = [jnp.exp(c - lse) for c in chunks]
        dot = functools.reduce(
            jnp.add, [jnp.sum(a * b, axis=0, keepdims=True) for a, b in zip(probs, d_probs)]
        )
        d_scores = [(a * (b - dot)).astype(BF16) for a, b in zip(probs, d_probs)]
        if t == 0 and block == 0:
            sums = dict(
                dv=[None] * (keys // LANE), dk=[None] * (keys // LANE), dq=[[], []]
            )
        if block == 0:
            near_sum = jnp.zeros((LANE, LANE), F32)
            diag_sum = jnp.zeros((LANE, LANE), F32)
            far_sum = jnp.zeros((1, LANE), F32)
        if diag_ref is not None:
            for j in range(count):
                wide = d_scores[j].astype(F32)
                for c in range(step // LANE):
                    tile = wide[:, c * LANE : (c + 1) * LANE]
                    offset = block * step // LANE + c - j
                    if offset == 0:
                        diag_sum = diag_sum + tile
                    elif offset == 1:
                        near_sum = near_sum + tile
                    elif offset > 1:
                        far_sum = far_sum + jnp.sum(tile, axis=0, keepdims=True)
        d_all = jnp.concatenate(d_scores, axis=0)
        p_all = jnp.concatenate([a.astype(BF16) for a in probs], axis=0)
        dv_new = nn(p_all, do_ref[at, lanes] * masks[t])
        dk_new = nn(d_all, q_ref[at, lanes] * masks[t])
        for name, new in (("dv", dv_new), ("dk", dk_new)):
            for j in range(count):
                part = new[j * LANE : (j + 1) * LANE]
                old = sums[name][j]
                sums[name][j] = part if old is None else old + part
        k_t = pair_values(p)[2]
        sums["dq"][t].append(nn(k_t[t * HD : (t + 1) * HD, : count * LANE], d_all))
        if diag_ref is not None and block == n_blocks - 1:
            both = jnp.concatenate([near_sum, diag_sum], axis=0)
            both = jnp.concatenate([both, jnp.zeros_like(both)], axis=1)
            acc = jnp.zeros((8, QB), F32)
            for g in range(QB // 8):
                piece = both[8 * g : 8 * g + 8]
                turned = (LANE - 8 * g) % QB
                acc = acc + (pltpu.roll(piece, turned, 1) if turned else piece)
            line = acc[0:1]
            for g in range(1, 8):
                line = line + pltpu.roll(acc, QB - g, 1)[g : g + 1]
            far_total = jnp.sum(far_sum, axis=1, keepdims=True)
            diag_ref[h] = line + jnp.where(lane_id == QB - 1, far_total, 0.0)
        if t == 1 and block == n_blocks - 1:
            dq_t = jnp.concatenate([jnp.concatenate(v, axis=1) for v in sums["dq"]], axis=0)
            done = (
                jnp.transpose(dq_t),
                jnp.concatenate(sums["dk"], axis=0),
                jnp.concatenate(sums["dv"], axis=0),
            )
            for (ref, first), value in zip(grads, done):
                ref[:, first + p * LANE : first + (p + 1) * LANE] = value.astype(BF16)


def attend_pairs(q_ref, k_ref, v_ref, o_ref, lse_ref, bias_ref, length, lse_base=0):
    rows, width = q_ref.shape
    keys = k_ref.shape[0]
    masks = head_masks(BF16)
    step = QB
    n_blocks = rows // step
    units = [(h, b) for h in range(width // HD) for b in range(n_blocks)]

    def start(h, block):
        p, t = divmod(h, 2)
        lanes = slice(p * LANE, (p + 1) * LANE)
        k_m = k_ref[:, lanes] * masks[t]
        count = (block + 1) * step // LANE if bias_ref is not None else keys // LANE
        q_blk = q_ref[block * step : (block + 1) * step, lanes]
        return score_chunks(k_m, q_blk, bias_ref, h, block * step // LANE, count, length)

    queue = [start(*u) for u in units[:AHEAD]]
    for i, (h, block) in enumerate(units):
        p, t = divmod(h, 2)
        lanes = slice(p * LANE, (p + 1) * LANE)
        chunks = queue.pop(0)
        if i + AHEAD < len(units):
            queue.append(start(*units[i + AHEAD]))
        if t == 0 and block == 0:
            v_t = jnp.transpose(v_ref[:, lanes].astype(F32)).astype(BF16)
            halves = []
        if block == 0:
            outs = []
        top = functools.reduce(jnp.maximum, [jnp.max(c, axis=0, keepdims=True) for c in chunks])
        exps = [jnp.exp(c - top) for c in chunks]
        total = functools.reduce(jnp.add, [jnp.sum(c, axis=0, keepdims=True) for c in exps])
        scale = 1.0 / total
        probs = jnp.concatenate([(c * scale).astype(BF16) for c in exps], axis=0)
        outs.append(nn(v_t[t * HD : (t + 1) * HD, : probs.shape[0]], probs))
        lse_ref[lse_base + h, :, block * step : (block + 1) * step] = top + jnp.log(total)
        if block == n_blocks - 1:
            halves.append(jnp.concatenate(outs, axis=1))
            if t == 1:
                o_ref[:, lanes] = jnp.transpose(jnp.concatenate(halves, axis=0)).astype(BF16)


def row_blocks(rows, step, fn):
    def one(i, carry):
        fn(pl.ds(pl.multiple_of(i * step, step), step))
        return carry

    lax.fori_loop(0, rows // step, one, 0)


def rms_rows(h, gain):
    return h * lax.rsqrt(jnp.mean(h * h, axis=-1, keepdims=True) + norm_eps) * gain


def rms_back(h, gain, dn):
    inv = lax.rsqrt(jnp.mean(h * h, axis=-1, keepdims=True) + norm_eps)
    gd = gain * dn
    dh = gd * inv - h * (jnp.mean(gd * h, axis=-1, keepdims=True) * (inv * inv * inv))
    return dh, jnp.sum(dn * h * inv, axis=0, keepdims=True)


ROWS = 128
NB = 768


def col_blocks(width):
    return [slice(i, min(i + NB, width)) for i in range(0, width, NB)]


def self_forward(first, io, *refs):
    if first:
        lens, x_ref, gain_ref, w_ref, table_ref, spread_ref, a_ref, q_ref, k_ref, v_ref, o_ref, lse_ref, bias_ref = refs

        io.wait(x_ref, gain_ref)

        def norm(rows):
            a_ref[rows, :] = rms_rows(x_ref[rows, :].astype(F32), gain_ref[0:1, :]).astype(BF16)

        row_blocks(x_ref.shape[0], ROWS, norm)
        io.flush(a_ref)
    else:
        lens, a_ref, w_ref, table_ref, spread_ref, q_ref, k_ref, v_ref, o_ref, lse_ref, bias_ref = refs
    io.wait(table_ref, spread_ref)
    lines = lax.dot_general(
        table_ref[...], spread_ref[...], (((1,), (1,)), ((), ())), precision=highest,
        preferred_element_type=F32,
    )
    row = lax.broadcasted_iota(jnp.int32, (QB, LANE), 0)
    col = lax.broadcasted_iota(jnp.int32, (QB, LANE), 1)
    for h in range(bias_ref.shape[0]):
        line = jnp.broadcast_to(lines[h : h + 1, :], (QB, QB))
        tile = pltpu.roll(line, 0, 1, stride=1, stride_axis=0)[:, :LANE]
        bias_ref[h] = jnp.where(col - row + LANE < 0, masked_value, tile)
    io.flush(bias_ref)
    io.wait(lens, a_ref, w_ref)
    for i, ref in enumerate((q_ref, k_ref, v_ref)):
        ref[...] = nn(a_ref[...], w_ref[i]).astype(BF16)
        io.flush(ref)
    attend_pairs(q_ref, k_ref, v_ref, o_ref, lse_ref, bias_ref, lens[lax.axis_index("mp")])
    io.flush(o_ref, lse_ref)


def cross_forward(
    io, lens, x_ref, gain_ref, m_ref, oo, on, woo, won, wqo, wqn, wkvo, wkvn, wco, wcn,
    h1_ref, b_ref, qo, qn, ko, kn, vo, vn, oco, ocn, lse_ref, h2_ref, c_ref,
):
    io.wait(lens, m_ref)
    for k, v, w in ((ko, vo, wkvo), (kn, vn, wkvn)):
        io.wait(w)
        k[...] = nn(m_ref[...], w[0]).astype(BF16)
        v[...] = nn(m_ref[...], w[1]).astype(BF16)
        io.flush(k, v)
    io.wait(x_ref, gain_ref, oo, on, woo, won)
    for c in col_blocks(x_ref.shape[1]):
        h1_ref[:, c] = x_ref[:, c].astype(F32) + nn(oo[...], woo[:, c]) + nn(on[...], won[:, c])

    def first(rows):
        b_ref[rows, :] = rms_rows(h1_ref[rows, :], gain_ref[1:2, :]).astype(BF16)

    row_blocks(x_ref.shape[0], ROWS, first)
    io.flush(h1_ref, b_ref)
    io.wait(wqo, wqn)
    qo[...] = nn(b_ref[...], wqo[...]).astype(BF16)
    qn[...] = nn(b_ref[...], wqn[...]).astype(BF16)
    io.flush(qo, qn)
    heads = qo.shape[1] // HD
    length = lens[lax.axis_index("mp")]
    attend_pairs(qo, ko, vo, oco, lse_ref, None, length)
    attend_pairs(qn, kn, vn, ocn, lse_ref, None, length, heads)
    io.flush(oco, ocn, lse_ref)
    io.wait(wco, wcn)
    for c in col_blocks(x_ref.shape[1]):
        h2_ref[:, c] = h1_ref[:, c] + nn(oco[...], wco[:, c]) + nn(ocn[...], wcn[:, c])

    def last(rows):
        c_ref[rows, :] = rms_rows(h2_ref[rows, :], gain_ref[2:3, :]).astype(BF16)

    row_blocks(x_ref.shape[0], ROWS, last)
    io.flush(h2_ref, c_ref)


HB = 512


def hidden_block(c_ref, og_ref, wi, wd, out, at):
    root = np.float32(np.sqrt(2.0 / np.pi))
    width = out.shape[1] // 3
    gate = nn(c_ref[...], wi[0])
    up = nn(c_ref[...], wi[1])
    d_hid = nt(og_ref[...], wd[...])
    sq = gate * gate
    th = jnp.tanh(root * gate * (1.0 + 0.044715 * sq))
    half = 0.5 + 0.5 * th
    gelu = gate * half
    slope = half + 0.5 * gate * (1.0 - th * th) * (root * (1.0 + np.float32(3 * 0.044715) * sq))
    out[:, at : at + HB] = (d_hid * up * slope).astype(BF16)
    out[:, width + at : width + at + HB] = (d_hid * gelu).astype(BF16)
    out[:, 2 * width + at : 2 * width + at + HB] = (gelu * up).astype(BF16)


def ffn_other(io, c_ref, og_ref, *refs):
    weights, out = refs[:-1], refs[-1]
    io.wait(c_ref, og_ref)
    for i in range(0, len(weights), 2):
        io.wait(*weights[i : i + 2])
        hidden_block(c_ref, og_ref, weights[i], weights[i + 1], out, i // 2 * HB)
        for k in range(3):
            io.flush_columns(k * out.shape[1] // 3 + i // 2 * HB, HB, out)


def ffn_own(io, c_ref, og_ref, h2_ref, gain_ref, *refs):
    own, res_ref, g1_ref, w1_ref, dgain, acc = refs[-6:]
    weights, (nbr, win, wdn) = refs[:-9], refs[-9:-6]
    width = own.shape[1] // 3
    io.wait(c_ref, og_ref)
    for i in range(0, len(weights), 2):
        io.wait(*weights[i : i + 2])
        hidden_block(c_ref, og_ref, weights[i], weights[i + 1], own, i // 2 * HB)
    io.flush(own)
    first = True
    for i in range(0, len(weights), 2):
        wi, wd = weights[i], weights[i + 1]
        at = i // 2 * HB
        gate, up, hid = [own[:, k * width + at : k * width + at + HB] for k in range(3)]
        down, out = nt(gate, wi[0]) + nt(up, wi[1]), nn(hid, wd[...])
        g1_ref[...] = down if first else g1_ref[...] + down
        acc[...] = out if first else acc[...] + out
        first = False
    io.wait(nbr, win, wdn)
    g1_ref[...] += nt(nbr[:, 0:width], win[0]) + nt(nbr[:, width : 2 * width], win[1])
    acc[...] += nn(nbr[:, 2 * width :], wdn[...])
    io.wait(h2_ref, gain_ref)
    dgain[...] = jnp.zeros_like(dgain)

    def last(rows):
        h2 = h2_ref[rows, :]
        res_ref[rows, :] = (h2 + acc[rows, :]).astype(BF16)
        dh, dg = rms_back(h2, gain_ref[2:3, :], g1_ref[rows, :])
        g1 = og_ref[rows, :].astype(F32) + dh
        g1_ref[rows, :] = g1
        w1_ref[rows, :] = g1.astype(BF16)
        dgain[...] += dg

    row_blocks(h2_ref.shape[0], ROWS, last)
    io.flush(res_ref, g1_ref, w1_ref, dgain)


def cross_backward(
    io, lens, w1_ref, g1_ref, h1_ref, gain_ref, qo, qn, ko, kn, vo, vn, lse_ref, wco, wcn, wqo, wqn, wkvo, wkvn,
    do_own, dq_nbr, dkv_nbr, g0_ref, w0_ref, dm_ref, dgain, doo, don,
):
    half = qo.shape[1]
    heads = half // HD
    io.wait(lens, w1_ref, wco, wcn)
    doo[...] = nt(w1_ref[...], wco[...]).astype(BF16)
    don[...] = nt(w1_ref[...], wcn[...]).astype(BF16)
    length = lens[lax.axis_index("mp")]
    io.wait(qn, kn, vn, lse_ref)
    grads = ((dq_nbr, 0), (dkv_nbr, 0), (dkv_nbr, half))
    attend_back_pairs(qn, kn, vn, don, grads, lse_ref, None, length, heads)
    io.flush(dq_nbr, dkv_nbr)
    io.wait(qo, ko, vo)
    grads = ((do_own, 0), (do_own, half), (do_own, 2 * half))
    attend_back_pairs(qo, ko, vo, doo, grads, lse_ref, None, length)
    io.flush(do_own)
    io.wait(wqo, wqn, wkvo, wkvn)
    for c in col_blocks(w1_ref.shape[1]):
        g0_ref[:, c] = nt(do_own[:, 0:half], wqo[c, :]) + nt(dq_nbr[...], wqn[c, :])
        dm_ref[:, c] = (
            nt(do_own[:, half : 2 * half], wkvo[0, c, :])
            + nt(do_own[:, 2 * half :], wkvo[1, c, :])
            + nt(dkv_nbr[:, 0:half], wkvn[0, c, :])
            + nt(dkv_nbr[:, half:], wkvn[1, c, :])
        ).astype(BF16)
    io.flush(dm_ref)
    io.wait(g1_ref, h1_ref, gain_ref)
    dgain[...] = jnp.zeros_like(dgain)

    def last(rows):
        dh, dg = rms_back(h1_ref[rows, :], gain_ref[1:2, :], g0_ref[rows, :])
        g0 = g1_ref[rows, :] + dh
        g0_ref[rows, :] = g0
        w0_ref[rows, :] = g0.astype(BF16)
        dgain[...] += dg

    row_blocks(w1_ref.shape[0], ROWS, last)
    io.flush(g0_ref, w0_ref, dgain)


def self_backward(io, lens, w0_ref, *refs):
    parts, outs, do_ref = (refs[:6], refs[6:12]), refs[12:17], refs[17]
    io.wait(lens, w0_ref)
    for i, (wo, q_ref, k_ref, v_ref, lse_ref, bias_ref) in enumerate(parts):
        half = q_ref.shape[1]
        if i == 0:
            mine, diag_ref = outs[:2], outs[2]
            grads = ((outs[0], 0), (outs[1], 0), (outs[1], half))
        else:
            mine, diag_ref = outs[3:4], outs[4]
            grads = [(outs[3], k * half) for k in range(3)]
        io.wait(wo)
        do_ref[...] = nt(w0_ref[...], wo[...]).astype(BF16)
        io.wait(q_ref, k_ref, v_ref, lse_ref, bias_ref)
        attend_back_pairs(
            q_ref, k_ref, v_ref, do_ref, grads, lse_ref, bias_ref, lens[lax.axis_index("mp")], 0, diag_ref
        )
        io.flush(*mine, diag_ref)


def input_backward(io, *refs):
    pairs, (x_ref, gain_ref, g0_ref, out_ref, dgain, acc) = refs[:-6], refs[-6:]
    for i in range(0, len(pairs), 4):
        io.wait(*pairs[i : i + 4])
        term = nt(pairs[i][...], pairs[i + 1][0]) + nt(pairs[i + 2][...], pairs[i + 3][0])
        acc[...] = acc[...] + term if i else term
    io.wait(x_ref, gain_ref, g0_ref)
    dgain[...] = jnp.zeros_like(dgain)

    def some(rows):
        dh, dg = rms_back(x_ref[rows, :].astype(F32), gain_ref[0:1, :], acc[rows, :])
        out_ref[rows, :] = (g0_ref[rows, :] + dh).astype(BF16)
        dgain[...] += dg

    row_blocks(x_ref.shape[0], ROWS, some)
    io.flush(out_ref, dgain)


LINE = (0, 8, 4, 12)
ORDERS = ((1, 2), (2, 1))


def weight_grads(parts, layouts, io, *refs):
    outs, total = refs[-1 - sum(len(v) for v in layouts) : -1], refs[-1]
    rows = outs[0].shape[1]
    device = lax.axis_index("dp")
    first = 0
    for jobs, layout in zip(parts, layouts):
        mine = outs[first : first + len(layout)]
        first += len(layout)
        at = 0
        for lo, ln, ro, rn, width in jobs:
            done = 0
            while done < width:
                step = width if width <= 640 else min(512, width - done)
                src = slice(done, done + step)
                io.wait(refs[lo], refs[ro])
                total[:, 0:step] = tn(refs[lo][...], refs[ro][:, src])
                io.wait(refs[ln], refs[rn])
                total[:, 0:step] += tn(refs[ln][...], refs[rn][:, src])
                dst = slice(at + done, at + done + step)
                for out, nears in zip(mine, layout):
                    for j, mask in enumerate([near ^ far for near in nears for far in LINE]):
                        chunk = lax.bitwise_xor(device, jnp.int32(mask))
                        part = total[pl.ds(pl.multiple_of(chunk * rows, 16), rows), 0:step]
                        out[j, :, dst] = part.astype(out.dtype)
                io.flush_columns(at + done, step, *mine)
                done += step
            at += width


def add_terms(plan, io, *refs):
    at = 0
    outs = refs[-len(plan) :]
    for counts, out in zip(plan, outs):
        start = 0
        for count in counts:
            terms = refs[at : at + count]
            at += count
            io.wait(*terms)
            cols = slice(start, start + terms[0].shape[-1])
            start = cols.stop
            for j in range(out.shape[0]):
                total = terms[0][j]
                for t in terms[1:]:
                    total = total + t[j].astype(F32)
                out[j, :, cols] = total.astype(out.dtype)
        io.flush(out)


def swap_dp(v, mask):
    return lax.ppermute(v, "dp", [(i, i ^ mask) for i in range(16)])


def swap_mp(v):
    return lax.ppermute(v, "mp", [(0, 1), (1, 0)])


def make_grads(parts, depth, n_data, direct=False):
    if n_data != 16:

        def piece(a):
            if not isinstance(a, tuple):
                return a
            value = a[0]
            for axis, start, size in a[1]:
                start = start() if callable(start) else start
                value = lax.dynamic_slice_in_dim(value, start, size, axis)
            return value

        cols = []
        for job in [job for jobs in parts for job in jobs]:
            lo, ln, ro, rn = [piece(a) for a in job]
            cols.append(tn(lo, ro) + tn(ln, rn))
        return lax.psum_scatter(
            jnp.concatenate(cols, axis=1), "dp", scatter_dimension=0, tiled=True
        )
    arrays, keys, plan, shapes, layouts = [], [], [], [], []
    rows = depth // 16
    for jobs in parts:
        spots = []
        for job in jobs:
            place = []
            for a in job:
                key = (id(a[0]),) + a[1:] if isinstance(a, tuple) else id(a)
                if key not in keys:
                    arrays.append(a)
                    keys.append(key)
                place.append(keys.index(key))
            spots.append(tuple(place) + (job[2][1][-1][2],))
        plan.append(tuple(spots))
        width = sum(job[2][1][-1][2] for job in jobs)
        if direct:
            layouts.append(((0,), (1,), (2,), (3,)))
        else:
            one, two = ORDERS[len(layouts)]
            layouts.append(((0, two), (one, one ^ two)))
        for nears in layouts[-1]:
            shapes.append(sds((4 * len(nears), rows, width), F32 if 0 in nears else BF16))
    widest = max(job[4] if job[4] <= 640 else 512 for jobs in plan for job in jobs)
    return dma_call(
        functools.partial(weight_grads, tuple(plan), tuple(layouts)),
        shapes,
        arrays,
        0,
        [pltpu.VMEM((depth, widest), F32)],
        flops=4 * 512 * depth * 1024,
        n_writes=64,
    )


class Reduction:
    def __init__(self, made, n_data, direct=False, near=False):
        self.plain = n_data != 16
        self.made, self.direct = made, direct
        self.far = []
        if not self.plain:
            if direct or near:
                self.keeps, self.done = [made[0]], 2
                self.got = [[swap_dp(v, m) for v, m in zip(made[1:], (1, 2, 3))]]
            else:
                self.keeps, self.done = list(made[::2]), 1
                self.got = [[swap_dp(v, o[0])] for v, o in zip(made[1::2], ORDERS)]

    def near(self, start, size):
        return [[leading(t, start, size) for t in [k] + g] for k, g in zip(self.keeps, self.got)]

    def sends(self):
        rows, widths = self.keeps[0].shape[1], [k.shape[2] for k in self.keeps]
        if self.done == 1:
            parts = self.near(4, 4)
            shapes = [sds((4, rows, w), BF16) for w in widths]
            return [(len(p),) for p in parts], shapes, [t for p in parts for t in p]
        if self.direct:
            spots = ((1, 1), (2, 1), (3, 1))
        else:
            spots = ((2, 2),) if self.done == 2 else ((1, 1),)
        plan, shapes, terms = [], [], []
        for start, size in spots:
            parts, at = self.near(start, size), 0
            for part, w in zip(parts, widths):
                part += [leading(columns(t, at, w), start, size) for t in self.far]
                at += w
            plan.append(tuple(len(p) for p in parts))
            shapes.append(sds((size, rows, sum(widths)), BF16))
            terms += [t for part in parts for t in part]
        return plan, shapes, terms

    def sent(self, sends):
        if self.done == 1:
            for got, send, order in zip(self.got, sends, ORDERS):
                got.append(swap_dp(send, order[1]))
        elif self.direct:
            self.far = [swap_dp(v, m) for v, m in zip(sends, LINE[1:])]
        else:
            self.far.append(swap_dp(sends[0], 4 if self.done == 2 else 8))
        self.done += 1

    def terms(self):
        if self.plain:
            return [[self.made[None]]]
        parts, at = self.near(0, 1), 0
        for part, k in zip(parts, self.keeps):
            part += [leading(columns(t, at, k.shape[2]), 0, 1) for t in self.far]
            at += k.shape[2]
        return parts


def exchange(*steps, others=()):
    steps = [r for r in steps if not r.plain]
    if not steps:
        return []
    made = [r.sends() for r in steps]
    plan = [p for m in made for p in m[0]]
    shapes = [p for m in made for p in m[1]]
    terms = [p for m in made for p in m[2]]
    if others:
        terms[0] = (after(terms[0][0], *others), terms[0][1])
    sends = dma_call(functools.partial(add_terms, tuple(plan)), shapes, terms)
    at = 0
    for r, m in zip(steps, made):
        r.sent(sends[at : at + len(m[0])])
        at += len(m[0])
    return list(sends)


def squares_of(mats, first, all_ref, cols_ref, row_sums):
    rows = all_ref.shape[0]
    lane = lax.broadcasted_iota(jnp.int32, (rows, LANE), 1)
    for i, (start, width) in enumerate(mats):
        part = all_ref[:, start : start + width]
        sq = part * part
        cols_ref[:, start : start + width] = jnp.sum(sq, axis=0, keepdims=True)
        row_sums = row_sums + jnp.where(lane == first + i, jnp.sum(sq, axis=1, keepdims=True), 0.0)
    return row_sums


def end_sums(counts, io, refs, all_ref):
    start = at = 0
    for count in counts:
        terms = refs[at : at + count]
        io.wait(*terms)
        total = terms[0][0]
        for t in terms[1:]:
            total = total + t[0].astype(F32)
        all_ref[:, start : start + total.shape[1]] = total
        at += count
        start += total.shape[1]


def early_statistics(counts, mats, io, *refs):
    all_ref, cols_ref, rows_ref = refs[-3:]
    end_sums(counts, io, refs, all_ref)
    rows_ref[...] = squares_of(mats, 0, all_ref, cols_ref, jnp.zeros_like(rows_ref))
    io.flush(all_ref, cols_ref, rows_ref)


def statistics(counts, mats, first, io, *refs):
    all_ref, pack_ref, cols_ref = refs[-3:]
    rows_ref, spread = refs[-10], refs[-4]
    gains, diags = refs[-9:-6], refs[-6:-4]
    io.wait(rows_ref, *gains, *diags, spread)
    pack_ref[...] = jnp.zeros_like(pack_ref)
    for i, gain in enumerate(gains):
        pack_ref[i : i + 1, :] = gain[...]
    for i, diag in enumerate(diags):
        heads = diag.shape[0]
        lines = jnp.concatenate([diag[h] for h in range(heads)], axis=0)
        pack_ref[8 : 8 + heads, i * LANE : i * LANE + BUCKETS] = lax.dot_general(
            lines, spread[...], (((1,), (0,)), ((), ())), precision=highest,
            preferred_element_type=F32,
        )
    end_sums(counts, io, refs, all_ref)
    rows = all_ref.shape[0]
    pack_ref[16 : 16 + rows, 0:LANE] = squares_of(mats, first, all_ref, cols_ref, rows_ref[...])
    io.flush(all_ref, pack_ref, cols_ref)


def merge_kernel(io, own_ref, got_ref, early_ref, late_ref, out_ref, rows_ref):
    io.wait(own_ref, got_ref, early_ref, late_ref)
    rows = rows_ref.shape[0]
    n_early, depth = early_ref.shape[1], own_ref.shape[1]
    n_all = n_early + late_ref.shape[1]
    full = own_ref[16 : 16 + rows, 0:LANE] + got_ref[16 : 16 + rows, 0:LANE]
    rows_ref[...] = full
    out_ref[:, 0:n_early] = early_ref[...]
    out_ref[:, n_early:n_all] = late_ref[...]
    at = n_all
    for i in range(3):
        out_ref[:, at : at + depth] = own_ref[i : i + 1, :] + got_ref[i : i + 1, :]
        at += depth
    out_ref[:, at : at + LANE] = jnp.sum(full, axis=0, keepdims=True)
    for side in range(2):
        mine = own_ref[8:16, side * LANE : (side + 1) * LANE]
        theirs = got_ref[8:16, (1 - side) * LANE : (2 - side) * LANE]
        both = mine + theirs
        for h in range(8):
            at += LANE
            out_ref[:, at : at + LANE] = both[h : h + 1]
    io.flush(out_ref, rows_ref)


def turn(v):
    rows = v.shape[0]
    if rows < LANE:
        v = jnp.concatenate([v, jnp.zeros((LANE - rows, v.shape[1]), v.dtype)], axis=0)
    return jnp.transpose(v)[:, :rows]


def update_kernel(plan, n_terms, io, *refs):
    terms = refs[:n_terms]
    rows_ref, early_ref, late_ref = refs[n_terms : n_terms + 3]
    weights = refs[n_terms + 3 : n_terms + 3 + len(plan)]
    outs = refs[n_terms + 3 + len(plan) :]
    io.wait(*terms)
    line = functools.reduce(jnp.add, [p[...] for p in terms])
    n_early = early_ref.shape[1]
    n_all = n_early + late_ref.shape[1]
    gain_ref, table_ref, norm_ref = outs[0], outs[1], outs[-1]
    depth = gain_ref.shape[1]
    gains_at, totals_at = n_all, n_all + 3 * depth
    tables_at = totals_at + LANE
    for i in range(3):
        gain_ref[i : i + 1, :] = line[:, gains_at + i * depth : gains_at + (i + 1) * depth]
    for h in range(table_ref.shape[0]):
        at = tables_at + h * LANE
        table_ref[h : h + 1, :] = line[:, at : at + BUCKETS]
    totals = line[:, totals_at:tables_at]
    gains, tables = line[:, gains_at:totals_at], line[:, tables_at:]
    squares = (
        jnp.sum(gains * gains, axis=1, keepdims=True)
        + jnp.sum(tables * tables, axis=1, keepdims=True)
        + jnp.sum(totals, axis=1, keepdims=True)
    )
    norm_ref[...] = jnp.sqrt(squares)
    io.flush(gain_ref, table_ref, norm_ref)
    io.wait(rows_ref, early_ref, late_ref)
    row_sums = rows_ref[...]
    row_lines = turn(row_sums)
    at = 2
    for (natural, members), weight in zip(plan, weights):
        new_ref, row_out, col_out = outs[at : at + 3]
        at += 3
        io.wait(weight)
        for k, (i, start, width) in enumerate(members):
            size = 2 * width
            by_row = row_sums[:, i : i + 1] / size + stat_eps
            by_col = line[:, start : start + width] / depth + stat_eps
            mean = totals[:, i : i + 1] / (size * depth) + stat_eps
            if start < n_early:
                grad = early_ref[:, start : start + width]
            else:
                grad = late_ref[:, start - n_early : start - n_early + width]
            change = (
                learn_rate
                * grad
                * lax.rsqrt(by_row * by_col / mean)
            )
            row_line = row_lines[i : i + 1, :] / size + stat_eps
            new_ref[k] = weight[k].astype(F32) - change
            lines = (row_line, by_col) if natural else (by_col, row_line)
            for out, value in zip((row_out, col_out), lines):
                if len(out.shape) == 1:
                    out[...] = value.reshape(out.shape)
                else:
                    out[k : k + 1, :] = value
        io.flush(new_ref, row_out, col_out)


def after(value, *others):
    return lax.optimization_barrier((value,) + others)[0]


def body(
    tokens,
    memory,
    out_grad,
    tgt_lens,
    mem_lens,
    norm_gains,
    rel_table,
    self_qkv,
    self_out,
    cross_q,
    cross_kv,
    cross_out,
    ffn_in,
    ffn_out,
):
    n_data = lax.axis_size("dp")
    mp = lax.axis_index("mp")
    dp = lax.axis_index("dp")
    rows = tokens.shape[0]
    depth = tokens.shape[1]
    heads = rel_table.shape[1]
    half = heads * HD
    width = ffn_out.shape[0]
    chunk = depth // n_data
    qkv_n = swap_mp(self_qkv)
    table = rel_table.T
    table_n = swap_mp(table)
    so_n = swap_mp(self_out)
    ckv_n = swap_mp(cross_kv)
    cq_n = swap_mp(cross_q)

    dist = np.arange(QB)
    line_dist = np.where(dist < LANE, dist + LANE, dist - LANE)
    spread = jnp.asarray((bucket_of(line_dist)[:, None] == np.arange(BUCKETS)).astype(np.float32))
    gather = jnp.asarray((bucket_of(dist)[:, None] == np.arange(BUCKETS)).astype(np.float32))

    attn_flops = 4 * rows * rows * HD * heads
    bias_shape = sds((heads, QB, LANE), F32)
    act = sds((rows, half), BF16)
    wide = sds((rows, depth), BF16)
    full = sds((rows, depth), F32)
    gain_row = sds((1, depth), F32)
    lse = sds((heads, 1, rows), F32)
    lse2 = sds((2 * heads, 1, rows), F32)
    a, qs_o, ks_o, vs_o, os_o, lses_o, bias_o = dma_call(
        functools.partial(self_forward, True),
        [wide, act, act, act, act, lse, bias_shape],
        [tgt_lens, tokens, norm_gains, self_qkv, table, spread],
        1,
        flops=6 * rows * depth * half + attn_flops,
    )
    a, qkv_n, table_n, so_n, cq_n, ckv_n, cross_out_b, ffn_in_b, ffn_out_b, out_grad_b = (
        lax.optimization_barrier(
            (a, qkv_n, table_n, so_n, cq_n, ckv_n, cross_out, ffn_in, ffn_out, out_grad)
        )
    )
    co_n = swap_mp(cross_out_b)
    fi_n = swap_mp(ffn_in_b)
    fo_n = swap_mp(ffn_out_b)
    og_n = swap_mp(out_grad_b)
    a_n = swap_mp(a)
    qs_n, ks_n, vs_n, os_n, lses_n, bias_n = dma_call(
        functools.partial(self_forward, False),
        [act, act, act, act, lse, bias_shape],
        [tgt_lens, a, qkv_n, table_n, spread],
        1,
        flops=6 * rows * depth * half + attn_flops,
    )
    mem_own = leading(memory, lambda: pl.multiple_of(lax.axis_index("mp") * rows, rows), rows)
    mem_nbr = leading(memory, lambda: pl.multiple_of((1 - lax.axis_index("mp")) * rows, rows), rows)
    os_x = swap_mp(os_n)
    h1, b, qc_o, qc_n, kc_o, kc_n, vc_o, vc_n, oc_o, oc_n, lsec, h2, c = dma_call(
        cross_forward,
        [full, wide, act, act, act, act, act, act, act, act, lse2, full, wide],
        [mem_lens, tokens, norm_gains, mem_own, os_o, os_n, self_out, so_n, cross_q, cq_n, cross_kv, ckv_n, cross_out, co_n],
        1,
        flops=20 * rows * depth * half + 2 * attn_flops,
    )
    c, os_x, a_n = lax.optimization_barrier((c, os_x, a_n))
    b_n = swap_mp(b)
    oc_x = swap_mp(oc_n)
    c_n = swap_mp(c)
    hid = sds((rows, 3 * width), BF16)
    def hidden_weights(wi, wd):
        return [v for i in range(0, width, HB) for v in (columns(wi, i, HB), leading(wd, i, HB))]

    f_nbr = dma_call(
        ffn_other,
        [hid],
        [c, out_grad] + hidden_weights(fi_n, fo_n),
        flops=6 * rows * depth * width,
        n_writes=3 * width // HB,
    )[0]
    f_x = swap_mp(f_nbr)
    f_own, result, g1, w1, gain_c = dma_call(
        ffn_own,
        [hid, wide, full, wide, gain_row],
        [c, out_grad, h2, norm_gains] + hidden_weights(ffn_in, ffn_out) + [f_nbr, fi_n, fo_n],
        0,
        [pltpu.VMEM((rows, depth), F32)],
        flops=18 * rows * depth * width,
    )
    w1_n = swap_mp(w1)
    def pair(own, nbr, start, size):
        return columns(own, start, size), columns(nbr, start, size)

    w1, f_own = lax.optimization_barrier((w1, f_own))
    early_down = width // 2
    left = (2 * width + early_down) // 2
    ffn_made = make_grads(
        (
            ((c, c_n) + pair(f_own, f_x, 0, left),),
            (
                (c, c_n) + pair(f_own, f_x, left, 2 * width - left),
                (out_grad, og_n) + pair(f_own, f_x, 2 * width, early_down),
            ),
        ),
        depth,
        n_data,
    )
    w1_b = after(w1, w1_n, b_n, oc_x, *jax.tree.leaves(ffn_made))
    ffn_sum = Reduction(ffn_made, n_data)
    c_own, cq_nbr, ckv_nbr, g0, w0, d_mem, gain_b = dma_call(
        cross_backward,
        [sds((rows, 3 * half), BF16), act, sds((rows, 2 * half), BF16), full, wide, wide, gain_row],
        [mem_lens, w1_b, g1, h1, norm_gains, qc_o, qc_n, kc_o, kc_n, vc_o, vc_n, lsec, cross_out, co_n, cross_q, cq_n, cross_kv, ckv_n],
        1,
        [pltpu.VMEM((rows, half), BF16), pltpu.VMEM((rows, half), BF16)],
        flops=16 * rows * depth * half + 5 * attn_flops,
    )
    cq_x, ckv_x = swap_mp(cq_nbr), swap_mp(ckv_nbr)
    w0_n = swap_mp(w0)
    diag = sds((heads, 1, QB), F32)

    sent = exchange(ffn_sum, others=(c_own,))
    if sent:
        w0, w0_n, cq_x, ckv_x = lax.optimization_barrier((w0, w0_n, cq_x, ckv_x, *sent))[:4]
    split = 2 * LANE
    split = 2 * LANE
    cross_made = make_grads(
        (
            (
                (out_grad, og_n) + pair(f_own, f_x, 2 * width + early_down, width - early_down),
                (w1, w1_n) + pair(oc_o, oc_x, 0, half),
                (w0, w0_n) + pair(os_o, os_x, 0, split),
            ),
            (
                (w0, w0_n) + pair(os_o, os_x, split, half - split),
                (b, b_n, columns(c_own, 0, half), columns(cq_x, 0, half)),
                (mem_own, mem_nbr, columns(c_own, half, 2 * half), columns(ckv_x, 0, 2 * half)),
            ),
        ),
        depth,
        n_data,
    )
    cross_sum = Reduction(cross_made, n_data)
    sent = exchange(ffn_sum, others=jax.tree.leaves(cross_made))
    w0_b = after(w0, *sent, *jax.tree.leaves(cross_made))
    sq_nbr, skv_nbr, diag_n, s_own, diag_o = dma_call(
        self_backward,
        [act, sds((rows, 2 * half), BF16), diag, sds((rows, 3 * half), BF16), diag],
        [tgt_lens, w0_b, so_n, qs_n, ks_n, vs_n, lses_n, bias_n]
        + [self_out, qs_o, ks_o, vs_o, lses_o, bias_o],
        1,
        [pltpu.VMEM((rows, half), BF16)],
        flops=4 * rows * depth * half + 6 * attn_flops,
    )
    sent = exchange(ffn_sum, cross_sum, others=(s_own,))
    s_own, sq_nbr, skv_nbr = lax.optimization_barrier((s_own, sq_nbr, skv_nbr, *sent))[:3]
    sq_x, skv_x = swap_mp(sq_nbr), swap_mp(skv_nbr)
    grad_in, gain_a = dma_call(
        input_backward,
        [wide, gain_row],
        [
            v
            for i in range(3)
            for d, at, w in (
                (s_own, i, self_qkv),
                (sq_nbr if i == 0 else skv_nbr, max(i - 1, 0), qkv_n),
            )
            for v in (columns(d, at * half, half), leading(w, i, 1))
        ]
        + [tokens, norm_gains, g0],
        0,
        [pltpu.VMEM((rows, depth), F32)],
        flops=12 * rows * depth * half,
    )
    s_own, sq_x, skv_x = lax.optimization_barrier((s_own, sq_x, skv_x, grad_in))[:3]
    self_made = make_grads(
        (
            (
                (a, a_n, columns(s_own, 0, half), columns(sq_x, 0, half)),
                (a, a_n, columns(s_own, half, 2 * half), columns(skv_x, 0, 2 * half)),
            ),
        ),
        depth,
        n_data,
        direct=True,
    )
    self_sum = Reduction(self_made, n_data, direct=True)
    exchange(cross_sum, others=jax.tree.leaves(self_made))
    exchange(cross_sum)

    sizes = [width, width, width] + [half] * 8
    starts = [int(v) for v in np.cumsum([0] + sizes[:-1])]
    mats = tuple(zip(starts, sizes))
    n_all = sum(sizes)
    plan = (
        (True, (8, 9, 10)),
        (False, (4,)),
        (True, (5,)),
        (True, (6, 7)),
        (False, (3,)),
        (True, (0, 1)),
        (False, (2,)),
    )
    plan = tuple((n, tuple((i, starts[i], sizes[i]) for i in m)) for n, m in plan)
    weights = (self_qkv, self_out, cross_q, cross_kv, cross_out, ffn_in, ffn_out)
    slices, shapes = [], [sds((3, depth), F32), sds((heads, BUCKETS), F32)]
    for (natural, members), weight in zip(plan, weights):
        count, size = len(members), members[0][2]
        if natural:
            stacked = weight.reshape((count,) + weight.shape[-2:])
            part = cut(stacked, 1, lambda: pl.multiple_of(lax.axis_index("dp") * chunk, chunk), chunk)
            if n_data != 16:
                part = lax.dynamic_slice_in_dim(stacked, dp * chunk, chunk, 1)
        else:
            part = lax.dynamic_slice_in_dim(weight, dp * chunk, chunk, 1).T[None]
        slices.append(part)
        line_sizes = (chunk, size) if natural else (size, chunk)
        shapes += [sds((count, chunk, size), F32)]
        shapes += [sds((n,) if weight.ndim == 2 else (count, n), F32) for n in line_sizes]
    shapes.append(sds((1, 1), F32))
    sent = exchange(self_sum, others=[v for v in slices if not isinstance(v, tuple)])
    n_early = starts[8]
    early = ffn_sum.terms() + cross_sum.terms()
    if sent:
        early[0][0] = (after(early[0][0][0], *sent), early[0][0][1])
    grads, cols, row_parts = dma_call(
        functools.partial(early_statistics, tuple(len(t) for t in early), mats[:8]),
        [sds((chunk, n_early), F32), sds((1, n_early), F32), sds((chunk, LANE), F32)],
        [t for part in early for t in part],
    )
    late = self_sum.terms()
    pack_rows = -(-(16 + chunk) // 8) * 8
    late_grads, pack, late_cols = dma_call(
        functools.partial(statistics, tuple(len(t) for t in late), tuple((a - n_early, b) for a, b in mats[8:]), 8),
        [sds((chunk, n_all - n_early), F32), sds((pack_rows, depth), F32), sds((1, n_all - n_early), F32)],
        [t for part in late for t in part] + [row_parts, gain_a, gain_b, gain_c, diag_o, diag_n, gather],
    )
    line, row_sums = dma_call(
        merge_kernel,
        [sds((1, n_all + 3 * depth + 17 * LANE), F32), sds((chunk, LANE), F32)],
        [pack, swap_mp(pack), cols, late_cols],
    )
    if n_data == 16:
        terms = [line]
        for group in ((1, 2, 3), (4, 8, 12)):
            if len(terms) > 1:
                terms = [functools.reduce(jnp.add, terms)]
            terms = terms + [swap_dp(terms[0], m) for m in group]
    else:
        terms = [lax.psum(line, "dp")]

    done = dma_call(
        functools.partial(update_kernel, plan, len(terms)),
        shapes,
        terms + [row_sums, grads, late_grads] + slices,
    )
    finals = [result, grad_in, d_mem, done[0], done[1].T]
    for i, ((natural, _), weight) in enumerate(zip(plan, weights)):
        new, row, col = done[2 + 3 * i : 5 + 3 * i]
        if weight.ndim == 2:
            new = new[0] if natural else new[0].T
        finals += [new, row, col]
    return tuple(finals + [done[-1][0, 0]])


def solution(mesh):
    placed = (
        P(("dp", "mp"), None),
        P("dp", None),
        P(("dp", "mp"), None),
        P("dp"),
        P("dp"),
        P(),
        P(None, "mp"),
        P(None, None, "mp"),
        P("mp", None),
        P(None, "mp"),
        P(None, None, "mp"),
        P("mp", None),
        P(None, None, "mp"),
        P("mp", None),
    )
    return jax.shard_map(
        body,
        mesh=mesh,
        in_specs=placed,
        out_specs=(
            P(("dp", "mp"), None),
            P(("dp", "mp"), None),
            P(("dp", "mp"), None),
            P(),
            P(None, "mp"),
            P(None, "dp", "mp"),
            P(None, "dp"),
            P(None, "mp"),
            P("mp", "dp"),
            P("mp"),
            P("dp"),
            P("dp", "mp"),
            P("dp"),
            P("mp"),
            P(None, "dp", "mp"),
            P(None, "dp"),
            P(None, "mp"),
            P("mp", "dp"),
            P("mp"),
            P("dp"),
            P(None, "dp", "mp"),
            P(None, "dp"),
            P(None, "mp"),
            P("mp", "dp"),
            P("mp"),
            P("dp"),
            P(),
        ),
        check_vma=False,
    )
```

```python
import functools

import jax
import jax.numpy as jnp
import numpy as np
from jax import lax
from jax.experimental import pallas as pl
from jax.experimental.pallas import tpu as pltpu
from jax.sharding import PartitionSpec as P

BUCKETS = 32
MAX_DIST = 128
HD = 64
LANE = 128
VMEM_BYTES = 64 * 1024 * 1024 - 64 * 1024
QB = 256
AHEAD = 3
norm_eps = 1e-06
stat_eps = 1e-30
masked_value = -1e30
learn_rate = 0.04
highest = lax.Precision.HIGHEST
F32 = jnp.float32
BF16 = jnp.bfloat16
VMEM = pl.BlockSpec(memory_space=pltpu.VMEM)
SMEM = pl.BlockSpec(memory_space=pltpu.SMEM)


def bucket_of(dist):
    exact_span = BUCKETS // 2
    dist = np.maximum(dist, 0)
    log_ratio = np.log(np.maximum(dist, 1) / exact_span) / np.log(MAX_DIST / exact_span)
    far = np.minimum(
        exact_span + np.floor(log_ratio * (BUCKETS - exact_span)).astype(np.int64), BUCKETS - 1
    )
    return np.where(dist < exact_span, dist, far).astype(np.int32)


def nn(a, b):
    return lax.dot_general(a, b, (((1,), (0,)), ((), ())), preferred_element_type=F32)


def nt(a, b):
    return lax.dot_general(a, b, (((1,), (1,)), ((), ())), preferred_element_type=F32)


def tn(a, b):
    return lax.dot_general(a, b, (((0,), (0,)), ((), ())), preferred_element_type=F32)


class Copies:
    def __init__(self, pairs_in, pairs_out, sem_in, sem_out):
        self.reads = [
            (dst, pltpu.make_async_copy(src, dst, sem_in.at[i]))
            for i, (src, dst) in enumerate(pairs_in)
        ]
        self.writes = [
            (src, pltpu.make_async_copy(src, dst, sem_out.at[i]))
            for i, (src, dst) in enumerate(pairs_out)
        ]
        self.pairs_out, self.sem_out = pairs_out, sem_out
        self.pending, self.begun = list(self.reads), []
        for _, copy in self.reads:
            copy.start()

    def wait(self, *refs):
        for ref in refs:
            for entry in self.pending:
                if entry[0] is ref:
                    entry[1].wait()
                    self.pending = [e for e in self.pending if e is not entry]
                    break

    def flush(self, *refs):
        for ref in refs:
            for src, copy in self.writes:
                if src is ref:
                    copy.start()
                    self.begun.append(copy)

    def flush_columns(self, start, size, *refs):
        cols = pl.ds(start, size)
        for src, dst in self.pairs_out:
            if not any(src is r for r in refs):
                continue
            copy = pltpu.make_async_copy(
                src.at[..., cols], dst.at[..., cols], self.sem_out.at[len(self.begun)]
            )
            copy.start()
            self.begun.append(copy)

    def close(self):
        assert not self.pending and len(self.begun) >= len(self.writes)
        for copy in self.begun:
            copy.wait()


def columns(array, start, size):
    return cut(array, -1, start, size)


def leading(array, start, size):
    return cut(array, 0, start, size)


def cut(array, axis, start, size):
    array, cuts = array if isinstance(array, tuple) else (array, ())
    return (array, cuts + ((axis % array.ndim, start, size),))


def dma_call(kernel, outs, args, n_smem=0, scratch=(), flops=0, n_writes=0):
    args = [a if isinstance(a, tuple) else (a, ()) for a in args]
    arrays = [a[0] for a in args]
    n_in, n_out = len(arrays), len(outs)
    held = []
    for i, (a, cuts) in enumerate(args):
        shape = list(a.shape)
        for axis, _, size in cuts:
            shape[axis] = size
        shape = tuple(shape)
        held.append((pltpu.SMEM if i < n_smem else pltpu.VMEM)(shape, a.dtype))
    held += [pltpu.VMEM(o.shape, o.dtype) for o in outs]

    def part(ref, arg):
        index = [slice(None)] * arg[0].ndim
        for axis, start, size in arg[1]:
            index[axis] = pl.ds(start() if callable(start) else start, size)
        return ref.at[tuple(index)] if arg[1] else ref

    def run(*refs):
        given, made = refs[:n_in], refs[n_in : n_in + n_out]
        local = refs[n_in + n_out : 2 * (n_in + n_out)]
        rest, (sem_in, sem_out) = refs[2 * (n_in + n_out) : -2], refs[-2:]
        sources = [part(r, a) for r, a in zip(given, args)]
        io = Copies(
            list(zip(sources, local[:n_in])), list(zip(local[n_in:], made)), sem_in, sem_out
        )
        kernel(io, *local, *rest)
        io.close()

    moved = sum(h.shape[0] * int(np.prod(h.shape[1:])) * np.dtype(h.dtype).itemsize for h in held)
    return pl.pallas_call(
        run,
        out_shape=list(outs),
        in_specs=[pl.BlockSpec(memory_space=pltpu.HBM)] * n_in,
        out_specs=[pl.BlockSpec(memory_space=pltpu.HBM)] * n_out,
        scratch_shapes=held
        + list(scratch)
        + [pltpu.SemaphoreType.DMA((n_in,)), pltpu.SemaphoreType.DMA((max(n_out, n_writes),))],
        compiler_params=pltpu.CompilerParams(vmem_limit_bytes=VMEM_BYTES),
        cost_estimate=pl.CostEstimate(flops=flops, bytes_accessed=moved, transcendentals=0),
    )(*arrays)


def sds(shape, dtype):
    return jax.ShapeDtypeStruct(shape, dtype)


def head_masks(dtype):
    lane = lax.broadcasted_iota(jnp.int32, (1, LANE), 1)
    return [(lane < HD).astype(dtype), (lane >= HD).astype(dtype)]


def bias_chunks(bias_ref, head, first, count, blocks):
    near = bias_ref[head, 0:LANE, :]
    diag = bias_ref[head, LANE : 2 * LANE, :]
    const = jnp.broadcast_to(bias_ref[head, 0:1, :], (LANE, LANE))
    none = jnp.full((LANE, LANE), masked_value, F32)

    def tile(offset):
        return none if offset < 0 else diag if offset == 0 else near if offset == 1 else const

    return [
        jnp.concatenate([tile(first + i - j) for i in range(blocks)], axis=1)
        for j in range(count)
    ]


def score_chunks(keys_masked, queries, bias_ref, head, first, count, length):
    width = queries.shape[0]
    scores = nt(keys_masked[: count * LANE], queries)
    row = lax.broadcasted_iota(jnp.int32, (LANE, width), 0)
    chunks = []
    if bias_ref is not None:
        bias = bias_chunks(bias_ref, head, first, count, width // LANE)
    for j in range(count):
        part = scores[j * LANE : (j + 1) * LANE]
        if bias_ref is not None:
            part = part + bias[j]
        chunks.append(jnp.where(row < length - j * LANE, part, masked_value))
    return chunks


def attend_back_pairs(
    q_ref, k_ref, v_ref, do_ref, grads, lse_ref, bias_ref, length, lse_base=0, diag_ref=None
):
    rows, width = q_ref.shape
    keys = k_ref.shape[0]
    masks = head_masks(BF16)
    lane_id = lax.broadcasted_iota(jnp.int32, (1, QB), 1)
    step = QB
    n_blocks = rows // step
    units = [(h, b) for h in range(width // HD) for b in range(n_blocks)]
    kept = {}

    def pair_values(p):
        if p not in kept:
            lanes = slice(p * LANE, (p + 1) * LANE)
            k_pair, v_pair = k_ref[:, lanes], v_ref[:, lanes]
            kept[p] = (
                [k_pair * m for m in masks],
                [v_pair * m for m in masks],
                jnp.transpose(k_pair.astype(F32)).astype(BF16),
            )
        return kept[p]

    def start(h, block):
        p, t = divmod(h, 2)
        lanes = slice(p * LANE, (p + 1) * LANE)
        count = (block + 1) * step // LANE if bias_ref is not None else keys // LANE
        k_m, v_m, _ = pair_values(p)
        at = slice(block * step, (block + 1) * step)
        q_blk, do_blk = q_ref[at, lanes], do_ref[at, lanes]
        chunks = score_chunks(k_m[t], q_blk, bias_ref, h, block * step // LANE, count, length)
        d_probs = nt(v_m[t][: count * LANE], do_blk)
        return chunks, [d_probs[j * LANE : (j + 1) * LANE] for j in range(count)]

    ahead = start(*units[0])
    sums = {}
    for i, (h, block) in enumerate(units):
        p, t = divmod(h, 2)
        lanes = slice(p * LANE, (p + 1) * LANE)
        at = slice(block * step, (block + 1) * step)
        chunks, d_probs = ahead
        if i + 1 < len(units):
            ahead = start(*units[i + 1])
        count = len(chunks)
        lse = lse_ref[lse_base + h, :, at]
        probs = [jnp.exp(c - lse) for c in chunks]
        dot = functools.reduce(
            jnp.add, [jnp.sum(a * b, axis=0, keepdims=True) for a, b in zip(probs, d_probs)]
        )
        d_scores = [(a * (b - dot)).astype(BF16) for a, b in zip(probs, d_probs)]
        if t == 0 and block == 0:
            sums = dict(
                dv=[None] * (keys // LANE), dk=[None] * (keys // LANE), dq=[[], []]
            )
        if block == 0:
            near_sum = jnp.zeros((LANE, LANE), F32)
            diag_sum = jnp.zeros((LANE, LANE), F32)
            far_sum = jnp.zeros((1, LANE), F32)
        if diag_ref is not None:
            for j in range(count):
                wide = d_scores[j].astype(F32)
                for c in range(step // LANE):
                    tile = wide[:, c * LANE : (c + 1) * LANE]
                    offset = block * step // LANE + c - j
                    if offset == 0:
                        diag_sum = diag_sum + tile
                    elif offset == 1:
                        near_sum = near_sum + tile
                    elif offset > 1:
                        far_sum = far_sum + jnp.sum(tile, axis=0, keepdims=True)
        d_all = jnp.concatenate(d_scores, axis=0)
        p_all = jnp.concatenate([a.astype(BF16) for a in probs], axis=0)
        dv_new = nn(p_all, do_ref[at, lanes] * masks[t])
        dk_new = nn(d_all, q_ref[at, lanes] * masks[t])
        for name, new in (("dv", dv_new), ("dk", dk_new)):
            for j in range(count):
                part = new[j * LANE : (j + 1) * LANE]
                old = sums[name][j]
                sums[name][j] = part if old is None else old + part
        k_t = pair_values(p)[2]
        sums["dq"][t].append(nn(k_t[t * HD : (t + 1) * HD, : count * LANE], d_all))
        if diag_ref is not None and block == n_blocks - 1:
            both = jnp.concatenate([near_sum, diag_sum], axis=0)
            both = jnp.concatenate([both, jnp.zeros_like(both)], axis=1)
            acc = jnp.zeros((8, QB), F32)
            for g in range(QB // 8):
                piece = both[8 * g : 8 * g + 8]
                turned = (LANE - 8 * g) % QB
                acc = acc + (pltpu.roll(piece, turned, 1) if turned else piece)
            line = acc[0:1]
            for g in range(1, 8):
                line = line + pltpu.roll(acc, QB - g, 1)[g : g + 1]
            far_total = jnp.sum(far_sum, axis=1, keepdims=True)
            diag_ref[h] = line + jnp.where(lane_id == QB - 1, far_total, 0.0)
        if t == 1 and block == n_blocks - 1:
            dq_t = jnp.concatenate([jnp.concatenate(v, axis=1) for v in sums["dq"]], axis=0)
            done = (
                jnp.transpose(dq_t),
                jnp.concatenate(sums["dk"], axis=0),
                jnp.concatenate(sums["dv"], axis=0),
            )
            for (ref, first), value in zip(grads, done):
                ref[:, first + p * LANE : first + (p + 1) * LANE] = value.astype(BF16)


def attend_pairs(q_ref, k_ref, v_ref, o_ref, lse_ref, bias_ref, length, lse_base=0):
    rows, width = q_ref.shape
    keys = k_ref.shape[0]
    masks = head_masks(BF16)
    step = QB
    n_blocks = rows // step
    units = [(h, b) for h in range(width // HD) for b in range(n_blocks)]

    def start(h, block):
        p, t = divmod(h, 2)
        lanes = slice(p * LANE, (p + 1) * LANE)
        k_m = k_ref[:, lanes] * masks[t]
        count = (block + 1) * step // LANE if bias_ref is not None else keys // LANE
        q_blk = q_ref[block * step : (block + 1) * step, lanes]
        return score_chunks(k_m, q_blk, bias_ref, h, block * step // LANE, count, length)

    queue = [start(*u) for u in units[:AHEAD]]
    for i, (h, block) in enumerate(units):
        p, t = divmod(h, 2)
        lanes = slice(p * LANE, (p + 1) * LANE)
        chunks = queue.pop(0)
        if i + AHEAD < len(units):
            queue.append(start(*units[i + AHEAD]))
        if t == 0 and block == 0:
            v_t = jnp.transpose(v_ref[:, lanes].astype(F32)).astype(BF16)
            halves = []
        if block == 0:
            outs = []
        top = functools.reduce(jnp.maximum, [jnp.max(c, axis=0, keepdims=True) for c in chunks])
        exps = [jnp.exp(c - top) for c in chunks]
        total = functools.reduce(jnp.add, [jnp.sum(c, axis=0, keepdims=True) for c in exps])
        scale = 1.0 / total
        probs = jnp.concatenate([(c * scale).astype(BF16) for c in exps], axis=0)
        outs.append(nn(v_t[t * HD : (t + 1) * HD, : probs.shape[0]], probs))
        lse_ref[lse_base + h, :, block * step : (block + 1) * step] = top + jnp.log(total)
        if block == n_blocks - 1:
            halves.append(jnp.concatenate(outs, axis=1))
            if t == 1:
                o_ref[:, lanes] = jnp.transpose(jnp.concatenate(halves, axis=0)).astype(BF16)


def row_blocks(rows, step, fn):
    def one(i, carry):
        fn(pl.ds(pl.multiple_of(i * step, step), step))
        return carry

    lax.fori_loop(0, rows // step, one, 0)


def rms_rows(h, gain):
    return h * lax.rsqrt(jnp.mean(h * h, axis=-1, keepdims=True) + norm_eps) * gain


def rms_back(h, gain, dn):
    inv = lax.rsqrt(jnp.mean(h * h, axis=-1, keepdims=True) + norm_eps)
    gd = gain * dn
    dh = gd * inv - h * (jnp.mean(gd * h, axis=-1, keepdims=True) * (inv * inv * inv))
    return dh, jnp.sum(dn * h * inv, axis=0, keepdims=True)


ROWS = 128
NB = 768


def col_blocks(width):
    return [slice(i, min(i + NB, width)) for i in range(0, width, NB)]


def self_forward(first, io, *refs):
    if first:
        lens, x_ref, gain_ref, w_ref, table_ref, spread_ref, a_ref, q_ref, k_ref, v_ref, o_ref, lse_ref, bias_ref = refs

        io.wait(x_ref, gain_ref)

        def norm(rows):
            a_ref[rows, :] = rms_rows(x_ref[rows, :].astype(F32), gain_ref[0:1, :]).astype(BF16)

        row_blocks(x_ref.shape[0], ROWS, norm)
        io.flush(a_ref)
    else:
        lens, a_ref, w_ref, table_ref, spread_ref, q_ref, k_ref, v_ref, o_ref, lse_ref, bias_ref = refs
    io.wait(table_ref, spread_ref)
    lines = lax.dot_general(
        table_ref[...], spread_ref[...], (((1,), (1,)), ((), ())), precision=highest,
        preferred_element_type=F32,
    )
    row = lax.broadcasted_iota(jnp.int32, (QB, LANE), 0)
    col = lax.broadcasted_iota(jnp.int32, (QB, LANE), 1)
    for h in range(bias_ref.shape[0]):
        line = jnp.broadcast_to(lines[h : h + 1, :], (QB, QB))
        tile = pltpu.roll(line, 0, 1, stride=1, stride_axis=0)[:, :LANE]
        bias_ref[h] = jnp.where(col - row + LANE < 0, masked_value, tile)
    io.flush(bias_ref)
    io.wait(lens, a_ref, w_ref)
    for i, ref in enumerate((q_ref, k_ref, v_ref)):
        ref[...] = nn(a_ref[...], w_ref[i]).astype(BF16)
        io.flush(ref)
    attend_pairs(q_ref, k_ref, v_ref, o_ref, lse_ref, bias_ref, lens[lax.axis_index("mp")])
    io.flush(o_ref, lse_ref)


def cross_forward(
    io, lens, x_ref, gain_ref, m_ref, oo, on, woo, won, wqo, wqn, wkvo, wkvn, wco, wcn,
    h1_ref, b_ref, qo, qn, ko, kn, vo, vn, oco, ocn, lse_ref, h2_ref, c_ref,
):
    io.wait(lens, m_ref)
    for k, v, w in ((ko, vo, wkvo), (kn, vn, wkvn)):
        io.wait(w)
        k[...] = nn(m_ref[...], w[0]).astype(BF16)
        v[...] = nn(m_ref[...], w[1]).astype(BF16)
        io.flush(k, v)
    io.wait(x_ref, gain_ref, oo, on, woo, won)
    for c in col_blocks(x_ref.shape[1]):
        h1_ref[:, c] = x_ref[:, c].astype(F32) + nn(oo[...], woo[:, c]) + nn(on[...], won[:, c])

    def first(rows):
        b_ref[rows, :] = rms_rows(h1_ref[rows, :], gain_ref[1:2, :]).astype(BF16)

    row_blocks(x_ref.shape[0], ROWS, first)
    io.flush(h1_ref, b_ref)
    io.wait(wqo, wqn)
    qo[...] = nn(b_ref[...], wqo[...]).astype(BF16)
    qn[...] = nn(b_ref[...], wqn[...]).astype(BF16)
    io.flush(qo, qn)
    heads = qo.shape[1] // HD
    length = lens[lax.axis_index("mp")]
    attend_pairs(qo, ko, vo, oco, lse_ref, None, length)
    attend_pairs(qn, kn, vn, ocn, lse_ref, None, length, heads)
    io.flush(oco, ocn, lse_ref)
    io.wait(wco, wcn)
    for c in col_blocks(x_ref.shape[1]):
        h2_ref[:, c] = h1_ref[:, c] + nn(oco[...], wco[:, c]) + nn(ocn[...], wcn[:, c])

    def last(rows):
        c_ref[rows, :] = rms_rows(h2_ref[rows, :], gain_ref[2:3, :]).astype(BF16)

    row_blocks(x_ref.shape[0], ROWS, last)
    io.flush(h2_ref, c_ref)


HB = 512


def hidden_block(c_ref, og_ref, wi, wd, out, at):
    root = np.float32(np.sqrt(2.0 / np.pi))
    width = out.shape[1] // 3
    gate = nn(c_ref[...], wi[0])
    up = nn(c_ref[...], wi[1])
    d_hid = nt(og_ref[...], wd[...])
    sq = gate * gate
    th = jnp.tanh(root * gate * (1.0 + 0.044715 * sq))
    half = 0.5 + 0.5 * th
    gelu = gate * half
    slope = half + 0.5 * gate * (1.0 - th * th) * (root * (1.0 + np.float32(3 * 0.044715) * sq))
    out[:, at : at + HB] = (d_hid * up * slope).astype(BF16)
    out[:, width + at : width + at + HB] = (d_hid * gelu).astype(BF16)
    out[:, 2 * width + at : 2 * width + at + HB] = (gelu * up).astype(BF16)


def ffn_other(io, c_ref, og_ref, *refs):
    weights, out = refs[:-1], refs[-1]
    io.wait(c_ref, og_ref)
    for i in range(0, len(weights), 2):
        io.wait(*weights[i : i + 2])
        hidden_block(c_ref, og_ref, weights[i], weights[i + 1], out, i // 2 * HB)
        for k in range(3):
            io.flush_columns(k * out.shape[1] // 3 + i // 2 * HB, HB, out)


def ffn_own(io, c_ref, og_ref, h2_ref, gain_ref, *refs):
    own, res_ref, g1_ref, w1_ref, dgain, acc = refs[-6:]
    weights, (nbr, win, wdn) = refs[:-9], refs[-9:-6]
    width = own.shape[1] // 3
    io.wait(c_ref, og_ref)
    for i in range(0, len(weights), 2):
        io.wait(*weights[i : i + 2])
        hidden_block(c_ref, og_ref, weights[i], weights[i + 1], own, i // 2 * HB)
    io.flush(own)
    first = True
    for i in range(0, len(weights), 2):
        wi, wd = weights[i], weights[i + 1]
        at = i // 2 * HB
        gate, up, hid = [own[:, k * width + at : k * width + at + HB] for k in range(3)]
        down, out = nt(gate, wi[0]) + nt(up, wi[1]), nn(hid, wd[...])
        g1_ref[...] = down if first else g1_ref[...] + down
        acc[...] = out if first else acc[...] + out
        first = False
    io.wait(nbr, win, wdn)
    g1_ref[...] += nt(nbr[:, 0:width], win[0]) + nt(nbr[:, width : 2 * width], win[1])
    acc[...] += nn(nbr[:, 2 * width :], wdn[...])
    io.wait(h2_ref, gain_ref)
    dgain[...] = jnp.zeros_like(dgain)

    def last(rows):
        h2 = h2_ref[rows, :]
        res_ref[rows, :] = (h2 + acc[rows, :]).astype(BF16)
        dh, dg = rms_back(h2, gain_ref[2:3, :], g1_ref[rows, :])
        g1 = og_ref[rows, :].astype(F32) + dh
        g1_ref[rows, :] = g1
        w1_ref[rows, :] = g1.astype(BF16)
        dgain[...] += dg

    row_blocks(h2_ref.shape[0], ROWS, last)
    io.flush(res_ref, g1_ref, w1_ref, dgain)


def cross_backward(
    io, lens, w1_ref, g1_ref, h1_ref, gain_ref, qo, qn, ko, kn, vo, vn, lse_ref, wco, wcn, wqo, wqn, wkvo, wkvn,
    do_own, dq_nbr, dkv_nbr, g0_ref, w0_ref, dm_ref, dgain, doo, don,
):
    half = qo.shape[1]
    heads = half // HD
    io.wait(lens, w1_ref, wco, wcn)
    doo[...] = nt(w1_ref[...], wco[...]).astype(BF16)
    don[...] = nt(w1_ref[...], wcn[...]).astype(BF16)
    length = lens[lax.axis_index("mp")]
    io.wait(qn, kn, vn, lse_ref)
    grads = ((dq_nbr, 0), (dkv_nbr, 0), (dkv_nbr, half))
    attend_back_pairs(qn, kn, vn, don, grads, lse_ref, None, length, heads)
    io.flush(dq_nbr, dkv_nbr)
    io.wait(qo, ko, vo)
    grads = ((do_own, 0), (do_own, half), (do_own, 2 * half))
    attend_back_pairs(qo, ko, vo, doo, grads, lse_ref, None, length)
    io.flush(do_own)
    io.wait(wqo, wqn, wkvo, wkvn)
    for c in col_blocks(w1_ref.shape[1]):
        g0_ref[:, c] = nt(do_own[:, 0:half], wqo[c, :]) + nt(dq_nbr[...], wqn[c, :])
        dm_ref[:, c] = (
            nt(do_own[:, half : 2 * half], wkvo[0, c, :])
            + nt(do_own[:, 2 * half :], wkvo[1, c, :])
            + nt(dkv_nbr[:, 0:half], wkvn[0, c, :])
            + nt(dkv_nbr[:, half:], wkvn[1, c, :])
        ).astype(BF16)
    io.flush(dm_ref)
    io.wait(g1_ref, h1_ref, gain_ref)
    dgain[...] = jnp.zeros_like(dgain)

    def last(rows):
        dh, dg = rms_back(h1_ref[rows, :], gain_ref[1:2, :], g0_ref[rows, :])
        g0 = g1_ref[rows, :] + dh
        g0_ref[rows, :] = g0
        w0_ref[rows, :] = g0.astype(BF16)
        dgain[...] += dg

    row_blocks(w1_ref.shape[0], ROWS, last)
    io.flush(g0_ref, w0_ref, dgain)


def self_backward(io, lens, w0_ref, *refs):
    parts, outs, do_ref = (refs[:6], refs[6:12]), refs[12:17], refs[17]
    io.wait(lens, w0_ref)
    for i, (wo, q_ref, k_ref, v_ref, lse_ref, bias_ref) in enumerate(parts):
        half = q_ref.shape[1]
        if i == 0:
            mine, diag_ref = outs[:2], outs[2]
            grads = ((outs[0], 0), (outs[1], 0), (outs[1], half))
        else:
            mine, diag_ref = outs[3:4], outs[4]
            grads = [(outs[3], k * half) for k in range(3)]
        io.wait(wo)
        do_ref[...] = nt(w0_ref[...], wo[...]).astype(BF16)
        io.wait(q_ref, k_ref, v_ref, lse_ref, bias_ref)
        attend_back_pairs(
            q_ref, k_ref, v_ref, do_ref, grads, lse_ref, bias_ref, lens[lax.axis_index("mp")], 0, diag_ref
        )
        io.flush(*mine, diag_ref)


def input_backward(io, *refs):
    pairs, (x_ref, gain_ref, g0_ref, out_ref, dgain, acc) = refs[:-6], refs[-6:]
    for i in range(0, len(pairs), 4):
        io.wait(*pairs[i : i + 4])
        term = nt(pairs[i][...], pairs[i + 1][0]) + nt(pairs[i + 2][...], pairs[i + 3][0])
        acc[...] = acc[...] + term if i else term
    io.wait(x_ref, gain_ref, g0_ref)
    dgain[...] = jnp.zeros_like(dgain)

    def some(rows):
        dh, dg = rms_back(x_ref[rows, :].astype(F32), gain_ref[0:1, :], acc[rows, :])
        out_ref[rows, :] = (g0_ref[rows, :] + dh).astype(BF16)
        dgain[...] += dg

    row_blocks(x_ref.shape[0], ROWS, some)
    io.flush(out_ref, dgain)


LINE = (0, 8, 4, 12)
ORDERS = ((1, 2), (2, 1))


def weight_grads(parts, layouts, io, *refs):
    outs, total = refs[-1 - sum(len(v) for v in layouts) : -1], refs[-1]
    rows = outs[0].shape[1]
    device = lax.axis_index("dp")
    first = 0
    for jobs, layout in zip(parts, layouts):
        mine = outs[first : first + len(layout)]
        first += len(layout)
        at = 0
        for lo, ln, ro, rn, width in jobs:
            done = 0
            while done < width:
                step = width if width <= 640 else min(512, width - done)
                src = slice(done, done + step)
                io.wait(refs[lo], refs[ro])
                total[:, 0:step] = tn(refs[lo][...], refs[ro][:, src])
                io.wait(refs[ln], refs[rn])
                total[:, 0:step] += tn(refs[ln][...], refs[rn][:, src])
                dst = slice(at + done, at + done + step)
                for out, nears in zip(mine, layout):
                    for j, mask in enumerate([near ^ far for near in nears for far in LINE]):
                        chunk = lax.bitwise_xor(device, jnp.int32(mask))
                        part = total[pl.ds(pl.multiple_of(chunk * rows, 16), rows), 0:step]
                        out[j, :, dst] = part.astype(out.dtype)
                io.flush_columns(at + done, step, *mine)
                done += step
            at += width


def add_terms(plan, io, *refs):
    at = 0
    outs = refs[-len(plan) :]
    for counts, out in zip(plan, outs):
        start = 0
        for count in counts:
            terms = refs[at : at + count]
            at += count
            io.wait(*terms)
            cols = slice(start, start + terms[0].shape[-1])
            start = cols.stop
            for j in range(out.shape[0]):
                total = terms[0][j]
                for t in terms[1:]:
                    total = total + t[j].astype(F32)
                out[j, :, cols] = total.astype(out.dtype)
        io.flush(out)


def swap_dp(v, mask):
    return lax.ppermute(v, "dp", [(i, i ^ mask) for i in range(16)])


def swap_mp(v):
    return lax.ppermute(v, "mp", [(0, 1), (1, 0)])


def make_grads(parts, depth, n_data, direct=False):
    if n_data != 16:

        def piece(a):
            if not isinstance(a, tuple):
                return a
            value = a[0]
            for axis, start, size in a[1]:
                start = start() if callable(start) else start
                value = lax.dynamic_slice_in_dim(value, start, size, axis)
            return value

        cols = []
        for job in [job for jobs in parts for job in jobs]:
            lo, ln, ro, rn = [piece(a) for a in job]
            cols.append(tn(lo, ro) + tn(ln, rn))
        return lax.psum_scatter(
            jnp.concatenate(cols, axis=1), "dp", scatter_dimension=0, tiled=True
        )
    arrays, keys, plan, shapes, layouts = [], [], [], [], []
    rows = depth // 16
    for jobs in parts:
        spots = []
        for job in jobs:
            place = []
            for a in job:
                key = (id(a[0]),) + a[1:] if isinstance(a, tuple) else id(a)
                if key not in keys:
                    arrays.append(a)
                    keys.append(key)
                place.append(keys.index(key))
            spots.append(tuple(place) + (job[2][1][-1][2],))
        plan.append(tuple(spots))
        width = sum(job[2][1][-1][2] for job in jobs)
        if direct:
            layouts.append(((0,), (1,), (2,), (3,)))
        else:
            one, two = ORDERS[len(layouts)]
            layouts.append(((0, two), (one, one ^ two)))
        for nears in layouts[-1]:
            shapes.append(sds((4 * len(nears), rows, width), F32 if 0 in nears else BF16))
    widest = max(job[4] if job[4] <= 640 else 512 for jobs in plan for job in jobs)
    return dma_call(
        functools.partial(weight_grads, tuple(plan), tuple(layouts)),
        shapes,
        arrays,
        0,
        [pltpu.VMEM((depth, widest), F32)],
        flops=4 * 512 * depth * 1024,
        n_writes=64,
    )


class Reduction:
    def __init__(self, made, n_data, direct=False, near=False):
        self.plain = n_data != 16
        self.made, self.direct = made, direct
        self.far = []
        if not self.plain:
            if direct or near:
                self.keeps, self.done = [made[0]], 2
                self.got = [[swap_dp(v, m) for v, m in zip(made[1:], (1, 2, 3))]]
            else:
                self.keeps, self.done = list(made[::2]), 1
                self.got = [[swap_dp(v, o[0])] for v, o in zip(made[1::2], ORDERS)]

    def near(self, start, size):
        return [[leading(t, start, size) for t in [k] + g] for k, g in zip(self.keeps, self.got)]

    def sends(self):
        rows, widths = self.keeps[0].shape[1], [k.shape[2] for k in self.keeps]
        if self.done == 1:
            parts = self.near(4, 4)
            shapes = [sds((4, rows, w), BF16) for w in widths]
            return [(len(p),) for p in parts], shapes, [t for p in parts for t in p]
        if self.direct:
            spots = ((1, 1), (2, 1), (3, 1))
        else:
            spots = ((2, 2),) if self.done == 2 else ((1, 1),)
        plan, shapes, terms = [], [], []
        for start, size in spots:
            parts, at = self.near(start, size), 0
            for part, w in zip(parts, widths):
                part += [leading(columns(t, at, w), start, size) for t in self.far]
                at += w
            plan.append(tuple(len(p) for p in parts))
            shapes.append(sds((size, rows, sum(widths)), BF16))
            terms += [t for part in parts for t in part]
        return plan, shapes, terms

    def sent(self, sends):
        if self.done == 1:
            for got, send, order in zip(self.got, sends, ORDERS):
                got.append(swap_dp(send, order[1]))
        elif self.direct:
            self.far = [swap_dp(v, m) for v, m in zip(sends, LINE[1:])]
        else:
            self.far.append(swap_dp(sends[0], 4 if self.done == 2 else 8))
        self.done += 1

    def terms(self):
        if self.plain:
            return [[self.made[None]]]
        parts, at = self.near(0, 1), 0
        for part, k in zip(parts, self.keeps):
            part += [leading(columns(t, at, k.shape[2]), 0, 1) for t in self.far]
            at += k.shape[2]
        return parts


def exchange(*steps, others=()):
    steps = [r for r in steps if not r.plain]
    if not steps:
        return []
    made = [r.sends() for r in steps]
    plan = [p for m in made for p in m[0]]
    shapes = [p for m in made for p in m[1]]
    terms = [p for m in made for p in m[2]]
    if others:
        terms[0] = (after(terms[0][0], *others), terms[0][1])
    sends = dma_call(functools.partial(add_terms, tuple(plan)), shapes, terms)
    at = 0
    for r, m in zip(steps, made):
        r.sent(sends[at : at + len(m[0])])
        at += len(m[0])
    return list(sends)


def squares_of(mats, first, all_ref, cols_ref, row_sums):
    rows = all_ref.shape[0]
    lane = lax.broadcasted_iota(jnp.int32, (rows, LANE), 1)
    for i, (start, width) in enumerate(mats):
        part = all_ref[:, start : start + width]
        sq = part * part
        cols_ref[:, start : start + width] = jnp.sum(sq, axis=0, keepdims=True)
        row_sums = row_sums + jnp.where(lane == first + i, jnp.sum(sq, axis=1, keepdims=True), 0.0)
    return row_sums


def end_sums(counts, io, refs, all_ref):
    start = at = 0
    for count in counts:
        terms = refs[at : at + count]
        io.wait(*terms)
        total = terms[0][0]
        for t in terms[1:]:
            total = total + t[0].astype(F32)
        all_ref[:, start : start + total.shape[1]] = total
        at += count
        start += total.shape[1]


def early_statistics(counts, mats, io, *refs):
    all_ref, cols_ref, rows_ref = refs[-3:]
    end_sums(counts, io, refs, all_ref)
    rows_ref[...] = squares_of(mats, 0, all_ref, cols_ref, jnp.zeros_like(rows_ref))
    io.flush(all_ref, cols_ref, rows_ref)


def statistics(counts, mats, first, io, *refs):
    all_ref, pack_ref, cols_ref = refs[-3:]
    rows_ref, spread = refs[-10], refs[-4]
    gains, diags = refs[-9:-6], refs[-6:-4]
    io.wait(rows_ref, *gains, *diags, spread)
    pack_ref[...] = jnp.zeros_like(pack_ref)
    for i, gain in enumerate(gains):
        pack_ref[i : i + 1, :] = gain[...]
    for i, diag in enumerate(diags):
        heads = diag.shape[0]
        lines = jnp.concatenate([diag[h] for h in range(heads)], axis=0)
        pack_ref[8 : 8 + heads, i * LANE : i * LANE + BUCKETS] = lax.dot_general(
            lines, spread[...], (((1,), (0,)), ((), ())), precision=highest,
            preferred_element_type=F32,
        )
    end_sums(counts, io, refs, all_ref)
    rows = all_ref.shape[0]
    pack_ref[16 : 16 + rows, 0:LANE] = squares_of(mats, first, all_ref, cols_ref, rows_ref[...])
    io.flush(all_ref, pack_ref, cols_ref)


def merge_kernel(io, own_ref, got_ref, early_ref, late_ref, out_ref, rows_ref):
    io.wait(own_ref, got_ref, early_ref, late_ref)
    rows = rows_ref.shape[0]
    n_early, depth = early_ref.shape[1], own_ref.shape[1]
    n_all = n_early + late_ref.shape[1]
    full = own_ref[16 : 16 + rows, 0:LANE] + got_ref[16 : 16 + rows, 0:LANE]
    rows_ref[...] = full
    out_ref[:, 0:n_early] = early_ref[...]
    out_ref[:, n_early:n_all] = late_ref[...]
    at = n_all
    for i in range(3):
        out_ref[:, at : at + depth] = own_ref[i : i + 1, :] + got_ref[i : i + 1, :]
        at += depth
    out_ref[:, at : at + LANE] = jnp.sum(full, axis=0, keepdims=True)
    for side in range(2):
        mine = own_ref[8:16, side * LANE : (side + 1) * LANE]
        theirs = got_ref[8:16, (1 - side) * LANE : (2 - side) * LANE]
        both = mine + theirs
        for h in range(8):
            at += LANE
            out_ref[:, at : at + LANE] = both[h : h + 1]
    io.flush(out_ref, rows_ref)


def turn(v):
    rows = v.shape[0]
    if rows < LANE:
        v = jnp.concatenate([v, jnp.zeros((LANE - rows, v.shape[1]), v.dtype)], axis=0)
    return jnp.transpose(v)[:, :rows]


def update_kernel(plan, n_terms, io, *refs):
    terms = refs[:n_terms]
    rows_ref, early_ref, late_ref = refs[n_terms : n_terms + 3]
    weights = refs[n_terms + 3 : n_terms + 3 + len(plan)]
    outs = refs[n_terms + 3 + len(plan) :]
    io.wait(*terms)
    line = functools.reduce(jnp.add, [p[...] for p in terms])
    n_early = early_ref.shape[1]
    n_all = n_early + late_ref.shape[1]
    gain_ref, table_ref, norm_ref = outs[0], outs[1], outs[-1]
    depth = gain_ref.shape[1]
    gains_at, totals_at = n_all, n_all + 3 * depth
    tables_at = totals_at + LANE
    for i in range(3):
        gain_ref[i : i + 1, :] = line[:, gains_at + i * depth : gains_at + (i + 1) * depth]
    for h in range(table_ref.shape[0]):
        at = tables_at + h * LANE
        table_ref[h : h + 1, :] = line[:, at : at + BUCKETS]
    totals = line[:, totals_at:tables_at]
    gains, tables = line[:, gains_at:totals_at], line[:, tables_at:]
    squares = (
        jnp.sum(gains * gains, axis=1, keepdims=True)
        + jnp.sum(tables * tables, axis=1, keepdims=True)
        + jnp.sum(totals, axis=1, keepdims=True)
    )
    norm_ref[...] = jnp.sqrt(squares)
    io.flush(gain_ref, table_ref, norm_ref)
    io.wait(rows_ref, early_ref, late_ref)
    row_sums = rows_ref[...]
    row_lines = turn(row_sums)
    at = 2
    for (natural, members), weight in zip(plan, weights):
        new_ref, row_out, col_out = outs[at : at + 3]
        at += 3
        io.wait(weight)
        for k, (i, start, width) in enumerate(members):
            size = 2 * width
            by_row = row_sums[:, i : i + 1] / size + stat_eps
            by_col = line[:, start : start + width] / depth + stat_eps
            mean = totals[:, i : i + 1] / (size * depth) + stat_eps
            if start < n_early:
                grad = early_ref[:, start : start + width]
            else:
                grad = late_ref[:, start - n_early : start - n_early + width]
            change = (
                learn_rate
                * grad
                * lax.rsqrt(by_row * by_col / mean)
            )
            row_line = row_lines[i : i + 1, :] / size + stat_eps
            new_ref[k] = weight[k].astype(F32) - change
            lines = (row_line, by_col) if natural else (by_col, row_line)
            for out, value in zip((row_out, col_out), lines):
                if len(out.shape) == 1:
                    out[...] = value.reshape(out.shape)
                else:
                    out[k : k + 1, :] = value
        io.flush(new_ref, row_out, col_out)


def after(value, *others):
    return lax.optimization_barrier((value,) + others)[0]


def body(
    tokens,
    memory,
    out_grad,
    tgt_lens,
    mem_lens,
    norm_gains,
    rel_table,
    self_qkv,
    self_out,
    cross_q,
    cross_kv,
    cross_out,
    ffn_in,
    ffn_out,
):
    n_data = lax.axis_size("dp")
    mp = lax.axis_index("mp")
    dp = lax.axis_index("dp")
    rows = tokens.shape[0]
    depth = tokens.shape[1]
    heads = rel_table.shape[1]
    half = heads * HD
    width = ffn_out.shape[0]
    chunk = depth // n_data
    qkv_n = swap_mp(self_qkv)
    table = rel_table.T
    table_n = swap_mp(table)
    so_n = swap_mp(self_out)
    ckv_n = swap_mp(cross_kv)
    cq_n = swap_mp(cross_q)

    dist = np.arange(QB)
    line_dist = np.where(dist < LANE, dist + LANE, dist - LANE)
    spread = jnp.asarray((bucket_of(line_dist)[:, None] == np.arange(BUCKETS)).astype(np.float32))
    gather = jnp.asarray((bucket_of(dist)[:, None] == np.arange(BUCKETS)).astype(np.float32))

    attn_flops = 4 * rows * rows * HD * heads
    bias_shape = sds((heads, QB, LANE), F32)
    act = sds((rows, half), BF16)
    wide = sds((rows, depth), BF16)
    full = sds((rows, depth), F32)
    gain_row = sds((1, depth), F32)
    lse = sds((heads, 1, rows), F32)
    lse2 = sds((2 * heads, 1, rows), F32)
    a, qs_o, ks_o, vs_o, os_o, lses_o, bias_o = dma_call(
        functools.partial(self_forward, True),
        [wide, act, act, act, act, lse, bias_shape],
        [tgt_lens, tokens, norm_gains, self_qkv, table, spread],
        1,
        flops=6 * rows * depth * half + attn_flops,
    )
    a, qkv_n, table_n, so_n, cq_n, ckv_n, cross_out_b, ffn_in_b, ffn_out_b, out_grad_b = (
        lax.optimization_barrier(
            (a, qkv_n, table_n, so_n, cq_n, ckv_n, cross_out, ffn_in, ffn_out, out_grad)
        )
    )
    co_n = swap_mp(cross_out_b)
    fi_n = swap_mp(ffn_in_b)
    fo_n = swap_mp(ffn_out_b)
    og_n = swap_mp(out_grad_b)
    a_n = swap_mp(a)
    qs_n, ks_n, vs_n, os_n, lses_n, bias_n = dma_call(
        functools.partial(self_forward, False),
        [act, act, act, act, lse, bias_shape],
        [tgt_lens, a, qkv_n, table_n, spread],
        1,
        flops=6 * rows * depth * half + attn_flops,
    )
    mem_own = leading(memory, lambda: pl.multiple_of(lax.axis_index("mp") * rows, rows), rows)
    mem_nbr = leading(memory, lambda: pl.multiple_of((1 - lax.axis_index("mp")) * rows, rows), rows)
    os_x = swap_mp(os_n)
    h1, b, qc_o, qc_n, kc_o, kc_n, vc_o, vc_n, oc_o, oc_n, lsec, h2, c = dma_call(
        cross_forward,
        [full, wide, act, act, act, act, act, act, act, act, lse2, full, wide],
        [mem_lens, tokens, norm_gains, mem_own, os_o, os_n, self_out, so_n, cross_q, cq_n, cross_kv, ckv_n, cross_out, co_n],
        1,
        flops=20 * rows * depth * half + 2 * attn_flops,
    )
    c, os_x, a_n = lax.optimization_barrier((c, os_x, a_n))
    b_n = swap_mp(b)
    oc_x = swap_mp(oc_n)
    c_n = swap_mp(c)
    hid = sds((rows, 3 * width), BF16)
    def hidden_weights(wi, wd):
        return [v for i in range(0, width, HB) for v in (columns(wi, i, HB), leading(wd, i, HB))]

    f_nbr = dma_call(
        ffn_other,
        [hid],
        [c, out_grad] + hidden_weights(fi_n, fo_n),
        flops=6 * rows * depth * width,
        n_writes=3 * width // HB,
    )[0]
    f_x = swap_mp(f_nbr)
    f_own, result, g1, w1, gain_c = dma_call(
        ffn_own,
        [hid, wide, full, wide, gain_row],
        [c, out_grad, h2, norm_gains] + hidden_weights(ffn_in, ffn_out) + [f_nbr, fi_n, fo_n],
        0,
        [pltpu.VMEM((rows, depth), F32)],
        flops=18 * rows * depth * width,
    )
    w1_n = swap_mp(w1)
    def pair(own, nbr, start, size):
        return columns(own, start, size), columns(nbr, start, size)

    w1, f_own = lax.optimization_barrier((w1, f_own))
    early_down = width // 2
    left = (2 * width + early_down) // 2
    ffn_made = make_grads(
        (
            ((c, c_n) + pair(f_own, f_x, 0, left),),
            (
                (c, c_n) + pair(f_own, f_x, left, 2 * width - left),
                (out_grad, og_n) + pair(f_own, f_x, 2 * width, early_down),
            ),
        ),
        depth,
        n_data,
    )
    w1_b = after(w1, w1_n, b_n, oc_x, *jax.tree.leaves(ffn_made))
    ffn_sum = Reduction(ffn_made, n_data)
    c_own, cq_nbr, ckv_nbr, g0, w0, d_mem, gain_b = dma_call(
        cross_backward,
        [sds((rows, 3 * half), BF16), act, sds((rows, 2 * half), BF16), full, wide, wide, gain_row],
        [mem_lens, w1_b, g1, h1, norm_gains, qc_o, qc_n, kc_o, kc_n, vc_o, vc_n, lsec, cross_out, co_n, cross_q, cq_n, cross_kv, ckv_n],
        1,
        [pltpu.VMEM((rows, half), BF16), pltpu.VMEM((rows, half), BF16)],
        flops=16 * rows * depth * half + 5 * attn_flops,
    )
    cq_x, ckv_x = swap_mp(cq_nbr), swap_mp(ckv_nbr)
    w0_n = swap_mp(w0)
    diag = sds((heads, 1, QB), F32)

    sent = exchange(ffn_sum, others=(c_own,))
    if sent:
        w0, w0_n, cq_x, ckv_x = lax.optimization_barrier((w0, w0_n, cq_x, ckv_x, *sent))[:4]
    split = 2 * LANE
    split = 2 * LANE
    cross_made = make_grads(
        (
            (
                (out_grad, og_n) + pair(f_own, f_x, 2 * width + early_down, width - early_down),
                (w1, w1_n) + pair(oc_o, oc_x, 0, half),
                (w0, w0_n) + pair(os_o, os_x, 0, split),
            ),
            (
                (w0, w0_n) + pair(os_o, os_x, split, half - split),
                (b, b_n, columns(c_own, 0, half), columns(cq_x, 0, half)),
                (mem_own, mem_nbr, columns(c_own, half, 2 * half), columns(ckv_x, 0, 2 * half)),
            ),
        ),
        depth,
        n_data,
    )
    cross_sum = Reduction(cross_made, n_data)
    sent = exchange(ffn_sum, others=jax.tree.leaves(cross_made))
    w0_b = after(w0, *sent, *jax.tree.leaves(cross_made))
    sq_nbr, skv_nbr, diag_n, s_own, diag_o = dma_call(
        self_backward,
        [act, sds((rows, 2 * half), BF16), diag, sds((rows, 3 * half), BF16), diag],
        [tgt_lens, w0_b, so_n, qs_n, ks_n, vs_n, lses_n, bias_n]
        + [self_out, qs_o, ks_o, vs_o, lses_o, bias_o],
        1,
        [pltpu.VMEM((rows, half), BF16)],
        flops=4 * rows * depth * half + 6 * attn_flops,
    )
    sq_x, skv_x = swap_mp(sq_nbr), swap_mp(skv_nbr)
    grad_in, gain_a = dma_call(
        input_backward,
        [wide, gain_row],
        [
            v
            for i in range(3)
            for d, at, w in (
                (s_own, i, self_qkv),
                (sq_nbr if i == 0 else skv_nbr, max(i - 1, 0), qkv_n),
            )
            for v in (columns(d, at * half, half), leading(w, i, 1))
        ]
        + [tokens, norm_gains, g0],
        0,
        [pltpu.VMEM((rows, depth), F32)],
        flops=12 * rows * depth * half,
    )
    sent = exchange(ffn_sum, cross_sum, others=(grad_in,))
    s_own, sq_x, skv_x = lax.optimization_barrier((s_own, sq_x, skv_x, grad_in, *sent))[:3]
    self_made = make_grads(
        (
            (
                (a, a_n, columns(s_own, 0, half), columns(sq_x, 0, half)),
                (a, a_n, columns(s_own, half, 2 * half), columns(skv_x, 0, 2 * half)),
            ),
        ),
        depth,
        n_data,
        direct=True,
    )
    self_sum = Reduction(self_made, n_data, direct=True)
    exchange(cross_sum, others=jax.tree.leaves(self_made) + ffn_sum.far)

    sizes = [width, width, width] + [half] * 8
    starts = [int(v) for v in np.cumsum([0] + sizes[:-1])]
    mats = tuple(zip(starts, sizes))
    n_all = sum(sizes)
    plan = (
        (True, (8, 9, 10)),
        (False, (4,)),
        (True, (5,)),
        (True, (6, 7)),
        (False, (3,)),
        (True, (0, 1)),
        (False, (2,)),
    )
    plan = tuple((n, tuple((i, starts[i], sizes[i]) for i in m)) for n, m in plan)
    weights = (self_qkv, self_out, cross_q, cross_kv, cross_out, ffn_in, ffn_out)
    slices, shapes = [], [sds((3, depth), F32), sds((heads, BUCKETS), F32)]
    for (natural, members), weight in zip(plan, weights):
        count, size = len(members), members[0][2]
        if natural:
            stacked = weight.reshape((count,) + weight.shape[-2:])
            part = cut(stacked, 1, lambda: pl.multiple_of(lax.axis_index("dp") * chunk, chunk), chunk)
            if n_data != 16:
                part = lax.dynamic_slice_in_dim(stacked, dp * chunk, chunk, 1)
        else:
            part = lax.dynamic_slice_in_dim(weight, dp * chunk, chunk, 1).T[None]
        slices.append(part)
        line_sizes = (chunk, size) if natural else (size, chunk)
        shapes += [sds((count, chunk, size), F32)]
        shapes += [sds((n,) if weight.ndim == 2 else (count, n), F32) for n in line_sizes]
    shapes.append(sds((1, 1), F32))
    exchange(cross_sum, others=[v for v in slices if not isinstance(v, tuple)])
    sent = exchange(self_sum)
    n_early = starts[8]
    early = ffn_sum.terms() + cross_sum.terms()
    if sent:
        early[0][0] = (after(early[0][0][0], *sent), early[0][0][1])
    grads, cols, row_parts = dma_call(
        functools.partial(early_statistics, tuple(len(t) for t in early), mats[:8]),
        [sds((chunk, n_early), F32), sds((1, n_early), F32), sds((chunk, LANE), F32)],
        [t for part in early for t in part],
    )
    late = self_sum.terms()
    pack_rows = -(-(16 + chunk) // 8) * 8
    late_grads, pack, late_cols = dma_call(
        functools.partial(statistics, tuple(len(t) for t in late), tuple((a - n_early, b) for a, b in mats[8:]), 8),
        [sds((chunk, n_all - n_early), F32), sds((pack_rows, depth), F32), sds((1, n_all - n_early), F32)],
        [t for part in late for t in part] + [row_parts, gain_a, gain_b, gain_c, diag_o, diag_n, gather],
    )
    line, row_sums = dma_call(
        merge_kernel,
        [sds((1, n_all + 3 * depth + 17 * LANE), F32), sds((chunk, LANE), F32)],
        [pack, swap_mp(pack), cols, late_cols],
    )
    if n_data == 16:
        terms = [line]
        for group in ((1, 2, 3), (4, 8, 12)):
            if len(terms) > 1:
                terms = [functools.reduce(jnp.add, terms)]
            terms = terms + [swap_dp(terms[0], m) for m in group]
    else:
        terms = [lax.psum(line, "dp")]

    done = dma_call(
        functools.partial(update_kernel, plan, len(terms)),
        shapes,
        terms + [row_sums, grads, late_grads] + slices,
    )
    finals = [result, grad_in, d_mem, done[0], done[1].T]
    for i, ((natural, _), weight) in enumerate(zip(plan, weights)):
        new, row, col = done[2 + 3 * i : 5 + 3 * i]
        if weight.ndim == 2:
            new = new[0] if natural else new[0].T
        finals += [new, row, col]
    return tuple(finals + [done[-1][0, 0]])


def solution(mesh):
    placed = (
        P(("dp", "mp"), None),
        P("dp", None),
        P(("dp", "mp"), None),
        P("dp"),
        P("dp"),
        P(),
        P(None, "mp"),
        P(None, None, "mp"),
        P("mp", None),
        P(None, "mp"),
        P(None, None, "mp"),
        P("mp", None),
        P(None, None, "mp"),
        P("mp", None),
    )
    return jax.shard_map(
        body,
        mesh=mesh,
        in_specs=placed,
        out_specs=(
            P(("dp", "mp"), None),
            P(("dp", "mp"), None),
            P(("dp", "mp"), None),
            P(),
            P(None, "mp"),
            P(None, "dp", "mp"),
            P(None, "dp"),
            P(None, "mp"),
            P("mp", "dp"),
            P("mp"),
            P("dp"),
            P("dp", "mp"),
            P("dp"),
            P("mp"),
            P(None, "dp", "mp"),
            P(None, "dp"),
            P(None, "mp"),
            P("mp", "dp"),
            P("mp"),
            P("dp"),
            P(None, "dp", "mp"),
            P(None, "dp"),
            P(None, "mp"),
            P("mp", "dp"),
            P("mp"),
            P("dp"),
            P(),
        ),
        check_vma=False,
    )
```

```python
import functools

import jax
import jax.numpy as jnp
import numpy as np
from jax import lax
from jax.experimental import pallas as pl
from jax.experimental.pallas import tpu as pltpu
from jax.sharding import PartitionSpec as P

BUCKETS = 32
MAX_DIST = 128
HD = 64
LANE = 128
VMEM_BYTES = 64 * 1024 * 1024 - 64 * 1024
QB = 256
AHEAD = 3
norm_eps = 1e-06
stat_eps = 1e-30
masked_value = -1e30
learn_rate = 0.04
highest = lax.Precision.HIGHEST
F32 = jnp.float32
BF16 = jnp.bfloat16
VMEM = pl.BlockSpec(memory_space=pltpu.VMEM)
SMEM = pl.BlockSpec(memory_space=pltpu.SMEM)


def bucket_of(dist):
    exact_span = BUCKETS // 2
    dist = np.maximum(dist, 0)
    log_ratio = np.log(np.maximum(dist, 1) / exact_span) / np.log(MAX_DIST / exact_span)
    far = np.minimum(
        exact_span + np.floor(log_ratio * (BUCKETS - exact_span)).astype(np.int64), BUCKETS - 1
    )
    return np.where(dist < exact_span, dist, far).astype(np.int32)


def nn(a, b):
    return lax.dot_general(a, b, (((1,), (0,)), ((), ())), preferred_element_type=F32)


def nt(a, b):
    return lax.dot_general(a, b, (((1,), (1,)), ((), ())), preferred_element_type=F32)


def tn(a, b):
    return lax.dot_general(a, b, (((0,), (0,)), ((), ())), preferred_element_type=F32)


class Copies:
    def __init__(self, pairs_in, pairs_out, sem_in, sem_out):
        self.reads = [
            (dst, pltpu.make_async_copy(src, dst, sem_in.at[i]))
            for i, (src, dst) in enumerate(pairs_in)
        ]
        self.writes = [
            (src, pltpu.make_async_copy(src, dst, sem_out.at[i]))
            for i, (src, dst) in enumerate(pairs_out)
        ]
        self.pairs_out, self.sem_out = pairs_out, sem_out
        self.pending, self.begun = list(self.reads), []
        for _, copy in self.reads:
            copy.start()

    def wait(self, *refs):
        for ref in refs:
            for entry in self.pending:
                if entry[0] is ref:
                    entry[1].wait()
                    self.pending = [e for e in self.pending if e is not entry]
                    break

    def flush(self, *refs):
        for ref in refs:
            for src, copy in self.writes:
                if src is ref:
                    copy.start()
                    self.begun.append(copy)

    def flush_columns(self, start, size, *refs):
        cols = pl.ds(start, size)
        for src, dst in self.pairs_out:
            if not any(src is r for r in refs):
                continue
            copy = pltpu.make_async_copy(
                src.at[..., cols], dst.at[..., cols], self.sem_out.at[len(self.begun)]
            )
            copy.start()
            self.begun.append(copy)

    def close(self):
        assert not self.pending and len(self.begun) >= len(self.writes)
        for copy in self.begun:
            copy.wait()


def columns(array, start, size):
    return cut(array, -1, start, size)


def leading(array, start, size):
    return cut(array, 0, start, size)


def cut(array, axis, start, size):
    array, cuts = array if isinstance(array, tuple) else (array, ())
    return (array, cuts + ((axis % array.ndim, start, size),))


def dma_call(kernel, outs, args, n_smem=0, scratch=(), flops=0, n_writes=0):
    args = [a if isinstance(a, tuple) else (a, ()) for a in args]
    arrays = [a[0] for a in args]
    n_in, n_out = len(arrays), len(outs)
    held = []
    for i, (a, cuts) in enumerate(args):
        shape = list(a.shape)
        for axis, _, size in cuts:
            shape[axis] = size
        shape = tuple(shape)
        held.append((pltpu.SMEM if i < n_smem else pltpu.VMEM)(shape, a.dtype))
    held += [pltpu.VMEM(o.shape, o.dtype) for o in outs]

    def part(ref, arg):
        index = [slice(None)] * arg[0].ndim
        for axis, start, size in arg[1]:
            index[axis] = pl.ds(start() if callable(start) else start, size)
        return ref.at[tuple(index)] if arg[1] else ref

    def run(*refs):
        given, made = refs[:n_in], refs[n_in : n_in + n_out]
        local = refs[n_in + n_out : 2 * (n_in + n_out)]
        rest, (sem_in, sem_out) = refs[2 * (n_in + n_out) : -2], refs[-2:]
        sources = [part(r, a) for r, a in zip(given, args)]
        io = Copies(
            list(zip(sources, local[:n_in])), list(zip(local[n_in:], made)), sem_in, sem_out
        )
        kernel(io, *local, *rest)
        io.close()

    moved = sum(h.shape[0] * int(np.prod(h.shape[1:])) * np.dtype(h.dtype).itemsize for h in held)
    return pl.pallas_call(
        run,
        out_shape=list(outs),
        in_specs=[pl.BlockSpec(memory_space=pltpu.HBM)] * n_in,
        out_specs=[pl.BlockSpec(memory_space=pltpu.HBM)] * n_out,
        scratch_shapes=held
        + list(scratch)
        + [pltpu.SemaphoreType.DMA((n_in,)), pltpu.SemaphoreType.DMA((max(n_out, n_writes),))],
        compiler_params=pltpu.CompilerParams(vmem_limit_bytes=VMEM_BYTES),
        cost_estimate=pl.CostEstimate(flops=flops, bytes_accessed=moved, transcendentals=0),
    )(*arrays)


def sds(shape, dtype):
    return jax.ShapeDtypeStruct(shape, dtype)


def head_masks(dtype):
    lane = lax.broadcasted_iota(jnp.int32, (1, LANE), 1)
    return [(lane < HD).astype(dtype), (lane >= HD).astype(dtype)]


def bias_chunks(bias_ref, head, first, count, blocks):
    near = bias_ref[head, 0:LANE, :]
    diag = bias_ref[head, LANE : 2 * LANE, :]
    const = jnp.broadcast_to(bias_ref[head, 0:1, :], (LANE, LANE))
    none = jnp.full((LANE, LANE), masked_value, F32)

    def tile(offset):
        return none if offset < 0 else diag if offset == 0 else near if offset == 1 else const

    return [
        jnp.concatenate([tile(first + i - j) for i in range(blocks)], axis=1)
        for j in range(count)
    ]


def score_chunks(keys_masked, queries, bias_ref, head, first, count, length):
    width = queries.shape[0]
    scores = nt(keys_masked[: count * LANE], queries)
    row = lax.broadcasted_iota(jnp.int32, (LANE, width), 0)
    chunks = []
    if bias_ref is not None:
        bias = bias_chunks(bias_ref, head, first, count, width // LANE)
    for j in range(count):
        part = scores[j * LANE : (j + 1) * LANE]
        if bias_ref is not None:
            part = part + bias[j]
        chunks.append(jnp.where(row < length - j * LANE, part, masked_value))
    return chunks


def attend_back_pairs(
    q_ref, k_ref, v_ref, do_ref, grads, lse_ref, bias_ref, length, lse_base=0, diag_ref=None
):
    rows, width = q_ref.shape
    keys = k_ref.shape[0]
    masks = head_masks(BF16)
    lane_id = lax.broadcasted_iota(jnp.int32, (1, QB), 1)
    step = QB
    n_blocks = rows // step
    units = [(h, b) for h in range(width // HD) for b in range(n_blocks)]
    kept = {}

    def pair_values(p):
        if p not in kept:
            lanes = slice(p * LANE, (p + 1) * LANE)
            k_pair, v_pair = k_ref[:, lanes], v_ref[:, lanes]
            kept[p] = (
                [k_pair * m for m in masks],
                [v_pair * m for m in masks],
                jnp.transpose(k_pair.astype(F32)).astype(BF16),
            )
        return kept[p]

    def start(h, block):
        p, t = divmod(h, 2)
        lanes = slice(p * LANE, (p + 1) * LANE)
        count = (block + 1) * step // LANE if bias_ref is not None else keys // LANE
        k_m, v_m, _ = pair_values(p)
        at = slice(block * step, (block + 1) * step)
        q_blk, do_blk = q_ref[at, lanes], do_ref[at, lanes]
        chunks = score_chunks(k_m[t], q_blk, bias_ref, h, block * step // LANE, count, length)
        d_probs = nt(v_m[t][: count * LANE], do_blk)
        return chunks, [d_probs[j * LANE : (j + 1) * LANE] for j in range(count)]

    ahead = start(*units[0])
    sums = {}
    for i, (h, block) in enumerate(units):
        p, t = divmod(h, 2)
        lanes = slice(p * LANE, (p + 1) * LANE)
        at = slice(block * step, (block + 1) * step)
        chunks, d_probs = ahead
        if i + 1 < len(units):
            ahead = start(*units[i + 1])
        count = len(chunks)
        lse = lse_ref[lse_base + h, :, at]
        probs = [jnp.exp(c - lse) for c in chunks]
        dot = functools.reduce(
            jnp.add, [jnp.sum(a * b, axis=0, keepdims=True) for a, b in zip(probs, d_probs)]
        )
        d_scores = [(a * (b - dot)).astype(BF16) for a, b in zip(probs, d_probs)]
        if t == 0 and block == 0:
            sums = dict(
                dv=[None] * (keys // LANE), dk=[None] * (keys // LANE), dq=[[], []]
            )
        if block == 0:
            near_sum = jnp.zeros((LANE, LANE), F32)
            diag_sum = jnp.zeros((LANE, LANE), F32)
            far_sum = jnp.zeros((1, LANE), F32)
        if diag_ref is not None:
            for j in range(count):
                wide = d_scores[j].astype(F32)
                for c in range(step // LANE):
                    tile = wide[:, c * LANE : (c + 1) * LANE]
                    offset = block * step // LANE + c - j
                    if offset == 0:
                        diag_sum = diag_sum + tile
                    elif offset == 1:
                        near_sum = near_sum + tile
                    elif offset > 1:
                        far_sum = far_sum + jnp.sum(tile, axis=0, keepdims=True)
        d_all = jnp.concatenate(d_scores, axis=0)
        p_all = jnp.concatenate([a.astype(BF16) for a in probs], axis=0)
        dv_new = nn(p_all, do_ref[at, lanes] * masks[t])
        dk_new = nn(d_all, q_ref[at, lanes] * masks[t])
        for name, new in (("dv", dv_new), ("dk", dk_new)):
            for j in range(count):
                part = new[j * LANE : (j + 1) * LANE]
                old = sums[name][j]
                sums[name][j] = part if old is None else old + part
        k_t = pair_values(p)[2]
        sums["dq"][t].append(nn(k_t[t * HD : (t + 1) * HD, : count * LANE], d_all))
        if diag_ref is not None and block == n_blocks - 1:
            both = jnp.concatenate([near_sum, diag_sum], axis=0)
            both = jnp.concatenate([both, jnp.zeros_like(both)], axis=1)
            acc = jnp.zeros((8, QB), F32)
            for g in range(QB // 8):
                piece = both[8 * g : 8 * g + 8]
                turned = (LANE - 8 * g) % QB
                acc = acc + (pltpu.roll(piece, turned, 1) if turned else piece)
            line = acc[0:1]
            for g in range(1, 8):
                line = line + pltpu.roll(acc, QB - g, 1)[g : g + 1]
            far_total = jnp.sum(far_sum, axis=1, keepdims=True)
            diag_ref[h] = line + jnp.where(lane_id == QB - 1, far_total, 0.0)
        if t == 1 and block == n_blocks - 1:
            dq_t = jnp.concatenate([jnp.concatenate(v, axis=1) for v in sums["dq"]], axis=0)
            done = (
                jnp.transpose(dq_t),
                jnp.concatenate(sums["dk"], axis=0),
                jnp.concatenate(sums["dv"], axis=0),
            )
            for (ref, first), value in zip(grads, done):
                ref[:, first + p * LANE : first + (p + 1) * LANE] = value.astype(BF16)


def attend_pairs(q_ref, k_ref, v_ref, o_ref, lse_ref, bias_ref, length, lse_base=0):
    rows, width = q_ref.shape
    keys = k_ref.shape[0]
    masks = head_masks(BF16)
    step = QB
    n_blocks = rows // step
    units = [(h, b) for h in range(width // HD) for b in range(n_blocks)]

    def start(h, block):
        p, t = divmod(h, 2)
        lanes = slice(p * LANE, (p + 1) * LANE)
        k_m = k_ref[:, lanes] * masks[t]
        count = (block + 1) * step // LANE if bias_ref is not None else keys // LANE
        q_blk = q_ref[block * step : (block + 1) * step, lanes]
        return score_chunks(k_m, q_blk, bias_ref, h, block * step // LANE, count, length)

    queue = [start(*u) for u in units[:AHEAD]]
    for i, (h, block) in enumerate(units):
        p, t = divmod(h, 2)
        lanes = slice(p * LANE, (p + 1) * LANE)
        chunks = queue.pop(0)
        if i + AHEAD < len(units):
            queue.append(start(*units[i + AHEAD]))
        if t == 0 and block == 0:
            v_t = jnp.transpose(v_ref[:, lanes].astype(F32)).astype(BF16)
            halves = []
        if block == 0:
            outs = []
        top = functools.reduce(jnp.maximum, [jnp.max(c, axis=0, keepdims=True) for c in chunks])
        exps = [jnp.exp(c - top) for c in chunks]
        total = functools.reduce(jnp.add, [jnp.sum(c, axis=0, keepdims=True) for c in exps])
        scale = 1.0 / total
        probs = jnp.concatenate([(c * scale).astype(BF16) for c in exps], axis=0)
        outs.append(nn(v_t[t * HD : (t + 1) * HD, : probs.shape[0]], probs))
        lse_ref[lse_base + h, :, block * step : (block + 1) * step] = top + jnp.log(total)
        if block == n_blocks - 1:
            halves.append(jnp.concatenate(outs, axis=1))
            if t == 1:
                o_ref[:, lanes] = jnp.transpose(jnp.concatenate(halves, axis=0)).astype(BF16)


def row_blocks(rows, step, fn):
    def one(i, carry):
        fn(pl.ds(pl.multiple_of(i * step, step), step))
        return carry

    lax.fori_loop(0, rows // step, one, 0)


def rms_rows(h, gain):
    return h * lax.rsqrt(jnp.mean(h * h, axis=-1, keepdims=True) + norm_eps) * gain


def rms_back(h, gain, dn):
    inv = lax.rsqrt(jnp.mean(h * h, axis=-1, keepdims=True) + norm_eps)
    gd = gain * dn
    dh = gd * inv - h * (jnp.mean(gd * h, axis=-1, keepdims=True) * (inv * inv * inv))
    return dh, jnp.sum(dn * h * inv, axis=0, keepdims=True)


ROWS = 128
NB = 768


def col_blocks(width):
    return [slice(i, min(i + NB, width)) for i in range(0, width, NB)]


def self_forward(first, io, *refs):
    if first:
        lens, x_ref, gain_ref, w_ref, table_ref, spread_ref, a_ref, q_ref, k_ref, v_ref, o_ref, lse_ref, bias_ref = refs

        io.wait(x_ref, gain_ref)

        def norm(rows):
            a_ref[rows, :] = rms_rows(x_ref[rows, :].astype(F32), gain_ref[0:1, :]).astype(BF16)

        row_blocks(x_ref.shape[0], ROWS, norm)
        io.flush(a_ref)
    else:
        lens, a_ref, w_ref, table_ref, spread_ref, q_ref, k_ref, v_ref, o_ref, lse_ref, bias_ref = refs
    io.wait(table_ref, spread_ref)
    lines = lax.dot_general(
        table_ref[...], spread_ref[...], (((1,), (1,)), ((), ())), precision=highest,
        preferred_element_type=F32,
    )
    row = lax.broadcasted_iota(jnp.int32, (QB, LANE), 0)
    col = lax.broadcasted_iota(jnp.int32, (QB, LANE), 1)
    for h in range(bias_ref.shape[0]):
        line = jnp.broadcast_to(lines[h : h + 1, :], (QB, QB))
        tile = pltpu.roll(line, 0, 1, stride=1, stride_axis=0)[:, :LANE]
        bias_ref[h] = jnp.where(col - row + LANE < 0, masked_value, tile)
    io.flush(bias_ref)
    io.wait(lens, a_ref, w_ref)
    for i, ref in enumerate((q_ref, k_ref, v_ref)):
        ref[...] = nn(a_ref[...], w_ref[i]).astype(BF16)
        io.flush(ref)
    attend_pairs(q_ref, k_ref, v_ref, o_ref, lse_ref, bias_ref, lens[lax.axis_index("mp")])
    io.flush(o_ref, lse_ref)


def cross_forward(
    io, lens, x_ref, gain_ref, m_ref, oo, on, woo, won, wqo, wqn, wkvo, wkvn, wco, wcn,
    h1_ref, b_ref, qo, qn, ko, kn, vo, vn, oco, ocn, lse_ref, h2_ref, c_ref,
):
    io.wait(lens, m_ref)
    for k, v, w in ((ko, vo, wkvo), (kn, vn, wkvn)):
        io.wait(w)
        k[...] = nn(m_ref[...], w[0]).astype(BF16)
        v[...] = nn(m_ref[...], w[1]).astype(BF16)
        io.flush(k, v)
    io.wait(x_ref, gain_ref, oo, on, woo, won)
    for c in col_blocks(x_ref.shape[1]):
        h1_ref[:, c] = x_ref[:, c].astype(F32) + nn(oo[...], woo[:, c]) + nn(on[...], won[:, c])

    def first(rows):
        b_ref[rows, :] = rms_rows(h1_ref[rows, :], gain_ref[1:2, :]).astype(BF16)

    row_blocks(x_ref.shape[0], ROWS, first)
    io.flush(h1_ref, b_ref)
    io.wait(wqo, wqn)
    qo[...] = nn(b_ref[...], wqo[...]).astype(BF16)
    qn[...] = nn(b_ref[...], wqn[...]).astype(BF16)
    io.flush(qo, qn)
    heads = qo.shape[1] // HD
    length = lens[lax.axis_index("mp")]
    attend_pairs(qo, ko, vo, oco, lse_ref, None, length)
    attend_pairs(qn, kn, vn, ocn, lse_ref, None, length, heads)
    io.flush(oco, ocn, lse_ref)
    io.wait(wco, wcn)
    for c in col_blocks(x_ref.shape[1]):
        h2_ref[:, c] = h1_ref[:, c] + nn(oco[...], wco[:, c]) + nn(ocn[...], wcn[:, c])

    def last(rows):
        c_ref[rows, :] = rms_rows(h2_ref[rows, :], gain_ref[2:3, :]).astype(BF16)

    row_blocks(x_ref.shape[0], ROWS, last)
    io.flush(h2_ref, c_ref)


HB = 512


def hidden_block(c_ref, og_ref, wi, wd, out, at):
    root = np.float32(np.sqrt(2.0 / np.pi))
    width = out.shape[1] // 3
    gate = nn(c_ref[...], wi[0])
    up = nn(c_ref[...], wi[1])
    d_hid = nt(og_ref[...], wd[...])
    sq = gate * gate
    th = jnp.tanh(root * gate * (1.0 + 0.044715 * sq))
    half = 0.5 + 0.5 * th
    gelu = gate * half
    slope = half + 0.5 * gate * (1.0 - th * th) * (root * (1.0 + np.float32(3 * 0.044715) * sq))
    out[:, at : at + HB] = (d_hid * up * slope).astype(BF16)
    out[:, width + at : width + at + HB] = (d_hid * gelu).astype(BF16)
    out[:, 2 * width + at : 2 * width + at + HB] = (gelu * up).astype(BF16)


def ffn_other(io, c_ref, og_ref, *refs):
    weights, out = refs[:-1], refs[-1]
    io.wait(c_ref, og_ref)
    for i in range(0, len(weights), 2):
        io.wait(*weights[i : i + 2])
        hidden_block(c_ref, og_ref, weights[i], weights[i + 1], out, i // 2 * HB)
        for k in range(3):
            io.flush_columns(k * out.shape[1] // 3 + i // 2 * HB, HB, out)


def ffn_own(io, c_ref, og_ref, h2_ref, gain_ref, *refs):
    own, res_ref, g1_ref, w1_ref, dgain, acc = refs[-6:]
    weights, (nbr, win, wdn) = refs[:-9], refs[-9:-6]
    width = own.shape[1] // 3
    io.wait(c_ref, og_ref)
    for i in range(0, len(weights), 2):
        io.wait(*weights[i : i + 2])
        hidden_block(c_ref, og_ref, weights[i], weights[i + 1], own, i // 2 * HB)
    io.flush(own)
    first = True
    for i in range(0, len(weights), 2):
        wi, wd = weights[i], weights[i + 1]
        at = i // 2 * HB
        gate, up, hid = [own[:, k * width + at : k * width + at + HB] for k in range(3)]
        down, out = nt(gate, wi[0]) + nt(up, wi[1]), nn(hid, wd[...])
        g1_ref[...] = down if first else g1_ref[...] + down
        acc[...] = out if first else acc[...] + out
        first = False
    io.wait(nbr, win, wdn)
    g1_ref[...] += nt(nbr[:, 0:width], win[0]) + nt(nbr[:, width : 2 * width], win[1])
    acc[...] += nn(nbr[:, 2 * width :], wdn[...])
    io.wait(h2_ref, gain_ref)
    dgain[...] = jnp.zeros_like(dgain)

    def last(rows):
        h2 = h2_ref[rows, :]
        res_ref[rows, :] = (h2 + acc[rows, :]).astype(BF16)
        dh, dg = rms_back(h2, gain_ref[2:3, :], g1_ref[rows, :])
        g1 = og_ref[rows, :].astype(F32) + dh
        g1_ref[rows, :] = g1
        w1_ref[rows, :] = g1.astype(BF16)
        dgain[...] += dg

    row_blocks(h2_ref.shape[0], ROWS, last)
    io.flush(res_ref, g1_ref, w1_ref, dgain)


def cross_backward(
    io, lens, w1_ref, g1_ref, h1_ref, gain_ref, qo, qn, ko, kn, vo, vn, lse_ref, wco, wcn, wqo, wqn, wkvo, wkvn,
    do_own, dq_nbr, dkv_nbr, g0_ref, w0_ref, dm_ref, dgain, doo, don,
):
    half = qo.shape[1]
    heads = half // HD
    io.wait(lens, w1_ref, wco, wcn)
    doo[...] = nt(w1_ref[...], wco[...]).astype(BF16)
    don[...] = nt(w1_ref[...], wcn[...]).astype(BF16)
    length = lens[lax.axis_index("mp")]
    io.wait(qn, kn, vn, lse_ref)
    grads = ((dq_nbr, 0), (dkv_nbr, 0), (dkv_nbr, half))
    attend_back_pairs(qn, kn, vn, don, grads, lse_ref, None, length, heads)
    io.flush(dq_nbr, dkv_nbr)
    io.wait(qo, ko, vo)
    grads = ((do_own, 0), (do_own, half), (do_own, 2 * half))
    attend_back_pairs(qo, ko, vo, doo, grads, lse_ref, None, length)
    io.flush(do_own)
    io.wait(wqo, wqn, wkvo, wkvn)
    for c in col_blocks(w1_ref.shape[1]):
        g0_ref[:, c] = nt(do_own[:, 0:half], wqo[c, :]) + nt(dq_nbr[...], wqn[c, :])
        dm_ref[:, c] = (
            nt(do_own[:, half : 2 * half], wkvo[0, c, :])
            + nt(do_own[:, 2 * half :], wkvo[1, c, :])
            + nt(dkv_nbr[:, 0:half], wkvn[0, c, :])
            + nt(dkv_nbr[:, half:], wkvn[1, c, :])
        ).astype(BF16)
    io.flush(dm_ref)
    io.wait(g1_ref, h1_ref, gain_ref)
    dgain[...] = jnp.zeros_like(dgain)

    def last(rows):
        dh, dg = rms_back(h1_ref[rows, :], gain_ref[1:2, :], g0_ref[rows, :])
        g0 = g1_ref[rows, :] + dh
        g0_ref[rows, :] = g0
        w0_ref[rows, :] = g0.astype(BF16)
        dgain[...] += dg

    row_blocks(w1_ref.shape[0], ROWS, last)
    io.flush(g0_ref, w0_ref, dgain)


def self_backward(io, lens, w0_ref, *refs):
    parts, outs, do_ref = (refs[:6], refs[6:12]), refs[12:17], refs[17]
    io.wait(lens, w0_ref)
    for i, (wo, q_ref, k_ref, v_ref, lse_ref, bias_ref) in enumerate(parts):
        half = q_ref.shape[1]
        if i == 0:
            mine, diag_ref = outs[:2], outs[2]
            grads = ((outs[0], 0), (outs[1], 0), (outs[1], half))
        else:
            mine, diag_ref = outs[3:4], outs[4]
            grads = [(outs[3], k * half) for k in range(3)]
        io.wait(wo)
        do_ref[...] = nt(w0_ref[...], wo[...]).astype(BF16)
        io.wait(q_ref, k_ref, v_ref, lse_ref, bias_ref)
        attend_back_pairs(
            q_ref, k_ref, v_ref, do_ref, grads, lse_ref, bias_ref, lens[lax.axis_index("mp")], 0, diag_ref
        )
        io.flush(*mine, diag_ref)


def input_backward(io, *refs):
    pairs, (x_ref, gain_ref, g0_ref, out_ref, dgain, acc) = refs[:-6], refs[-6:]
    for i in range(0, len(pairs), 4):
        io.wait(*pairs[i : i + 4])
        term = nt(pairs[i][...], pairs[i + 1][0]) + nt(pairs[i + 2][...], pairs[i + 3][0])
        acc[...] = acc[...] + term if i else term
    io.wait(x_ref, gain_ref, g0_ref)
    dgain[...] = jnp.zeros_like(dgain)

    def some(rows):
        dh, dg = rms_back(x_ref[rows, :].astype(F32), gain_ref[0:1, :], acc[rows, :])
        out_ref[rows, :] = (g0_ref[rows, :] + dh).astype(BF16)
        dgain[...] += dg

    row_blocks(x_ref.shape[0], ROWS, some)
    io.flush(out_ref, dgain)


LINE = (0, 8, 4, 12)
ORDERS = ((1, 2), (2, 1))


def weight_grads(parts, layouts, io, *refs):
    outs, total = refs[-1 - sum(len(v) for v in layouts) : -1], refs[-1]
    rows = outs[0].shape[1]
    device = lax.axis_index("dp")
    first = 0
    for jobs, layout in zip(parts, layouts):
        mine = outs[first : first + len(layout)]
        first += len(layout)
        at = 0
        for lo, ln, ro, rn, width in jobs:
            done = 0
            while done < width:
                step = width if width <= 640 else min(512, width - done)
                src = slice(done, done + step)
                io.wait(refs[lo], refs[ro])
                total[:, 0:step] = tn(refs[lo][...], refs[ro][:, src])
                io.wait(refs[ln], refs[rn])
                total[:, 0:step] += tn(refs[ln][...], refs[rn][:, src])
                dst = slice(at + done, at + done + step)
                for out, nears in zip(mine, layout):
                    for j, mask in enumerate([near ^ far for near in nears for far in LINE]):
                        chunk = lax.bitwise_xor(device, jnp.int32(mask))
                        part = total[pl.ds(pl.multiple_of(chunk * rows, 16), rows), 0:step]
                        out[j, :, dst] = part.astype(out.dtype)
                io.flush_columns(at + done, step, *mine)
                done += step
            at += width


def add_terms(plan, io, *refs):
    at = 0
    outs = refs[-len(plan) :]
    for counts, out in zip(plan, outs):
        start = 0
        for count in counts:
            terms = refs[at : at + count]
            at += count
            io.wait(*terms)
            cols = slice(start, start + terms[0].shape[-1])
            start = cols.stop
            for j in range(out.shape[0]):
                total = terms[0][j]
                for t in terms[1:]:
                    total = total + t[j].astype(F32)
                out[j, :, cols] = total.astype(out.dtype)
        io.flush(out)


def swap_dp(v, mask):
    return lax.ppermute(v, "dp", [(i, i ^ mask) for i in range(16)])


def swap_mp(v):
    return lax.ppermute(v, "mp", [(0, 1), (1, 0)])


def make_grads(parts, depth, n_data, direct=False):
    if n_data != 16:

        def piece(a):
            if not isinstance(a, tuple):
                return a
            value = a[0]
            for axis, start, size in a[1]:
                start = start() if callable(start) else start
                value = lax.dynamic_slice_in_dim(value, start, size, axis)
            return value

        cols = []
        for job in [job for jobs in parts for job in jobs]:
            lo, ln, ro, rn = [piece(a) for a in job]
            cols.append(tn(lo, ro) + tn(ln, rn))
        return lax.psum_scatter(
            jnp.concatenate(cols, axis=1), "dp", scatter_dimension=0, tiled=True
        )
    arrays, keys, plan, shapes, layouts = [], [], [], [], []
    rows = depth // 16
    for jobs in parts:
        spots = []
        for job in jobs:
            place = []
            for a in job:
                key = (id(a[0]),) + a[1:] if isinstance(a, tuple) else id(a)
                if key not in keys:
                    arrays.append(a)
                    keys.append(key)
                place.append(keys.index(key))
            spots.append(tuple(place) + (job[2][1][-1][2],))
        plan.append(tuple(spots))
        width = sum(job[2][1][-1][2] for job in jobs)
        if direct:
            layouts.append(((0,), (1,), (2,), (3,)))
        else:
            one, two = ORDERS[len(layouts)]
            layouts.append(((0, two), (one, one ^ two)))
        for nears in layouts[-1]:
            shapes.append(sds((4 * len(nears), rows, width), F32 if 0 in nears else BF16))
    widest = max(job[4] if job[4] <= 640 else 512 for jobs in plan for job in jobs)
    return dma_call(
        functools.partial(weight_grads, tuple(plan), tuple(layouts)),
        shapes,
        arrays,
        0,
        [pltpu.VMEM((depth, widest), F32)],
        flops=4 * 512 * depth * 1024,
        n_writes=64,
    )


class Reduction:
    def __init__(self, made, n_data, direct=False, near=False):
        self.plain = n_data != 16
        self.made, self.direct = made, direct
        self.far = []
        if not self.plain:
            if direct or near:
                self.keeps, self.done = [made[0]], 2
                self.got = [[swap_dp(v, m) for v, m in zip(made[1:], (1, 2, 3))]]
            else:
                self.keeps, self.done = list(made[::2]), 1
                self.got = [[swap_dp(v, o[0])] for v, o in zip(made[1::2], ORDERS)]

    def near(self, start, size):
        return [[leading(t, start, size) for t in [k] + g] for k, g in zip(self.keeps, self.got)]

    def sends(self):
        rows, widths = self.keeps[0].shape[1], [k.shape[2] for k in self.keeps]
        if self.done == 1:
            parts = self.near(4, 4)
            shapes = [sds((4, rows, w), BF16) for w in widths]
            return [(len(p),) for p in parts], shapes, [t for p in parts for t in p]
        if self.direct:
            spots = ((1, 1), (2, 1), (3, 1))
        else:
            spots = ((2, 2),) if self.done == 2 else ((1, 1),)
        plan, shapes, terms = [], [], []
        for start, size in spots:
            parts, at = self.near(start, size), 0
            for part, w in zip(parts, widths):
                part += [leading(columns(t, at, w), start, size) for t in self.far]
                at += w
            plan.append(tuple(len(p) for p in parts))
            shapes.append(sds((size, rows, sum(widths)), BF16))
            terms += [t for part in parts for t in part]
        return plan, shapes, terms

    def sent(self, sends):
        if self.done == 1:
            for got, send, order in zip(self.got, sends, ORDERS):
                got.append(swap_dp(send, order[1]))
        elif self.direct:
            self.far = [swap_dp(v, m) for v, m in zip(sends, LINE[1:])]
        else:
            self.far.append(swap_dp(sends[0], 4 if self.done == 2 else 8))
        self.done += 1

    def terms(self):
        if self.plain:
            return [[self.made[None]]]
        parts, at = self.near(0, 1), 0
        for part, k in zip(parts, self.keeps):
            part += [leading(columns(t, at, k.shape[2]), 0, 1) for t in self.far]
            at += k.shape[2]
        return parts


def exchange(*steps, others=()):
    steps = [r for r in steps if not r.plain]
    if not steps:
        return []
    made = [r.sends() for r in steps]
    plan = [p for m in made for p in m[0]]
    shapes = [p for m in made for p in m[1]]
    terms = [p for m in made for p in m[2]]
    if others:
        terms[0] = (after(terms[0][0], *others), terms[0][1])
    sends = dma_call(functools.partial(add_terms, tuple(plan)), shapes, terms)
    at = 0
    for r, m in zip(steps, made):
        r.sent(sends[at : at + len(m[0])])
        at += len(m[0])
    return list(sends)


def squares_of(mats, first, all_ref, cols_ref, row_sums):
    rows = all_ref.shape[0]
    lane = lax.broadcasted_iota(jnp.int32, (rows, LANE), 1)
    for i, (start, width) in enumerate(mats):
        part = all_ref[:, start : start + width]
        sq = part * part
        cols_ref[:, start : start + width] = jnp.sum(sq, axis=0, keepdims=True)
        row_sums = row_sums + jnp.where(lane == first + i, jnp.sum(sq, axis=1, keepdims=True), 0.0)
    return row_sums


def end_sums(counts, io, refs, all_ref):
    start = at = 0
    for count in counts:
        terms = refs[at : at + count]
        io.wait(*terms)
        total = terms[0][0]
        for t in terms[1:]:
            total = total + t[0].astype(F32)
        all_ref[:, start : start + total.shape[1]] = total
        at += count
        start += total.shape[1]


def early_statistics(counts, mats, io, *refs):
    all_ref, cols_ref, rows_ref = refs[-3:]
    end_sums(counts, io, refs, all_ref)
    rows_ref[...] = squares_of(mats, 0, all_ref, cols_ref, jnp.zeros_like(rows_ref))
    io.flush(all_ref, cols_ref, rows_ref)


def statistics(counts, mats, first, io, *refs):
    all_ref, pack_ref, cols_ref = refs[-3:]
    rows_ref, spread = refs[-10], refs[-4]
    gains, diags = refs[-9:-6], refs[-6:-4]
    io.wait(rows_ref, *gains, *diags, spread)
    pack_ref[...] = jnp.zeros_like(pack_ref)
    for i, gain in enumerate(gains):
        pack_ref[i : i + 1, :] = gain[...]
    for i, diag in enumerate(diags):
        heads = diag.shape[0]
        lines = jnp.concatenate([diag[h] for h in range(heads)], axis=0)
        pack_ref[8 : 8 + heads, i * LANE : i * LANE + BUCKETS] = lax.dot_general(
            lines, spread[...], (((1,), (0,)), ((), ())), precision=highest,
            preferred_element_type=F32,
        )
    end_sums(counts, io, refs, all_ref)
    rows = all_ref.shape[0]
    pack_ref[16 : 16 + rows, 0:LANE] = squares_of(mats, first, all_ref, cols_ref, rows_ref[...])
    io.flush(all_ref, pack_ref, cols_ref)


def merge_kernel(io, own_ref, got_ref, early_ref, late_ref, out_ref, rows_ref):
    io.wait(own_ref, got_ref, early_ref, late_ref)
    rows = rows_ref.shape[0]
    n_early, depth = early_ref.shape[1], own_ref.shape[1]
    n_all = n_early + late_ref.shape[1]
    full = own_ref[16 : 16 + rows, 0:LANE] + got_ref[16 : 16 + rows, 0:LANE]
    rows_ref[...] = full
    out_ref[:, 0:n_early] = early_ref[...]
    out_ref[:, n_early:n_all] = late_ref[...]
    at = n_all
    for i in range(3):
        out_ref[:, at : at + depth] = own_ref[i : i + 1, :] + got_ref[i : i + 1, :]
        at += depth
    out_ref[:, at : at + LANE] = jnp.sum(full, axis=0, keepdims=True)
    for side in range(2):
        mine = own_ref[8:16, side * LANE : (side + 1) * LANE]
        theirs = got_ref[8:16, (1 - side) * LANE : (2 - side) * LANE]
        both = mine + theirs
        for h in range(8):
            at += LANE
            out_ref[:, at : at + LANE] = both[h : h + 1]
    io.flush(out_ref, rows_ref)


def turn(v):
    rows = v.shape[0]
    if rows < LANE:
        v = jnp.concatenate([v, jnp.zeros((LANE - rows, v.shape[1]), v.dtype)], axis=0)
    return jnp.transpose(v)[:, :rows]


def update_kernel(plan, n_terms, io, *refs):
    terms = refs[:n_terms]
    rows_ref, early_ref, late_ref = refs[n_terms : n_terms + 3]
    weights = refs[n_terms + 3 : n_terms + 3 + len(plan)]
    outs = refs[n_terms + 3 + len(plan) :]
    io.wait(*terms)
    line = functools.reduce(jnp.add, [p[...] for p in terms])
    n_early = early_ref.shape[1]
    n_all = n_early + late_ref.shape[1]
    gain_ref, table_ref, norm_ref = outs[0], outs[1], outs[-1]
    depth = gain_ref.shape[1]
    gains_at, totals_at = n_all, n_all + 3 * depth
    tables_at = totals_at + LANE
    for i in range(3):
        gain_ref[i : i + 1, :] = line[:, gains_at + i * depth : gains_at + (i + 1) * depth]
    for h in range(table_ref.shape[0]):
        at = tables_at + h * LANE
        table_ref[h : h + 1, :] = line[:, at : at + BUCKETS]
    totals = line[:, totals_at:tables_at]
    gains, tables = line[:, gains_at:totals_at], line[:, tables_at:]
    squares = (
        jnp.sum(gains * gains, axis=1, keepdims=True)
        + jnp.sum(tables * tables, axis=1, keepdims=True)
        + jnp.sum(totals, axis=1, keepdims=True)
    )
    norm_ref[...] = jnp.sqrt(squares)
    io.flush(gain_ref, table_ref, norm_ref)
    io.wait(rows_ref, early_ref, late_ref)
    row_sums = rows_ref[...]
    row_lines = turn(row_sums)
    at = 2
    for (natural, members), weight in zip(plan, weights):
        new_ref, row_out, col_out = outs[at : at + 3]
        at += 3
        io.wait(weight)
        for k, (i, start, width) in enumerate(members):
            size = 2 * width
            by_row = row_sums[:, i : i + 1] / size + stat_eps
            by_col = line[:, start : start + width] / depth + stat_eps
            mean = totals[:, i : i + 1] / (size * depth) + stat_eps
            if start < n_early:
                grad = early_ref[:, start : start + width]
            else:
                grad = late_ref[:, start - n_early : start - n_early + width]
            change = (
                learn_rate
                * grad
                * lax.rsqrt(by_row * by_col / mean)
            )
            row_line = row_lines[i : i + 1, :] / size + stat_eps
            new_ref[k] = weight[k].astype(F32) - change
            lines = (row_line, by_col) if natural else (by_col, row_line)
            for out, value in zip((row_out, col_out), lines):
                if len(out.shape) == 1:
                    out[...] = value.reshape(out.shape)
                else:
                    out[k : k + 1, :] = value
        io.flush(new_ref, row_out, col_out)


def after(value, *others):
    return lax.optimization_barrier((value,) + others)[0]


def body(
    tokens,
    memory,
    out_grad,
    tgt_lens,
    mem_lens,
    norm_gains,
    rel_table,
    self_qkv,
    self_out,
    cross_q,
    cross_kv,
    cross_out,
    ffn_in,
    ffn_out,
):
    n_data = lax.axis_size("dp")
    mp = lax.axis_index("mp")
    dp = lax.axis_index("dp")
    rows = tokens.shape[0]
    depth = tokens.shape[1]
    heads = rel_table.shape[1]
    half = heads * HD
    width = ffn_out.shape[0]
    chunk = depth // n_data
    qkv_n = swap_mp(self_qkv)
    table = rel_table.T
    table_n = swap_mp(table)
    so_n = swap_mp(self_out)
    ckv_n = swap_mp(cross_kv)
    cq_n = swap_mp(cross_q)

    dist = np.arange(QB)
    line_dist = np.where(dist < LANE, dist + LANE, dist - LANE)
    spread = jnp.asarray((bucket_of(line_dist)[:, None] == np.arange(BUCKETS)).astype(np.float32))
    gather = jnp.asarray((bucket_of(dist)[:, None] == np.arange(BUCKETS)).astype(np.float32))

    attn_flops = 4 * rows * rows * HD * heads
    bias_shape = sds((heads, QB, LANE), F32)
    act = sds((rows, half), BF16)
    wide = sds((rows, depth), BF16)
    full = sds((rows, depth), F32)
    gain_row = sds((1, depth), F32)
    lse = sds((heads, 1, rows), F32)
    lse2 = sds((2 * heads, 1, rows), F32)
    a, qs_o, ks_o, vs_o, os_o, lses_o, bias_o = dma_call(
        functools.partial(self_forward, True),
        [wide, act, act, act, act, lse, bias_shape],
        [tgt_lens, tokens, norm_gains, self_qkv, table, spread],
        1,
        flops=6 * rows * depth * half + attn_flops,
    )
    a, qkv_n, table_n, so_n, cq_n, ckv_n, cross_out_b, ffn_in_b, ffn_out_b, out_grad_b = (
        lax.optimization_barrier(
            (a, qkv_n, table_n, so_n, cq_n, ckv_n, cross_out, ffn_in, ffn_out, out_grad)
        )
    )
    co_n = swap_mp(cross_out_b)
    fi_n = swap_mp(ffn_in_b)
    fo_n = swap_mp(ffn_out_b)
    og_n = swap_mp(out_grad_b)
    a_n = swap_mp(a)
    qs_n, ks_n, vs_n, os_n, lses_n, bias_n = dma_call(
        functools.partial(self_forward, False),
        [act, act, act, act, lse, bias_shape],
        [tgt_lens, a, qkv_n, table_n, spread],
        1,
        flops=6 * rows * depth * half + attn_flops,
    )
    mem_own = leading(memory, lambda: pl.multiple_of(lax.axis_index("mp") * rows, rows), rows)
    mem_nbr = leading(memory, lambda: pl.multiple_of((1 - lax.axis_index("mp")) * rows, rows), rows)
    os_x = swap_mp(os_n)
    h1, b, qc_o, qc_n, kc_o, kc_n, vc_o, vc_n, oc_o, oc_n, lsec, h2, c = dma_call(
        cross_forward,
        [full, wide, act, act, act, act, act, act, act, act, lse2, full, wide],
        [mem_lens, tokens, norm_gains, mem_own, os_o, os_n, self_out, so_n, cross_q, cq_n, cross_kv, ckv_n, cross_out, co_n],
        1,
        flops=20 * rows * depth * half + 2 * attn_flops,
    )
    c, os_x, a_n = lax.optimization_barrier((c, os_x, a_n))
    b_n = swap_mp(b)
    oc_x = swap_mp(oc_n)
    c_n = swap_mp(c)
    hid = sds((rows, 3 * width), BF16)
    def hidden_weights(wi, wd):
        return [v for i in range(0, width, HB) for v in (columns(wi, i, HB), leading(wd, i, HB))]

    f_nbr = dma_call(
        ffn_other,
        [hid],
        [c, out_grad] + hidden_weights(fi_n, fo_n),
        flops=6 * rows * depth * width,
        n_writes=3 * width // HB,
    )[0]
    f_x = swap_mp(f_nbr)
    f_own, result, g1, w1, gain_c = dma_call(
        ffn_own,
        [hid, wide, full, wide, gain_row],
        [c, out_grad, h2, norm_gains] + hidden_weights(ffn_in, ffn_out) + [f_nbr, fi_n, fo_n],
        0,
        [pltpu.VMEM((rows, depth), F32)],
        flops=18 * rows * depth * width,
    )
    w1_n = swap_mp(w1)
    def pair(own, nbr, start, size):
        return columns(own, start, size), columns(nbr, start, size)

    w1, f_own = lax.optimization_barrier((w1, f_own))
    early_down = width // 2
    left = (2 * width + early_down) // 2
    ffn_made = make_grads(
        (
            ((c, c_n) + pair(f_own, f_x, 0, left),),
            (
                (c, c_n) + pair(f_own, f_x, left, 2 * width - left),
                (out_grad, og_n) + pair(f_own, f_x, 2 * width, early_down),
            ),
        ),
        depth,
        n_data,
    )
    w1_b = after(w1, w1_n, b_n, oc_x, *jax.tree.leaves(ffn_made))
    ffn_sum = Reduction(ffn_made, n_data)
    c_own, cq_nbr, ckv_nbr, g0, w0, d_mem, gain_b = dma_call(
        cross_backward,
        [sds((rows, 3 * half), BF16), act, sds((rows, 2 * half), BF16), full, wide, wide, gain_row],
        [mem_lens, w1_b, g1, h1, norm_gains, qc_o, qc_n, kc_o, kc_n, vc_o, vc_n, lsec, cross_out, co_n, cross_q, cq_n, cross_kv, ckv_n],
        1,
        [pltpu.VMEM((rows, half), BF16), pltpu.VMEM((rows, half), BF16)],
        flops=16 * rows * depth * half + 5 * attn_flops,
    )
    cq_x, ckv_x = swap_mp(cq_nbr), swap_mp(ckv_nbr)
    w0_n = swap_mp(w0)
    diag = sds((heads, 1, QB), F32)

    sent = exchange(ffn_sum, others=(c_own,))
    if sent:
        w0, w0_n, cq_x, ckv_x = lax.optimization_barrier((w0, w0_n, cq_x, ckv_x, *sent))[:4]
    split = 2 * LANE
    split = 2 * LANE
    cross_made = make_grads(
        (
            (
                (out_grad, og_n) + pair(f_own, f_x, 2 * width + early_down, width - early_down),
                (w1, w1_n) + pair(oc_o, oc_x, 0, half),
                (w0, w0_n) + pair(os_o, os_x, 0, split),
            ),
            (
                (w0, w0_n) + pair(os_o, os_x, split, half - split),
                (b, b_n, columns(c_own, 0, half), columns(cq_x, 0, half)),
                (mem_own, mem_nbr, columns(c_own, half, 2 * half), columns(ckv_x, 0, 2 * half)),
            ),
        ),
        depth,
        n_data,
    )
    cross_sum = Reduction(cross_made, n_data)
    sent = [] if ffn_sum.plain else [g[-1] for g in ffn_sum.got]
    w0_b = after(w0, *sent, *jax.tree.leaves(cross_made))
    sq_nbr, skv_nbr, diag_n, s_own, diag_o = dma_call(
        self_backward,
        [act, sds((rows, 2 * half), BF16), diag, sds((rows, 3 * half), BF16), diag],
        [tgt_lens, w0_b, so_n, qs_n, ks_n, vs_n, lses_n, bias_n]
        + [self_out, qs_o, ks_o, vs_o, lses_o, bias_o],
        1,
        [pltpu.VMEM((rows, half), BF16)],
        flops=4 * rows * depth * half + 6 * attn_flops,
    )
    sq_x, skv_x = swap_mp(sq_nbr), swap_mp(skv_nbr)
    grad_in, gain_a = dma_call(
        input_backward,
        [wide, gain_row],
        [
            v
            for i in range(3)
            for d, at, w in (
                (s_own, i, self_qkv),
                (sq_nbr if i == 0 else skv_nbr, max(i - 1, 0), qkv_n),
            )
            for v in (columns(d, at * half, half), leading(w, i, 1))
        ]
        + [tokens, norm_gains, g0],
        0,
        [pltpu.VMEM((rows, depth), F32)],
        flops=12 * rows * depth * half,
    )
    sent = exchange(ffn_sum, cross_sum, others=(grad_in,))
    s_own, sq_x, skv_x = lax.optimization_barrier((s_own, sq_x, skv_x, grad_in, *sent))[:3]
    self_made = make_grads(
        (
            (
                (a, a_n, columns(s_own, 0, half), columns(sq_x, 0, half)),
                (a, a_n, columns(s_own, half, 2 * half), columns(skv_x, 0, 2 * half)),
            ),
        ),
        depth,
        n_data,
        direct=True,
    )
    self_sum = Reduction(self_made, n_data, direct=True)
    exchange(cross_sum, ffn_sum, others=jax.tree.leaves(self_made))

    sizes = [width, width, width] + [half] * 8
    starts = [int(v) for v in np.cumsum([0] + sizes[:-1])]
    mats = tuple(zip(starts, sizes))
    n_all = sum(sizes)
    plan = (
        (True, (8, 9, 10)),
        (False, (4,)),
        (True, (5,)),
        (True, (6, 7)),
        (False, (3,)),
        (True, (0, 1)),
        (False, (2,)),
    )
    plan = tuple((n, tuple((i, starts[i], sizes[i]) for i in m)) for n, m in plan)
    weights = (self_qkv, self_out, cross_q, cross_kv, cross_out, ffn_in, ffn_out)
    slices, shapes = [], [sds((3, depth), F32), sds((heads, BUCKETS), F32)]
    for (natural, members), weight in zip(plan, weights):
        count, size = len(members), members[0][2]
        if natural:
            stacked = weight.reshape((count,) + weight.shape[-2:])
            part = cut(stacked, 1, lambda: pl.multiple_of(lax.axis_index("dp") * chunk, chunk), chunk)
            if n_data != 16:
                part = lax.dynamic_slice_in_dim(stacked, dp * chunk, chunk, 1)
        else:
            part = lax.dynamic_slice_in_dim(weight, dp * chunk, chunk, 1).T[None]
        slices.append(part)
        line_sizes = (chunk, size) if natural else (size, chunk)
        shapes += [sds((count, chunk, size), F32)]
        shapes += [sds((n,) if weight.ndim == 2 else (count, n), F32) for n in line_sizes]
    shapes.append(sds((1, 1), F32))
    exchange(cross_sum, others=[v for v in slices if not isinstance(v, tuple)])
    sent = exchange(self_sum)
    n_early = starts[8]
    early = ffn_sum.terms() + cross_sum.terms()
    if sent:
        early[0][0] = (after(early[0][0][0], *sent), early[0][0][1])
    grads, cols, row_parts = dma_call(
        functools.partial(early_statistics, tuple(len(t) for t in early), mats[:8]),
        [sds((chunk, n_early), F32), sds((1, n_early), F32), sds((chunk, LANE), F32)],
        [t for part in early for t in part],
    )
    late = self_sum.terms()
    pack_rows = -(-(16 + chunk) // 8) * 8
    late_grads, pack, late_cols = dma_call(
        functools.partial(statistics, tuple(len(t) for t in late), tuple((a - n_early, b) for a, b in mats[8:]), 8),
        [sds((chunk, n_all - n_early), F32), sds((pack_rows, depth), F32), sds((1, n_all - n_early), F32)],
        [t for part in late for t in part] + [row_parts, gain_a, gain_b, gain_c, diag_o, diag_n, gather],
    )
    line, row_sums = dma_call(
        merge_kernel,
        [sds((1, n_all + 3 * depth + 17 * LANE), F32), sds((chunk, LANE), F32)],
        [pack, swap_mp(pack), cols, late_cols],
    )
    if n_data == 16:
        terms = [line]
        for group in ((1, 2, 3), (4, 8, 12)):
            if len(terms) > 1:
                terms = [functools.reduce(jnp.add, terms)]
            terms = terms + [swap_dp(terms[0], m) for m in group]
    else:
        terms = [lax.psum(line, "dp")]

    done = dma_call(
        functools.partial(update_kernel, plan, len(terms)),
        shapes,
        terms + [row_sums, grads, late_grads] + slices,
    )
    finals = [result, grad_in, d_mem, done[0], done[1].T]
    for i, ((natural, _), weight) in enumerate(zip(plan, weights)):
        new, row, col = done[2 + 3 * i : 5 + 3 * i]
        if weight.ndim == 2:
            new = new[0] if natural else new[0].T
        finals += [new, row, col]
    return tuple(finals + [done[-1][0, 0]])


def solution(mesh):
    placed = (
        P(("dp", "mp"), None),
        P("dp", None),
        P(("dp", "mp"), None),
        P("dp"),
        P("dp"),
        P(),
        P(None, "mp"),
        P(None, None, "mp"),
        P("mp", None),
        P(None, "mp"),
        P(None, None, "mp"),
        P("mp", None),
        P(None, None, "mp"),
        P("mp", None),
    )
    return jax.shard_map(
        body,
        mesh=mesh,
        in_specs=placed,
        out_specs=(
            P(("dp", "mp"), None),
            P(("dp", "mp"), None),
            P(("dp", "mp"), None),
            P(),
            P(None, "mp"),
            P(None, "dp", "mp"),
            P(None, "dp"),
            P(None, "mp"),
            P("mp", "dp"),
            P("mp"),
            P("dp"),
            P("dp", "mp"),
            P("dp"),
            P("mp"),
            P(None, "dp", "mp"),
            P(None, "dp"),
            P(None, "mp"),
            P("mp", "dp"),
            P("mp"),
            P("dp"),
            P(None, "dp", "mp"),
            P(None, "dp"),
            P(None, "mp"),
            P("mp", "dp"),
            P("mp"),
            P("dp"),
            P(),
        ),
        check_vma=False,
    )
```
